128 devices in a mesh: dp: 32 (over y, x_hi, z), mp: 4 (over x_lo, core).
Axes of the slice: x: 4 (x_hi: 2, x_lo: 2; x = x_hi * 2 + x_lo), y: 4, z: 4, core: 2. Of those that a mesh axis runs over, the one named last changes fastest.
Arguments:
- lag_sequences: bfloat16 [98304, 336], P(('dp', 'mp')), may hold values from -6 to 6
- sample_cluster_label: int32 [98304], P(('dp', 'mp')), may hold values from 0 to 3
- entry_dense_matrix: bfloat16 [2, 560, 512], P(None, None, 'mp'), may hold values from -0.5 to 0.5
- dense_matrix_middle: bfloat16 [2, 512, 512], P(None, 'mp'), may hold values from -0.25 to 0.25
- dense_matrix_later: bfloat16 [2, 512, 512], P(None, None, 'mp'), may hold values from -0.25 to 0.25
- dense_matrix_last: bfloat16 [2, 512, 512], P(None, 'mp'), may hold values from -0.25 to 0.25
- past_coefficient_matrix: bfloat16 [2, 512, 512], P(None, None, 'mp'), may hold values from -0.25 to 0.25
- future_coefficient_matrix: bfloat16 [2, 512, 512], P(None, None, 'mp'), may hold values from -0.25 to 0.25
- generic_expansion_matrix: bfloat16 [2, 512, 640], P(None, 'mp'), may hold values from -0.25 to 0.25
- prediction_adjoint: bfloat16 [98304, 48], P(('dp', 'mp')), may hold values from -6 to 6
- leftover_cotan: bfloat16 [98304, 336], P(('dp', 'mp')), may hold values from -6 to 6
Outputs:
- outlook_aggregate: float32 [98304, 48], P(('dp', 'mp'))
- residual: float32 [98304, 336], P(('dp', 'mp'))
- sequence_slope: float32 [98304, 336], P(('dp', 'mp'))
- grad_input: float32 [2, 560, 512], P(None, None, 'mp')
- grad_second: float32 [2, 512, 512], P(None, 'mp')
- grad_third: float32 [2, 512, 512], P(None, None, 'mp')
- grad_fourth: float32 [2, 512, 512], P(None, 'mp')
- grad_back: float32 [2, 512, 512], P(None, None, 'mp')
- grad_fore: float32 [2, 512, 512], P(None, None, 'mp')
- grad_basis: float32 [2, 512, 640], P(None, 'mp')
The draws below stay inside these ranges and needn't reach their ends.
Inputs may be any that keep to these rules, and one draw needn't show every extreme that they name: `sample_cluster_label`: each window's frequency group: 0 yearly, 1 quarterly, 2 monthly, 3 hourly.
All inputs are finite; a program needn't handle non-finite values.
Results may differ from the reference program's by a relative error of at most 0.015.
Values may be sent and summed in bfloat16 or wider, within the bound.
No kernel may reach another device: no remote copies, remote signals or barrier semaphores. Data moves between devices by JAX's collectives and lax.ppermute only.
A program may use at most 192 MiB of HBM per device.

```python
import math
import jax
import jax.numpy as jnp
from jax import lax

NEURON_WIDTH = 512
COEFF_WIDTH = 512
WIDEST_LOOKBEHIND = 336
COMBINED_REACH = 560
FAR_REACH = 48
HSUM = 80
UNIT_CHAIN = 2
SAMPLE_NUMBER = 98304


def with_ends(values, key, smallest, high):
    extent = values.shape
    spot = [jax.random.randint(jax.random.fold_in(key, axis), (), 0, extent[axis]) for axis in range(len(extent))]
    values = values.at[tuple(spot)].set(smallest)
    longest = extent.index(max(extent))
    spot[longest] = (spot[longest] + 1) % extent[longest]
    return values.at[tuple(spot)].set(high)


def steps_of(rng, shape, shards, least, high):
    level, own = 1.0, jax.random.fold_in(rng, 6)
    for axis_at, blocks in shards:
        draws = jnp.exp(jax.random.uniform(jax.random.fold_in(own, axis_at), (blocks,), jnp.float32, least / len(shards), high / len(shards)))
        level = level * jnp.repeat(draws, shape[axis_at] // blocks).reshape([-1 if axis == axis_at else 1 for axis in range(len(shape))])
    return level


def normal_values(rng, extent, spread, limit, shards=(), kind=jnp.bfloat16):
    values = spread * jax.random.normal(rng, extent, jnp.float32)
    if shards:
        values = values * steps_of(rng, extent, shards, -0.22, 0.18)
    return jnp.clip(values, -limit, limit).astype(kind)


def setup_inputs(seed: int = 0) -> dict:
    key_list = jax.random.split(jax.random.key(seed), 12)
    lag_sequences = normal_values(key_list[0], (SAMPLE_NUMBER, WIDEST_LOOKBEHIND), 1.0, 6.0, ((0, 128),))
    sample_cluster_label = with_ends(jax.random.randint(key_list[1], (SAMPLE_NUMBER,), 0, 4), jax.random.fold_in(key_list[1], 1), 0, 3).astype(jnp.int32)
    entry_dense_matrix = normal_values(key_list[2], (UNIT_CHAIN, COMBINED_REACH, NEURON_WIDTH), (WIDEST_LOOKBEHIND // 2) ** -0.5, 0.5, ((2, 4),))
    dense_matrix_middle = normal_values(key_list[3], (UNIT_CHAIN, NEURON_WIDTH, NEURON_WIDTH), NEURON_WIDTH ** -0.5, 0.25, ((1, 4),))
    dense_matrix_later = normal_values(key_list[4], (UNIT_CHAIN, NEURON_WIDTH, NEURON_WIDTH), NEURON_WIDTH ** -0.5, 0.25, ((2, 4),))
    dense_matrix_last = normal_values(key_list[5], (UNIT_CHAIN, NEURON_WIDTH, NEURON_WIDTH), NEURON_WIDTH ** -0.5, 0.25, ((1, 4),))
    past_coefficient_matrix = normal_values(key_list[6], (UNIT_CHAIN, NEURON_WIDTH, COEFF_WIDTH), NEURON_WIDTH ** -0.5, 0.25, ((2, 4),))
    future_coefficient_matrix = normal_values(key_list[7], (UNIT_CHAIN, NEURON_WIDTH, COEFF_WIDTH), NEURON_WIDTH ** -0.5, 0.25, ((2, 4),))
    generic_expansion_matrix = normal_values(key_list[8], (UNIT_CHAIN, COEFF_WIDTH, COMBINED_REACH + HSUM), COEFF_WIDTH ** -0.5, 0.25, ((1, 4),))
    prediction_adjoint = normal_values(key_list[9], (SAMPLE_NUMBER, FAR_REACH), 1.0, 6.0, ((0, 128),))
    leftover_cotan = normal_values(key_list[10], (SAMPLE_NUMBER, WIDEST_LOOKBEHIND), 1.0, 6.0, ((0, 128),))
    return {"lag_sequences": lag_sequences, "sample_cluster_label": sample_cluster_label, "entry_dense_matrix": entry_dense_matrix, "dense_matrix_middle": dense_matrix_middle, "dense_matrix_later": dense_matrix_later, "dense_matrix_last": dense_matrix_last, "past_coefficient_matrix": past_coefficient_matrix, "future_coefficient_matrix": future_coefficient_matrix, "generic_expansion_matrix": generic_expansion_matrix, "prediction_adjoint": prediction_adjoint, "leftover_cotan": leftover_cotan}


@jax.custom_vjp
def low(v):
    return lax.optimization_barrier(v.astype(jnp.bfloat16)).astype(jnp.float32)

@jax.custom_vjp
def low_back(v):
    return v

def low_keep(v):
    return (low(v), None)

def low_pass(kept, grad):
    return (grad,)

def back_keep(v):
    return (v, None)

def back_low(kept, grad):
    return (low(grad),)
low.defvjp(low_keep, low_pass)
low_back.defvjp(back_keep, back_low)
lookbehind_reaches = (42, 56, 126, 336)
upcoming_reaches = (6, 8, 18, 48)

def spread_across_members(values, periodicity_affiliation, lengths):
    return jnp.concatenate([periodicity_affiliation[:, group_index:group_index + 1] * values[:, :lengths[group_index]] for group_index in range(4)], axis=1)

def gather_items(values, periodicity_affiliation, lengths, span_width):
    summed = jnp.zeros((values.shape[0], span_width), values.dtype)
    begin = 0
    for group_index in range(4):
        segment = values[:, begin:begin + lengths[group_index]]
        summed = summed + periodicity_affiliation[:, group_index:group_index + 1] * jnp.pad(segment, ((0, 0), (0, span_width - lengths[group_index])))
        begin = begin + lengths[group_index]
    return summed

def lag_slot_flags(periodicity_affiliation, span_width):
    row_lengths = lax.optimization_barrier(jnp.sum(periodicity_affiliation * jnp.array(lookbehind_reaches, dtype=periodicity_affiliation.dtype)[None, :], axis=1))
    return (jnp.arange(span_width, dtype=periodicity_affiliation.dtype)[None, :] < row_lengths[:, None]).astype(periodicity_affiliation.dtype)

def product_outcome(left, right):
    return jnp.dot(left, right, precision=lax.Precision.HIGHEST)

def forward(lookbehind_place_ranks, parameter_tuple, periodicity_affiliation):
    entry_dense_matrix, dense_matrix_middle, dense_matrix_later, dense_matrix_last, past_coefficient_matrix, future_coefficient_matrix, generic_expansion_matrix = parameter_tuple
    carried_difference = lag_slot_flags(periodicity_affiliation, WIDEST_LOOKBEHIND) * lookbehind_place_ranks
    outlook_aggregate = jnp.zeros((lookbehind_place_ranks.shape[0], FAR_REACH), lookbehind_place_ranks.dtype)
    for module_position in range(UNIT_CHAIN):
        spread_copies = low(spread_across_members(carried_difference, periodicity_affiliation, lookbehind_reaches))
        act_one = low(jax.nn.silu(low_back(product_outcome(spread_copies, entry_dense_matrix[module_position]))))
        act_two = low(jax.nn.silu(low_back(product_outcome(act_one, dense_matrix_middle[module_position]))))
        act_three = low(jax.nn.silu(low_back(product_outcome(act_two, dense_matrix_later[module_position]))))
        activation_last = low(jax.nn.silu(low_back(product_outcome(act_three, dense_matrix_last[module_position]))))
        reverse_design_factors = low(low_back(product_outcome(activation_last, past_coefficient_matrix[module_position])))
        upcoming_weights_vector = low(low_back(product_outcome(activation_last, future_coefficient_matrix[module_position])))
        present_design = generic_expansion_matrix[module_position]
        combined_outlook_aggregates = low_back(jnp.concatenate([product_outcome(reverse_design_factors, present_design[:, :COMBINED_REACH]), product_outcome(upcoming_weights_vector, present_design[:, COMBINED_REACH:])], axis=1))
        carried_difference = carried_difference - gather_items(combined_outlook_aggregates[:, :COMBINED_REACH], periodicity_affiliation, lookbehind_reaches, WIDEST_LOOKBEHIND)
        outlook_aggregate = outlook_aggregate + gather_items(combined_outlook_aggregates[:, COMBINED_REACH:], periodicity_affiliation, upcoming_reaches, FAR_REACH)
    return (outlook_aggregate, carried_difference)

def reference(lag_sequences, sample_cluster_label, entry_dense_matrix, dense_matrix_middle, dense_matrix_later, dense_matrix_last, past_coefficient_matrix, future_coefficient_matrix, generic_expansion_matrix, prediction_adjoint, leftover_cotan):
    parameter_tuple = tuple((dense_table.astype(jnp.float32) for dense_table in (entry_dense_matrix, dense_matrix_middle, dense_matrix_later, dense_matrix_last, past_coefficient_matrix, future_coefficient_matrix, generic_expansion_matrix)))
    periodicity_affiliation = (sample_cluster_label[:, None] == jnp.arange(4, dtype=jnp.int32)[None, :]).astype(jnp.float32)
    module_pass_lines = math.gcd(SAMPLE_NUMBER, 4096)
    module_pass_number = SAMPLE_NUMBER // module_pass_lines
    piled_entries = (lag_sequences.astype(jnp.float32).reshape(module_pass_number, module_pass_lines, WIDEST_LOOKBEHIND), periodicity_affiliation.reshape(module_pass_number, module_pass_lines, 4), prediction_adjoint.astype(jnp.float32).reshape(module_pass_number, module_pass_lines, FAR_REACH), leftover_cotan.astype(jnp.float32).reshape(module_pass_number, module_pass_lines, WIDEST_LOOKBEHIND))

    def one_step(carry, inputs):
        rows_series, rows_onehot, rows_fore, rows_resid = inputs

        def run_rows(values, weight_tuple):
            return forward(values, weight_tuple, rows_onehot)
        outputs, pullback = jax.vjp(run_rows, rows_series, parameter_tuple)
        d_rows, d_weights = pullback((rows_fore, rows_resid))
        carry = jax.tree.map(jnp.add, carry, d_weights)
        return (carry, (outputs[0], outputs[1], d_rows))
    start_sums = tuple((jnp.zeros_like(dense_table) for dense_table in parameter_tuple))
    totals, (fore_rows, resid_rows, grad_rows) = lax.scan(one_step, start_sums, piled_entries)
    grad_scale = 1.0 / math.sqrt(SAMPLE_NUMBER)
    totals = tuple((total_sum * grad_scale for total_sum in totals))
    return (fore_rows.reshape(SAMPLE_NUMBER, FAR_REACH), resid_rows.reshape(SAMPLE_NUMBER, WIDEST_LOOKBEHIND), grad_rows.reshape(SAMPLE_NUMBER, WIDEST_LOOKBEHIND), totals[0], totals[1], totals[2], totals[3], totals[4], totals[5], totals[6])
```

```python
import functools
import math

import jax
import jax.numpy as jnp
from jax import lax
from jax.experimental import pallas as pl
from jax.experimental.pallas import tpu as pltpu
from jax.sharding import PartitionSpec as P

BF = jnp.bfloat16
F32 = jnp.float32
ROWS = 768
LOOKS = (42, 56, 126, 336)
LOOK_AT = (0, 42, 98, 224)
REACHES = (6, 8, 18, 48)
REACH_AT = (0, 6, 14, 32)
ENTRY, SECOND, THIRD, FOURTH, BACK, FORE, BASIS, USED = 0, 560, 1072, 1584, 2096, 2608, 3120, 3760
PACK = 3840
CHUNK, PIECE = PACK // 4, PACK // 16
VMEM_BYTES = 56 * 1024 * 1024
PARAMS = pltpu.CompilerParams(vmem_limit_bytes=VMEM_BYTES)


def place(y, x, z, c):
    y, x, z, c = y % 4, x % 4, z % 4, c % 2
    return ((((y * 2 + x // 2) * 4 + z) * 2) + x % 2) * 2 + c


def pairs(move):
    out = []
    for y in range(4):
        for x in range(4):
            for z in range(4):
                for c in range(2):
                    out.append((place(y, x, z, c), place(*move(y, x, z, c))))
    return tuple(out)


def to_core():
    return pairs(lambda y, x, z, c: (y, x, z, 1 - c))


def to_x(step):
    return pairs(lambda y, x, z, c: (y, x + step, z, c))


def to_x_by_core():
    return pairs(lambda y, x, z, c: (y, x + 1 - 2 * c, z, c))


def to_first(step):
    return pairs(lambda y, x, z, c: (y + step, x, z, c) if c == 0 else (y, x, z + step, c))


def to_second(step):
    return pairs(lambda y, x, z, c: (y, x, z + step, c) if c == 0 else (y + step, x, z, c))


def send(values, where):
    return lax.ppermute(values, ("dp", "mp"), where)


def lanes(rows, width=128):
    return lax.broadcasted_iota(jnp.int32, (rows, width), 1)


def turn(values, shift):
    return pltpu.roll(values, shift % 128, 1)


def widen_look(v, label):
    at = lanes(v[0].shape[0])
    zero = jnp.zeros_like(v[0])
    far = turn(v[0], 98)
    late = [turn(part, 96) for part in v]
    first = jnp.where(at < 42, v[0], jnp.where(at < 98, turn(v[0], 42), far))
    group = jnp.where(at < 42, 0, jnp.where(at < 98, 1, 2))
    out = [jnp.where(label == group, first, zero)]
    group = jnp.where(at < 96, 2, 3)
    out.append(jnp.where(label == group, jnp.where(at < 96, far, late[0]), zero))
    mine = label == 3
    out.append(jnp.where(mine, jnp.where(at < 96, late[0], late[1]), zero))
    out.append(jnp.where(mine, jnp.where(at < 96, late[1], late[2]), zero))
    out.append(jnp.where(mine & (at < 48), late[2], zero))
    return out


def pick_look(u, label):
    at = lanes(u[0].shape[0])
    zero = jnp.zeros_like(u[0])
    second = turn(u[0], -42)
    third = turn(jnp.where(at >= 98, u[0], u[1]), -98)
    fourth = [turn(jnp.where(at >= 96, u[i], u[i + 1]), -96) for i in (1, 2, 3)]
    chosen = jnp.where(
        label == 0, u[0], jnp.where(label == 1, second, jnp.where(label == 2, third, fourth[0]))
    )
    reach = jnp.where(label == 0, 42, jnp.where(label == 1, 56, jnp.where(label == 2, 126, 128)))
    out = [jnp.where(at < reach, chosen, zero)]
    mine = label == 3
    out.append(jnp.where(mine, fourth[1], zero))
    out.append(jnp.where(mine & (at < 80), fourth[2], zero))
    return out


def widen_reach(f, label):
    at = lanes(f.shape[0])
    spread = jnp.where(
        at < 54, turn(f, 48), jnp.where(at < 62, turn(f, 54), jnp.where(at < 80, turn(f, 62), turn(f, 80)))
    )
    group = jnp.where(at < 54, 0, jnp.where(at < 62, 1, jnp.where(at < 80, 2, 3)))
    return jnp.where((label == group) & (at >= 48), spread, jnp.zeros_like(f))


def pick_reach(u, label):
    at = lanes(u.shape[0])
    chosen = jnp.where(
        label == 0,
        turn(u, -48),
        jnp.where(label == 1, turn(u, -54), jnp.where(label == 2, turn(u, -62), turn(u, -80))),
    )
    reach = jnp.where(label == 0, 6, jnp.where(label == 1, 8, jnp.where(label == 2, 18, 48)))
    return jnp.where(at < reach, chosen, jnp.zeros_like(u))


def look_mask(label, block):
    at = lanes(label.shape[0]) + 128 * block
    reach = jnp.where(label == 0, 42, jnp.where(label == 1, 56, jnp.where(label == 2, 126, 336)))
    return at < reach


def padded(values, width):
    return jnp.concatenate(
        [values, jnp.zeros((values.shape[0], width - values.shape[1]), values.dtype)], axis=1
    )


def blocks_of(values):
    return [values[:, i : i + 128] for i in range(0, values.shape[1], 128)]


def by_columns(slots, begin, count):
    return jnp.concatenate([slot[begin : begin + count, :] for slot in slots], axis=1)


def by_rows(slots, begin, count):
    return jnp.concatenate(
        [
            jnp.concatenate(
                [slot[begin + 128 * i : begin + 128 * (i + 1), :] for i in range(count)], axis=1
            )
            for slot in slots
        ],
        axis=0,
    )


def dot(a, b):
    return jnp.dot(a, b, preferred_element_type=F32)


def dot_t(a, b):
    return lax.dot_general(a, b, (((1,), (1,)), ((), ())), preferred_element_type=F32)


def t_dot(a, b):
    return lax.dot_general(a, b, (((0,), (0,)), ((), ())), preferred_element_type=F32)


def silu_both(pre):
    s = 0.5 * jnp.tanh(0.5 * pre) + 0.5
    act = pre * s
    return act.astype(BF), (s + act * (1.0 - s)).astype(BF)


def run_forward(state, label, slots, e_ref, act_ref, slope_ref, theta_ref):
    wide = [part.astype(BF) for part in widen_look(state, label)]
    wide = jnp.concatenate(wide, axis=1)
    e_ref[...] = wide
    table = by_columns(slots, ENTRY, 560)
    table = jnp.concatenate([table, jnp.zeros((80, 512), BF)], axis=0)
    act, slope = silu_both(dot(wide, table))
    act_ref[0], slope_ref[0] = act, slope
    act, slope = silu_both(dot(act, by_rows(slots, SECOND, 4)))
    act_ref[1], slope_ref[1] = act, slope
    act, slope = silu_both(dot(act, by_columns(slots, THIRD, 512)))
    act_ref[2], slope_ref[2] = act, slope
    act, slope = silu_both(dot(act, by_rows(slots, FOURTH, 4)))
    act_ref[3], slope_ref[3] = act, slope
    theta_b = dot(act, by_columns(slots, BACK, 512)).astype(BF)
    theta_f = dot(act, by_columns(slots, FORE, 512)).astype(BF)
    theta_ref[0], theta_ref[1] = theta_b, theta_f
    basis = by_rows(slots, BASIS, 5)
    heads = dot(theta_b, basis)
    fore = dot(theta_f, basis[:, 512:])
    return blocks_of(heads), fore


def put_columns(out, begin, count, grad):
    for slot in range(4):
        out[slot % 2][slot // 2, begin : begin + count, :] = grad[
            :count, 128 * slot : 128 * (slot + 1)
        ].astype(BF)


def put_rows(out, begin, count, grad):
    for slot in range(4):
        for i in range(count):
            out[slot % 2][slot // 2, begin + 128 * i : begin + 128 * (i + 1), :] = grad[
                128 * slot : 128 * (slot + 1), 128 * i : 128 * (i + 1)
            ].astype(BF)


def run_backward(g, fore_wide, label, slots, e_ref, act_ref, slope_ref, theta_ref, out):
    for half in out:
        half[:, USED:PACK, :] = jnp.zeros((2, PACK - USED, 128), BF)
    wide = widen_look(g, label)
    d_back = jnp.concatenate([(-part).astype(BF) for part in wide], axis=1)
    d_fore = fore_wide.astype(BF)
    basis = by_rows(slots, BASIS, 5)
    d_theta_b = dot_t(d_back, basis).astype(BF)
    d_theta_f = dot_t(d_fore, basis[:, 512:]).astype(BF)
    grad = t_dot(theta_ref[0], d_back)
    last = grad[:, 512:] + t_dot(theta_ref[1], d_fore)
    put_rows(out, BASIS, 5, jnp.concatenate([grad[:, :512], last], axis=1))
    put_columns(out, BACK, 512, t_dot(act_ref[3], d_theta_b))
    put_columns(out, FORE, 512, t_dot(act_ref[3], d_theta_f))
    d_act = dot_t(d_theta_b, by_columns(slots, BACK, 512)) + dot_t(
        d_theta_f, by_columns(slots, FORE, 512)
    )
    d_pre = (d_act * slope_ref[3].astype(F32)).astype(BF)
    put_rows(out, FOURTH, 4, t_dot(act_ref[2], d_pre))
    d_act = dot_t(d_pre, by_rows(slots, FOURTH, 4))
    d_pre = (d_act * slope_ref[2].astype(F32)).astype(BF)
    put_columns(out, THIRD, 512, t_dot(act_ref[1], d_pre))
    d_act = dot_t(d_pre, by_columns(slots, THIRD, 512))
    d_pre = (d_act * slope_ref[1].astype(F32)).astype(BF)
    put_rows(out, SECOND, 4, t_dot(act_ref[0], d_pre))
    d_act = dot_t(d_pre, by_rows(slots, SECOND, 4))
    d_pre = (d_act * slope_ref[0].astype(F32)).astype(BF)
    put_columns(out, ENTRY, 560, t_dot(e_ref[...], d_pre))
    table = by_columns(slots, ENTRY, 560)
    table = jnp.concatenate([table, jnp.zeros((80, 512), BF)], axis=0)
    d_wide = blocks_of(dot_t(d_pre, table))
    return [old + new for old, new in zip(g, pick_look(d_wide, label))]


def pack_kernel(entry, second, third, fourth, back, fore, basis, one, two):
    for k, out in enumerate((one, two)):
        out[ENTRY:SECOND, :] = entry[k]
        out[THIRD:FOURTH, :] = third[k]
        out[BACK:FORE, :] = back[k]
        out[FORE:BASIS, :] = fore[k]
        for i in range(4):
            out[SECOND + 128 * i : SECOND + 128 * (i + 1), :] = second[k, :, 128 * i : 128 * (i + 1)]
            out[FOURTH + 128 * i : FOURTH + 128 * (i + 1), :] = fourth[k, :, 128 * i : 128 * (i + 1)]
        for i in range(5):
            out[BASIS + 128 * i : BASIS + 128 * (i + 1), :] = basis[k, :, 128 * i : 128 * (i + 1)]


def first_kernel(label, lag, s0, s1, s2, s3, state_out, look_out, e, act, slope, theta):
    labels = label[...]
    state = blocks_of(padded(lag[...], 384).astype(F32))
    state = [jnp.where(look_mask(labels, i), part, 0.0) for i, part in enumerate(state)]
    heads, fore = run_forward(state, labels, (s0, s1, s2, s3), e, act, slope, theta)
    for i, part in enumerate(pick_look(heads, labels)):
        state_out[:, 128 * i : 128 * (i + 1)] = state[i] - part
    look_out[...] = pick_reach(fore, labels)


def second_kernel(
    label, state_in, look_in, left, adjoint, s0, s1, s2, s3, rest, look, g_out, mine, theirs, e, act, slope, theta
):
    labels = label[...]
    slots = (s0, s1, s2, s3)
    state = blocks_of(state_in[...])
    heads, fore = run_forward(state, labels, slots, e, act, slope, theta)
    state = [old - part for old, part in zip(state, pick_look(heads, labels))]
    rest[...] = jnp.concatenate(state, axis=1)[:, :336]
    look[...] = (look_in[...] + pick_reach(fore, labels))[:, :48]
    g = blocks_of(padded(left[...], 384).astype(F32))
    fore_wide = widen_reach(padded(adjoint[...], 128).astype(F32), labels)
    g = run_backward(g, fore_wide, labels, slots, e, act, slope, theta, (mine, theirs))
    g_out[...] = jnp.concatenate(g, axis=1)


def third_kernel(label, g_in, adjoint, s0, s1, s2, s3, e, act, slope, theta, steep, mine, theirs):
    labels = label[...]
    g = blocks_of(g_in[...])
    fore_wide = widen_reach(padded(adjoint[...], 128).astype(F32), labels)
    g = run_backward(
        g, fore_wide, labels, (s0, s1, s2, s3), e, act, slope, theta, (mine, theirs)
    )
    g = [jnp.where(look_mask(labels, i), part, 0.0) for i, part in enumerate(g)]
    steep[...] = jnp.concatenate(g, axis=1)[:, :336]


def unpack_kernel(i1, i2, s0, s1, s2, s3, entry, second, third, fourth, back, fore, basis, whole, sem):
    copies = []
    for a, stack in zip((0, 3, 1, 2), (s0, s1, s2, s3)):
        chunk = lax.rem(i1[0] + a, 4)
        for slot, b in enumerate((0, 3, 1, 2)):
            piece = lax.rem(i2[0] + b, 4)
            at = pl.multiple_of(chunk * CHUNK + piece * PIECE, PIECE)
            copy = pltpu.make_async_copy(
                stack.at[slot], whole.at[:, pl.ds(at, PIECE), :], sem.at[len(copies)]
            )
            copy.start()
            copies.append(copy)
    for copy in copies:
        copy.wait()
    scale = 1.0 / math.sqrt(98304)

    def part(k, begin, count):
        return whole[k, begin : begin + count, :].astype(F32) * scale

    for k in range(2):
        entry[k] = part(k, ENTRY, 560)
        third[k] = part(k, THIRD, 512)
        back[k] = part(k, BACK, 512)
        fore[k] = part(k, FORE, 512)
        for i in range(4):
            second[k, :, 128 * i : 128 * (i + 1)] = part(k, SECOND + 128 * i, 128)
            fourth[k, :, 128 * i : 128 * (i + 1)] = part(k, FOURTH + 128 * i, 128)
        for i in range(5):
            basis[k, :, 128 * i : 128 * (i + 1)] = part(k, BASIS + 128 * i, 128)


def shape(*dims, kind=F32):
    return jax.ShapeDtypeStruct(dims, kind)


def whole_call(kernel, outs, name, scratch=(), in_specs=None):
    extra = {} if in_specs is None else {"in_specs": in_specs}
    return pl.pallas_call(
        kernel, out_shape=outs, scratch_shapes=scratch, compiler_params=PARAMS, name=name, **extra
    )


KEPT = [
    shape(ROWS, 640, kind=BF),
    shape(4, ROWS, 512, kind=BF),
    shape(4, ROWS, 512, kind=BF),
    shape(2, ROWS, 512, kind=BF),
]
HALF = [shape(2, PACK, 128, kind=BF)] * 2


def gather_weights(own):
    across = send(own, to_x_by_core())
    return own, send(own, to_core()), across, send(across, to_core())


def plus(*parts):
    return sum(part.astype(F32) for part in parts).astype(BF)


def shards(
    lag, label, entry, second, third, fourth, back, fore, basis, adjoint, left
):
    dp, mp = lax.axis_index("dp"), lax.axis_index("mp")
    y, z, core = dp // 8, dp % 4, mp % 2
    i1 = jnp.where(core == 0, y, z)
    i2 = jnp.where(core == 0, z, y)
    label = label[:, None]
    one, two = whole_call(
        pack_kernel, [shape(USED, 128, kind=BF)] * 2, "pack"
    )(entry, second, third, fourth, back, fore, basis)
    slots1 = gather_weights(one)
    slots2 = gather_weights(two)
    state1, look1, *kept = whole_call(
        first_kernel, [shape(ROWS, 384), shape(ROWS, 128)] + KEPT, "forward_one"
    )(label, lag, *slots1)
    rest, look, g1, mine2, theirs2 = whole_call(
        second_kernel,
        [shape(ROWS, 336), shape(ROWS, 48), shape(ROWS, 384)] + HALF,
        "block_two",
        scratch=[pltpu.VMEM(s.shape, s.dtype) for s in KEPT],
    )(label, state1, look1, left, adjoint, *slots2)
    steep, mine1, theirs1 = whole_call(
        third_kernel, [shape(ROWS, 336)] + HALF, "backward_one"
    )(label, g1, adjoint, *slots1, *kept)

    def first_axis(mine, theirs):
        both = plus(mine, send(theirs, to_core()))

        def chunk(a):
            return lax.dynamic_slice(both, (0, ((i1 + a) % 4) * CHUNK, 0), (2, CHUNK, 128))

        got = [send(chunk(a), to_first(a)) for a in (1, 3, 2)]
        return plus(chunk(0), *got)

    chunks = jnp.stack([first_axis(mine1, theirs1), first_axis(mine2, theirs2)], axis=1)

    def piece(b):
        return lax.dynamic_slice(
            chunks, (0, 0, ((i2 + b) % 4) * PIECE, 0), (2, 2, PIECE, 128)
        )

    got = [send(piece(b), to_second(b)) for b in (1, 3, 2)]
    done = plus(piece(0), *got)
    got = [send(done[1], to_x(1)), send(done[1], to_x(3)), send(done[0], to_x(2))]
    done = plus(done[0], *got)
    stack = jnp.stack([done] + [send(done, to_second(b)) for b in (1, 3, 2)])
    stacks = [stack] + [send(stack, to_first(a)) for a in (1, 3, 2)]
    smem = pl.BlockSpec(memory_space=pltpu.SMEM)
    grads = whole_call(
        unpack_kernel,
        [
            shape(2, 560, 128),
            shape(2, 128, 512),
            shape(2, 512, 128),
            shape(2, 128, 512),
            shape(2, 512, 128),
            shape(2, 512, 128),
            shape(2, 128, 640),
        ],
        "unpack",
        scratch=[pltpu.VMEM((2, PACK, 128), BF), pltpu.SemaphoreType.DMA((16,))],
        in_specs=[smem, smem] + [pl.BlockSpec(memory_space=pl.ANY)] * 4,
    )(i1.astype(jnp.int32)[None], i2.astype(jnp.int32)[None], *stacks)
    return (look, rest, steep, *grads)


def solution(mesh):
    windows = P(("dp", "mp"), None)
    columns, rows = P(None, None, "mp"), P(None, "mp", None)
    tables = (columns, rows, columns, rows, columns, columns, rows)
    return jax.shard_map(
        shards,
        mesh=mesh,
        in_specs=(windows, P(("dp", "mp")), *tables, windows, windows),
        out_specs=(windows, windows, windows, *tables),
        check_vma=False,
    )
```

```python
import functools
import math

import jax
import jax.numpy as jnp
from jax import lax
from jax.experimental import pallas as pl
from jax.experimental.pallas import tpu as pltpu
from jax.sharding import PartitionSpec as P

BF = jnp.bfloat16
F32 = jnp.float32
ROWS = 768
ENTRY, SECOND, THIRD, FOURTH, BACK, FORE, BASIS, USED = 0, 560, 1072, 1584, 2096, 2608, 3120, 3760
PACK = 3840
CHUNK, PIECE = PACK // 4, PACK // 16


def place(y, x, z, c):
    y, x, z, c = y % 4, x % 4, z % 4, c % 2
    return ((((y * 2 + x // 2) * 4 + z) * 2) + x % 2) * 2 + c


def pairs(move):
    out = []
    for y in range(4):
        for x in range(4):
            for z in range(4):
                for c in range(2):
                    out.append((place(y, x, z, c), place(*move(y, x, z, c))))
    return tuple(out)


def to_core():
    return pairs(lambda y, x, z, c: (y, x, z, 1 - c))


def to_x(step):
    return pairs(lambda y, x, z, c: (y, x + step, z, c))


def to_x_by_core():
    return pairs(lambda y, x, z, c: (y, x + 1 - 2 * c, z, c))


def to_first(step):
    return pairs(lambda y, x, z, c: (y + step, x, z, c) if c == 0 else (y, x, z + step, c))


def to_second(step):
    return pairs(lambda y, x, z, c: (y, x, z + step, c) if c == 0 else (y + step, x, z, c))


def send(values, where):
    return lax.ppermute(values, ("dp", "mp"), where)


def row_of(count, begin=0):
    return lax.broadcasted_iota(jnp.int32, (count, ROWS), 0) + begin


def turn(values, shift):
    return pltpu.roll(values, shift % values.shape[0], 0)


def widen_look(v, label):
    zero = jnp.float32(0)
    e = [label == g for g in range(4)]
    near = turn(v[:56], 2)
    far = turn(v[:128], 2)
    top = row_of(56) < 2
    tip = row_of(8) < 2
    mid = jnp.where(
        top, jnp.where(e[0], v[40:96], zero), jnp.where(e[1], near, zero)
    )
    joint = jnp.where(
        tip, jnp.where(e[1], near[:8], zero), jnp.where(e[2], far[:8], zero)
    )
    return jnp.concatenate(
        [
            jnp.where(e[0], v[:40], zero),
            mid,
            joint,
            jnp.where(e[2], far[8:], zero),
            jnp.where(e[3], v, zero),
        ],
        axis=0,
    )


def pick_look(u, label):
    zero = jnp.float32(0)
    e = [label == g for g in range(4)]
    last = jnp.where(e[3], u[224:560], zero)
    near = turn(u[40:104], -2)
    far = turn(u[96:224], -2)
    row = row_of(56)
    begin = jnp.where(
        e[2],
        far[:56],
        jnp.where(e[1], near[:56], jnp.where(e[0] & (row < 42), u[:56], last[:56])),
    )
    middle = jnp.where(e[2] & (row_of(72, 56) < 126), far[56:], last[56:128])
    return jnp.concatenate([begin, middle, last[128:]], axis=0)


def widen_reach(a, label):
    zero = jnp.float32(0)
    e = [label == g for g in range(4)]
    one = turn(a[:16], 6)
    two = turn(a[:24], 6)
    row = row_of(8)
    return jnp.concatenate(
        [
            jnp.where(row < 6, jnp.where(e[0], a[:8], zero), jnp.where(e[1], one[:8], zero)),
            jnp.where(row < 6, jnp.where(e[1], one[8:], zero), jnp.where(e[2], two[:8], zero)),
            jnp.where(e[2], two[8:], zero),
            jnp.where(e[3], a, zero),
        ],
        axis=0,
    )


def pick_reach(u, label):
    zero = jnp.float32(0)
    e = [label == g for g in range(4)]
    last = jnp.where(e[3], u[32:], zero)
    one = turn(u[:16], -6)
    two = turn(u[8:32], -6)
    row = row_of(8)
    return jnp.concatenate(
        [
            jnp.where(
                e[2],
                two[:8],
                jnp.where(e[1], one[:8], jnp.where(e[0] & (row < 6), u[:8], last[:8])),
            ),
            jnp.where(e[2] & (row_of(16, 8) < 18), two[8:], last[8:24]),
            last[24:],
        ],
        axis=0,
    )


def look_mask(label):
    reach = jnp.where(label == 0, 42, jnp.where(label == 1, 56, jnp.where(label == 2, 126, 336)))
    return row_of(336) < reach


def by_columns(slots, begin, count):
    return jnp.concatenate([slot[begin : begin + count, :] for slot in slots], axis=1)


def by_rows(slots, begin, count):
    return jnp.concatenate(
        [
            jnp.concatenate(
                [slot[begin + 128 * i : begin + 128 * (i + 1), :] for i in range(count)], axis=1
            )
            for slot in slots
        ],
        axis=0,
    )


def dot(a, b):
    return jnp.dot(a, b, preferred_element_type=F32)


def dot_t(a, b):
    return lax.dot_general(a, b, (((1,), (1,)), ((), ())), preferred_element_type=F32)


def t_dot(a, b):
    return lax.dot_general(a, b, (((0,), (0,)), ((), ())), preferred_element_type=F32)


def silu_both(pre):
    s = 0.5 * jnp.tanh(0.5 * pre) + 0.5
    act = pre * s
    return act.astype(BF), (s + act * (1.0 - s)).astype(BF)


TABLES = {
    "entry": (ENTRY, 560),
    "second": (SECOND, 512),
    "third": (THIRD, 512),
    "fourth": (FOURTH, 512),
    "back": (BACK, 512),
    "fore": (FORE, 512),
    "basis": (BASIS, 640),
}


class Weights:
    def __init__(self, slots):
        self.slots = slots

    def get(self, name):
        begin, count = TABLES[name]
        if name in ("second", "fourth"):
            return by_rows(self.slots, begin, 4)
        return by_columns(self.slots, begin, count)


def run_forward(state, label, weights, e_ref, act_ref, slope_ref, theta_ref):
    e_ref[...] = widen_look(state, label).astype(BF)
    act, slope = silu_both(t_dot(weights.get("entry"), e_ref[...]))
    act_ref[0], slope_ref[0] = act, slope
    for i, name in enumerate(("second", "third", "fourth")):
        act, slope = silu_both(t_dot(weights.get(name), act_ref[i]))
        act_ref[i + 1], slope_ref[i + 1] = act, slope
    theta_ref[0] = t_dot(weights.get("back"), act_ref[3]).astype(BF)
    theta_ref[1] = t_dot(weights.get("fore"), act_ref[3]).astype(BF)
    basis = weights.get("basis")
    return dot(basis[:560], theta_ref[0]), dot(basis[560:], theta_ref[1])


class Grads:
    def __init__(self, outs, base=0):
        self.outs, self.base = outs, base

    def put(self, name, grad):
        begin, count = TABLES[name]
        at = begin - self.base
        for slot in range(4):
            out = self.outs[slot % 2]
            if name in ("second", "fourth"):
                for i in range(4):
                    out[slot // 2, at + 128 * i : at + 128 * (i + 1), :] = grad[
                        128 * slot : 128 * (slot + 1), 128 * i : 128 * (i + 1)
                    ].astype(BF)
            else:
                out[slot // 2, at : at + count, :] = grad[:, 128 * slot : 128 * (slot + 1)].astype(BF)
        if name == "basis":
            for out in self.outs:
                out[:, USED - self.base : PACK - self.base, :] = jnp.zeros((2, PACK - USED, 128), BF)


def backward_heads(g, fore_wide, label, weights, act_ref, slope_ref, theta_ref, grads):
    d_back = -widen_look(g, label).astype(BF)
    d_fore = fore_wide.astype(BF)
    basis = weights.get("basis")
    d_theta_b = t_dot(basis[:560], d_back).astype(BF)
    d_theta_f = t_dot(basis[560:], d_fore).astype(BF)
    grads.put(
        "basis",
        jnp.concatenate([dot_t(d_back, theta_ref[0]), dot_t(d_fore, theta_ref[1])], axis=0),
    )
    d_act = dot(weights.get("back"), d_theta_b) + dot(weights.get("fore"), d_theta_f)
    grads.put("back", dot_t(act_ref[3], d_theta_b))
    grads.put("fore", dot_t(act_ref[3], d_theta_f))
    d_pre = (d_act * slope_ref[3].astype(F32)).astype(BF)
    grads.put("fourth", dot_t(act_ref[2], d_pre))
    return d_pre


def backward_layers(g, d_pre, label, weights, e_ref, act_ref, slope_ref, grads):
    d_act = dot(weights.get("fourth"), d_pre)
    d_pre = (d_act * slope_ref[2].astype(F32)).astype(BF)
    grads.put("third", dot_t(act_ref[1], d_pre))
    d_act = dot(weights.get("third"), d_pre)
    d_pre = (d_act * slope_ref[1].astype(F32)).astype(BF)
    grads.put("second", dot_t(act_ref[0], d_pre))
    d_act = dot(weights.get("second"), d_pre)
    d_pre = (d_act * slope_ref[0].astype(F32)).astype(BF)
    grads.put("entry", dot_t(e_ref[...], d_pre))
    return g + pick_look(dot(weights.get("entry"), d_pre), label)


def places():
    dp, core = lax.axis_index("dp"), lax.rem(lax.axis_index("mp"), 2)
    y, z = lax.div(dp, 8), lax.rem(dp, 4)
    return jnp.where(core == 0, y, z), jnp.where(core == 0, z, y)


def pack_kernel(k, *refs):
    ins, out, quarter = refs[:7], refs[7], refs[8:]
    entry, second, third, fourth, back, fore, basis = (ref.at[k] for ref in ins)
    out[ENTRY:SECOND, :] = entry[...]
    out[THIRD:FOURTH, :] = third[...]
    out[BACK:FORE, :] = back[...]
    out[FORE:BASIS, :] = fore[...]
    for i in range(4):
        out[SECOND + 128 * i : SECOND + 128 * (i + 1), :] = second[:, 128 * i : 128 * (i + 1)]
        out[FOURTH + 128 * i : FOURTH + 128 * (i + 1), :] = fourth[:, 128 * i : 128 * (i + 1)]
    for i in range(5):
        out[BASIS + 128 * i : BASIS + 128 * (i + 1), :] = basis[:, 128 * i : 128 * (i + 1)].T
    out[USED:PACK, :] = jnp.zeros((PACK - USED, 128), BF)
    if quarter:
        i1, _ = places()
        quarter[0][...] = out[pl.ds(pl.multiple_of(i1 * CHUNK, CHUNK), CHUNK), :]


def join_kernel(q0, q1, q2, q3, out):
    i1, _ = places()
    for a, quarter in zip((0, 3, 1, 2), (q0, q1, q2, q3)):
        begin = pl.multiple_of(lax.rem(i1 + a, 4) * CHUNK, CHUNK)
        out[pl.ds(begin, CHUNK), :] = quarter[...]


def first_kernel(label, lag, s0, s1, s2, s3, state_out, look_out, e, act, slope, theta):
    weights = Weights((s0, s1, s2, s3))
    labels = label[...]
    state = jnp.where(look_mask(labels), lag[...].astype(F32), 0.0)
    heads, fore = run_forward(state, labels, weights, e, act, slope, theta)
    state_out[...] = state - pick_look(heads, labels)
    look_out[...] = pick_reach(fore, labels)


def second_kernel(
    label, state_in, look_in, left, adjoint, s0, s1, s2, s3, rest, look, g_out, mine, theirs, e, act, slope, theta
):
    weights = Weights((s0, s1, s2, s3))
    labels = label[...]
    heads, fore = run_forward(state_in[...], labels, weights, e, act, slope, theta)
    rest[...] = state_in[...] - pick_look(heads, labels)
    look[...] = look_in[...] + pick_reach(fore, labels)
    grads = Grads((mine, theirs))
    g = left[...].astype(F32)
    fore_wide = widen_reach(adjoint[...].astype(F32), labels)
    d_pre = backward_heads(g, fore_wide, labels, weights, act, slope, theta, grads)
    g_out[...] = backward_layers(g, d_pre, labels, weights, e, act, slope, grads)


def third_kernel(label, g_in, adjoint, s0, s1, s2, s3, act, slope, theta, d_out, mine, theirs):
    grads = Grads((mine, theirs), FOURTH)
    labels = label[...]
    fore_wide = widen_reach(adjoint[...].astype(F32), labels)
    d_out[...] = backward_heads(
        g_in[...], fore_wide, labels, Weights((s0, s1, s2, s3)), act, slope, theta, grads
    )


def fourth_kernel(label, g_in, d_in, s0, s1, s2, s3, e, act, slope, steep, mine, theirs):
    grads = Grads((mine, theirs))
    labels = label[...]
    g = backward_layers(g_in[...], d_in[...], labels, Weights((s0, s1, s2, s3)), e, act, slope, grads)
    steep[...] = jnp.where(look_mask(labels), g, 0.0)


def cut_kernel(count, *refs):
    parts, outs, whole = refs[: 2 * count], refs[2 * count : -1], refs[-1]
    i1, _ = places()
    at = 0
    for mine, got in zip(parts[:count], parts[count:]):
        rows = mine.shape[1]
        whole[:, at : at + rows, :] = (
            mine[...].astype(F32) + got[...].astype(F32)
        ).astype(BF)
        at += rows
    for a, out in zip((1, 3, 2, 0), outs):
        begin = pl.multiple_of(lax.rem(i1 + a, 4) * CHUNK, CHUNK)
        out[...] = whole[:, pl.ds(begin, CHUNK), :]


def piece_kernel(*refs):
    chunks, outs, whole = refs[:8], refs[8:12], refs[12]
    _, i2 = places()
    for k in range(2):
        own, a, b, c = (ref[...].astype(F32) for ref in chunks[4 * k : 4 * k + 4])
        whole[:, k] = ((own + a) + (b + c)).astype(BF)
    for a, out in zip((1, 3, 2, 0), outs):
        begin = pl.multiple_of(lax.rem(i2 + a, 4) * PIECE, PIECE)
        out[...] = whole[:, :, pl.ds(begin, PIECE), :]


def unpack_kernel(s0, s1, s2, s3, entry, second, third, fourth, back, fore, basis, whole, sem):
    i1, i2 = places()
    copies = []
    for a, stack in zip((0, 3, 1, 2), (s0, s1, s2, s3)):
        chunk = lax.rem(i1 + a, 4)
        for slot, b in enumerate((0, 3, 1, 2)):
            piece = lax.rem(i2 + b, 4)
            at = pl.multiple_of(chunk * CHUNK + piece * PIECE, PIECE)
            copy = pltpu.make_async_copy(
                stack.at[slot], whole.at[:, pl.ds(at, PIECE), :], sem.at[len(copies)]
            )
            copy.start()
            copies.append(copy)
    for copy in copies:
        copy.wait()
    scale = 1.0 / math.sqrt(98304)

    def part(k, begin, count):
        return whole[k, begin : begin + count, :].astype(F32) * scale

    for k in range(2):
        entry[k] = part(k, ENTRY, 560)
        third[k] = part(k, THIRD, 512)
        back[k] = part(k, BACK, 512)
        fore[k] = part(k, FORE, 512)
        for i in range(4):
            second[k, :, 128 * i : 128 * (i + 1)] = part(k, SECOND + 128 * i, 128)
            fourth[k, :, 128 * i : 128 * (i + 1)] = part(k, FOURTH + 128 * i, 128)
        for i in range(5):
            basis[k, :, 128 * i : 128 * (i + 1)] = part(k, BASIS + 128 * i, 128).T


def shape(*dims, kind=F32):
    return jax.ShapeDtypeStruct(dims, kind)


def vmem(*dims, kind=BF):
    return pltpu.VMEM(dims, kind)


M1, M2, M3, M4, M5 = 12, 20, 12, 12, 8
DMA = pltpu.SemaphoreType.DMA
IN_VMEM = pl.BlockSpec(memory_space=pltpu.VMEM)
ANYWHERE = pl.BlockSpec(memory_space=pl.ANY)


def call(kernel, name, ins, outs, scratch, mib, us):
    return pl.pallas_call(
        kernel,
        out_shape=[o[0] for o in outs],
        in_specs=ins,
        out_specs=[o[1] for o in outs],
        scratch_shapes=scratch,
        compiler_params=pltpu.CompilerParams(vmem_limit_bytes=mib * 1024 * 1024),
        cost_estimate=pl.CostEstimate(
            flops=int(us * 8e8), bytes_accessed=int(us * 1e6), transcendentals=0
        ),
        name=name,
    )


ACTS = (4, 512, ROWS)
KEPT = [(560, ROWS), ACTS, ACTS, (2, 512, ROWS)]
TOP, LOW = PACK - FOURTH, FOURTH


def plus(*parts):
    return sum(part.astype(F32) for part in parts).astype(BF)


def shards(lag, label, entry, second, third, fourth, back, fore, basis, adjoint, left):
    label = label[None, :]
    lag, adjoint, left = lag.T, adjoint.T, left.T
    whole, part = shape(PACK, 128, kind=BF), shape(CHUNK, 128, kind=BF)
    tables = (entry, second, third, fourth, back, fore, basis)
    two, quarter = call(
        functools.partial(pack_kernel, 1), "pack_two", [IN_VMEM] * 7, [(whole, IN_VMEM), (part, IN_VMEM)], [], 60, 2
    )(*tables)
    quarter, *tables = lax.optimization_barrier((quarter, *tables))
    one = call(functools.partial(pack_kernel, 0), "pack_one", [IN_VMEM] * 7, [(whole, IN_VMEM)], [], 60, 2)(*tables)[0]
    quarter = send(quarter, to_x_by_core())
    quarters = [quarter]
    one, quarters[0] = lax.optimization_barrier((one, quarters[0]))
    across = send(one, to_x_by_core())
    quarters += [send(quarters[0], to_first(a)) for a in (1, 3, 2)]
    across, *quarters = lax.optimization_barrier((across, *quarters))
    slots1 = (one, send(one, to_core()), across, send(across, to_core()))
    across = call(join_kernel, "join", [IN_VMEM] * 4, [(whole, IN_VMEM)], [], M5, 1)(*quarters)[0]
    slots2 = (two, send(two, to_core()), across, send(across, to_core()))
    state1, look1, e1, act1, slope1, theta1 = call(
        first_kernel,
        "forward_one",
        [IN_VMEM] * 6,
        [(shape(336, ROWS), IN_VMEM), (shape(48, ROWS), IN_VMEM)]
        + [(shape(*k, kind=BF), IN_VMEM) for k in KEPT],
        [],
        M1,
        6,
    )(label, lag, *slots1)
    rest, look, g1, mine2, theirs2 = call(
        second_kernel,
        "block_two",
        [IN_VMEM] * 9,
        [(shape(336, ROWS), IN_VMEM), (shape(48, ROWS), IN_VMEM), (shape(336, ROWS), IN_VMEM)]
        + [(shape(2, PACK, 128, kind=BF), IN_VMEM)] * 2,
        [vmem(*k) for k in KEPT],
        M2,
        14,
    )(label, state1, look1, left, adjoint, *slots2)
    got2 = send(theirs2, to_core())
    d_pre, mine1a, theirs1a = call(
        third_kernel,
        "backward_one_heads",
        [IN_VMEM] * 10,
        [(shape(512, ROWS, kind=BF), IN_VMEM)] + [(shape(2, TOP, 128, kind=BF), IN_VMEM)] * 2,
        [],
        M3,
        6,
    )(label, g1, adjoint, *slots1, act1, slope1, theta1)
    got1a = send(theirs1a, to_core())

    def cut(mine, got, name):
        return call(
            functools.partial(cut_kernel, len(mine)),
            name,
            [IN_VMEM] * (2 * len(mine)),
            [(shape(2, CHUNK, 128, kind=BF), IN_VMEM)] * 4,
            [vmem(2, PACK, 128)],
            M5,
            2,
        )(*mine, *got)

    *out2, own2 = cut([mine2], [got2], "cut_two")
    got2 = [send(part, to_first(a)) for part, a in zip(out2, (1, 3, 2))]
    d_pre, *out2 = lax.optimization_barrier((d_pre, *out2))
    steep, mine1b, theirs1b = call(
        fourth_kernel,
        "backward_one_layers",
        [IN_VMEM] * 10,
        [(shape(336, ROWS), IN_VMEM)] + [(shape(2, LOW, 128, kind=BF), IN_VMEM)] * 2,
        [],
        M4,
        6,
    )(label, g1, d_pre, *slots1, e1, act1, slope1)
    got1b = send(theirs1b, to_core())
    *out1, own1 = cut([mine1b, mine1a], [got1b, got1a], "cut_one")
    got1 = [send(part, to_first(a)) for part, a in zip(out1, (1, 3, 2))]
    *out, own = call(
        piece_kernel,
        "pieces",
        [IN_VMEM] * 8,
        [(shape(2, 2, PIECE, 128, kind=BF), IN_VMEM)] * 4,
        [vmem(2, 2, CHUNK, 128)],
        M5,
        2,
    )(own1, *got1, own2, *got2)
    got = [send(part, to_second(b)) for part, b in zip(out, (1, 3, 2))]
    done = plus(own, *got)
    got = [send(done[1], to_x(1)), send(done[1], to_x(3)), send(done[0], to_x(2))]
    done = plus(done[0], *got)
    stack = jnp.stack([done] + [send(done, to_second(b)) for b in (1, 3, 2)])
    stacks = [stack] + [send(stack, to_first(a)) for a in (1, 3, 2)]
    grads = call(
        unpack_kernel,
        "unpack",
        [ANYWHERE] * 4,
        [
            (shape(*dims), IN_VMEM)
            for dims in (
                (2, 560, 128), (2, 128, 512), (2, 512, 128), (2, 128, 512), (2, 512, 128), (2, 512, 128), (2, 128, 640),
            )
        ],
        [vmem(2, PACK, 128), DMA((16,))],
        32,
        3,
    )(*stacks)
    return (look.T, rest.T, steep.T, *grads)


def solution(mesh):
    windows = P(("dp", "mp"), None)
    columns, rows = P(None, None, "mp"), P(None, "mp", None)
    tables = (columns, rows, columns, rows, columns, columns, rows)
    return jax.shard_map(
        shards,
        mesh=mesh,
        in_specs=(windows, P(("dp", "mp")), *tables, windows, windows),
        out_specs=(windows, windows, windows, *tables),
        check_vma=False,
    )
```

```python
import functools
import math

import jax
import jax.numpy as jnp
from jax import lax
from jax.experimental import pallas as pl
from jax.experimental.pallas import tpu as pltpu
from jax.sharding import PartitionSpec as P

BF = jnp.bfloat16
F32 = jnp.float32
ROWS = 768
ENTRY, SECOND, THIRD, FOURTH, BACK, FORE, BASIS, USED = 0, 560, 1072, 1584, 2096, 2608, 3120, 3760
PACK = 3840
PEERS = (1, 3, 2)
CHUNK, PIECE = PACK // 4, PACK // 16


def place(y, x, z, c):
    y, x, z, c = y % 4, x % 4, z % 4, c % 2
    return ((((y * 2 + x // 2) * 4 + z) * 2) + x % 2) * 2 + c


def pairs(move):
    out = []
    for y in range(4):
        for x in range(4):
            for z in range(4):
                for c in range(2):
                    out.append((place(y, x, z, c), place(*move(y, x, z, c))))
    return tuple(out)


def to_core():
    return pairs(lambda y, x, z, c: (y, x, z, 1 - c))


def to_x(bits):
    return pairs(lambda y, x, z, c: (y, x ^ bits, z, c))


def to_x_by_core():
    return pairs(lambda y, x, z, c: (y, x ^ (1 if c == 0 else 3), z, c))


def to_first(bits):
    return pairs(lambda y, x, z, c: (y ^ bits, x, z, c) if c == 0 else (y, x, z ^ bits, c))


def to_second(bits):
    return pairs(lambda y, x, z, c: (y, x, z ^ bits, c) if c == 0 else (y ^ bits, x, z, c))


def send(values, where):
    return lax.ppermute(values, ("dp", "mp"), where)


def row_of(count, begin=0):
    return lax.broadcasted_iota(jnp.int32, (count, ROWS), 0) + begin


def turn(values, shift):
    return pltpu.roll(values, shift % values.shape[0], 0)


def widen_look(v, label):
    zero = jnp.float32(0)
    e = [label == g for g in range(4)]
    near = turn(v[:56], 2)
    far = turn(v[:128], 2)
    top = row_of(56) < 2
    tip = row_of(8) < 2
    mid = jnp.where(
        top, jnp.where(e[0], v[40:96], zero), jnp.where(e[1], near, zero)
    )
    joint = jnp.where(
        tip, jnp.where(e[1], near[:8], zero), jnp.where(e[2], far[:8], zero)
    )
    return jnp.concatenate(
        [
            jnp.where(e[0], v[:40], zero),
            mid,
            joint,
            jnp.where(e[2], far[8:], zero),
            jnp.where(e[3], v, zero),
        ],
        axis=0,
    )


def pick_look(u, label):
    zero = jnp.float32(0)
    e = [label == g for g in range(4)]
    last = jnp.where(e[3], u[224:560], zero)
    near = turn(u[40:104], -2)
    far = turn(u[96:224], -2)
    row = row_of(56)
    begin = jnp.where(
        e[2],
        far[:56],
        jnp.where(e[1], near[:56], jnp.where(e[0] & (row < 42), u[:56], last[:56])),
    )
    middle = jnp.where(e[2] & (row_of(72, 56) < 126), far[56:], last[56:128])
    return jnp.concatenate([begin, middle, last[128:]], axis=0)


def widen_reach(a, label):
    zero = jnp.float32(0)
    e = [label == g for g in range(4)]
    one = turn(a[:16], 6)
    two = turn(a[:24], 6)
    row = row_of(8)
    return jnp.concatenate(
        [
            jnp.where(row < 6, jnp.where(e[0], a[:8], zero), jnp.where(e[1], one[:8], zero)),
            jnp.where(row < 6, jnp.where(e[1], one[8:], zero), jnp.where(e[2], two[:8], zero)),
            jnp.where(e[2], two[8:], zero),
            jnp.where(e[3], a, zero),
        ],
        axis=0,
    )


def pick_reach(u, label):
    zero = jnp.float32(0)
    e = [label == g for g in range(4)]
    last = jnp.where(e[3], u[32:], zero)
    one = turn(u[:16], -6)
    two = turn(u[8:32], -6)
    row = row_of(8)
    return jnp.concatenate(
        [
            jnp.where(
                e[2],
                two[:8],
                jnp.where(e[1], one[:8], jnp.where(e[0] & (row < 6), u[:8], last[:8])),
            ),
            jnp.where(e[2] & (row_of(16, 8) < 18), two[8:], last[8:24]),
            last[24:],
        ],
        axis=0,
    )


def look_mask(label):
    reach = jnp.where(label == 0, 42, jnp.where(label == 1, 56, jnp.where(label == 2, 126, 336)))
    return row_of(336) < reach


def by_columns(slots, begin, count):
    return jnp.concatenate([slot[begin : begin + count, :] for slot in slots], axis=1)


def by_rows(slots, begin, count):
    return jnp.concatenate(
        [
            jnp.concatenate(
                [slot[begin + 128 * i : begin + 128 * (i + 1), :] for i in range(count)], axis=1
            )
            for slot in slots
        ],
        axis=0,
    )


def dot(a, b):
    return jnp.dot(a, b, preferred_element_type=F32)


def dot_t(a, b):
    return lax.dot_general(a, b, (((1,), (1,)), ((), ())), preferred_element_type=F32)


def t_dot(a, b):
    return lax.dot_general(a, b, (((0,), (0,)), ((), ())), preferred_element_type=F32)


def silu_both(pre):
    s = 0.5 * jnp.tanh(0.5 * pre) + 0.5
    act = pre * s
    return act.astype(BF), (s + act * (1.0 - s)).astype(BF)


TABLES = {
    "entry": (ENTRY, 560),
    "second": (SECOND, 512),
    "third": (THIRD, 512),
    "fourth": (FOURTH, 512),
    "back": (BACK, 512),
    "fore": (FORE, 512),
    "basis": (BASIS, 640),
}


class Weights:
    def __init__(self, slots):
        self.slots = slots

    def get(self, name):
        begin, count = TABLES[name]
        if name in ("second", "fourth"):
            return by_rows(self.slots, begin, 4)
        return by_columns(self.slots, begin, count)


def run_forward(state, label, weights, e_ref, act_ref, slope_ref, theta_ref):
    e_ref[...] = widen_look(state, label).astype(BF)
    act, slope = silu_both(t_dot(weights.get("entry"), e_ref[...]))
    act_ref[0], slope_ref[0] = act, slope
    for i, name in enumerate(("second", "third", "fourth")):
        act, slope = silu_both(t_dot(weights.get(name), act_ref[i]))
        act_ref[i + 1], slope_ref[i + 1] = act, slope
    theta_ref[0] = t_dot(weights.get("back"), act_ref[3]).astype(BF)
    theta_ref[1] = t_dot(weights.get("fore"), act_ref[3]).astype(BF)
    basis = weights.get("basis")
    return dot(basis[:560], theta_ref[0]), dot(basis[560:], theta_ref[1])


class Grads:
    def __init__(self, outs, base=0):
        self.outs, self.base = outs, base

    def put(self, name, grad):
        begin, count = TABLES[name]
        at = begin - self.base
        for slot in range(4):
            out = self.outs[slot % 2]
            if name in ("second", "fourth"):
                for i in range(4):
                    out[slot // 2, at + 128 * i : at + 128 * (i + 1), :] = grad[
                        128 * slot : 128 * (slot + 1), 128 * i : 128 * (i + 1)
                    ].astype(BF)
            else:
                out[slot // 2, at : at + count, :] = grad[:, 128 * slot : 128 * (slot + 1)].astype(BF)
        if name == "basis":
            for out in self.outs:
                out[:, USED - self.base : PACK - self.base, :] = jnp.zeros((2, PACK - USED, 128), BF)


def backward_heads(g, fore_wide, label, weights, act_ref, slope_ref, theta_ref, grads):
    d_back = -widen_look(g, label).astype(BF)
    d_fore = fore_wide.astype(BF)
    basis = weights.get("basis")
    d_theta_b = t_dot(basis[:560], d_back).astype(BF)
    d_theta_f = t_dot(basis[560:], d_fore).astype(BF)
    grads.put(
        "basis",
        jnp.concatenate([dot_t(d_back, theta_ref[0]), dot_t(d_fore, theta_ref[1])], axis=0),
    )
    d_act = dot(weights.get("back"), d_theta_b) + dot(weights.get("fore"), d_theta_f)
    grads.put("back", dot_t(act_ref[3], d_theta_b))
    grads.put("fore", dot_t(act_ref[3], d_theta_f))
    d_pre = (d_act * slope_ref[3].astype(F32)).astype(BF)
    grads.put("fourth", dot_t(act_ref[2], d_pre))
    return d_pre


def backward_layers(g, d_pre, label, weights, e_ref, act_ref, slope_ref, grads):
    d_act = dot(weights.get("fourth"), d_pre)
    d_pre = (d_act * slope_ref[2].astype(F32)).astype(BF)
    grads.put("third", dot_t(act_ref[1], d_pre))
    d_act = dot(weights.get("third"), d_pre)
    d_pre = (d_act * slope_ref[1].astype(F32)).astype(BF)
    grads.put("second", dot_t(act_ref[0], d_pre))
    d_act = dot(weights.get("second"), d_pre)
    d_pre = (d_act * slope_ref[0].astype(F32)).astype(BF)
    grads.put("entry", dot_t(e_ref[...], d_pre))
    return g + pick_look(dot(weights.get("entry"), d_pre), label)


def places():
    dp, core = lax.axis_index("dp"), lax.rem(lax.axis_index("mp"), 2)
    y, z = lax.div(dp, 8), lax.rem(dp, 4)
    return jnp.where(core == 0, y, z), jnp.where(core == 0, z, y)


def pack_kernel(k, *refs):
    ins, out, quarter = refs[:7], refs[7], refs[8:]
    entry, second, third, fourth, back, fore, basis = (ref.at[k] for ref in ins)
    out[ENTRY:SECOND, :] = entry[...]
    out[THIRD:FOURTH, :] = third[...]
    out[BACK:FORE, :] = back[...]
    out[FORE:BASIS, :] = fore[...]
    for i in range(4):
        out[SECOND + 128 * i : SECOND + 128 * (i + 1), :] = second[:, 128 * i : 128 * (i + 1)]
        out[FOURTH + 128 * i : FOURTH + 128 * (i + 1), :] = fourth[:, 128 * i : 128 * (i + 1)]
    for i in range(5):
        out[BASIS + 128 * i : BASIS + 128 * (i + 1), :] = basis[:, 128 * i : 128 * (i + 1)].T
    out[USED:PACK, :] = jnp.zeros((PACK - USED, 128), BF)
    if quarter:
        i1, _ = places()
        quarter[0][...] = out[pl.ds(pl.multiple_of(i1 * CHUNK, CHUNK), CHUNK), :]


def join_kernel(q0, q1, q2, q3, out):
    i1, _ = places()
    for bits, quarter in zip((0, *PEERS), (q0, q1, q2, q3)):
        begin = pl.multiple_of((i1 ^ bits) * CHUNK, CHUNK)
        out[pl.ds(begin, CHUNK), :] = quarter[...]


def first_kernel(label, lag, s0, s1, s2, s3, state_out, look_out, e, act, slope, theta):
    weights = Weights((s0, s1, s2, s3))
    labels = label[...]
    state = jnp.where(look_mask(labels), lag[...].astype(F32), 0.0)
    heads, fore = run_forward(state, labels, weights, e, act, slope, theta)
    state_out[...] = state - pick_look(heads, labels)
    look_out[...] = pick_reach(fore, labels)


def second_kernel(
    label, state_in, look_in, left, adjoint, s0, s1, s2, s3, rest, look, g_out, mine, theirs, e, act, slope, theta
):
    weights = Weights((s0, s1, s2, s3))
    labels = label[...]
    heads, fore = run_forward(state_in[...], labels, weights, e, act, slope, theta)
    rest[...] = state_in[...] - pick_look(heads, labels)
    look[...] = look_in[...] + pick_reach(fore, labels)
    grads = Grads((mine, theirs))
    g = left[...].astype(F32)
    fore_wide = widen_reach(adjoint[...].astype(F32), labels)
    d_pre = backward_heads(g, fore_wide, labels, weights, act, slope, theta, grads)
    g_out[...] = backward_layers(g, d_pre, labels, weights, e, act, slope, grads)


def third_kernel(label, g_in, adjoint, s0, s1, s2, s3, act, slope, theta, d_out, mine, theirs):
    grads = Grads((mine, theirs), FOURTH)
    labels = label[...]
    fore_wide = widen_reach(adjoint[...].astype(F32), labels)
    d_out[...] = backward_heads(
        g_in[...], fore_wide, labels, Weights((s0, s1, s2, s3)), act, slope, theta, grads
    )


def fourth_kernel(label, g_in, d_in, s0, s1, s2, s3, e, act, slope, steep, mine, theirs):
    grads = Grads((mine, theirs))
    labels = label[...]
    g = backward_layers(g_in[...], d_in[...], labels, Weights((s0, s1, s2, s3)), e, act, slope, grads)
    steep[...] = jnp.where(look_mask(labels), g, 0.0)


def cut_kernel(count, *refs):
    parts, outs, whole = refs[: 2 * count], refs[2 * count : -1], refs[-1]
    i1, _ = places()
    at = 0
    for mine, got in zip(parts[:count], parts[count:]):
        rows = mine.shape[1]
        whole[:, at : at + rows, :] = (
            mine[...].astype(F32) + got[...].astype(F32)
        ).astype(BF)
        at += rows
    for bits, out in zip((*PEERS, 0), outs):
        begin = pl.multiple_of((i1 ^ bits) * CHUNK, CHUNK)
        out[...] = whole[:, pl.ds(begin, CHUNK), :]


def piece_kernel(*refs):
    chunks, outs, whole = refs[:8], refs[8:12], refs[12]
    _, i2 = places()
    for k in range(2):
        own, a, b, c = (ref[...].astype(F32) for ref in chunks[4 * k : 4 * k + 4])
        whole[:, k] = ((own + a) + (b + c)).astype(BF)
    for bits, out in zip((*PEERS, 0), outs):
        begin = pl.multiple_of((i2 ^ bits) * PIECE, PIECE)
        out[...] = whole[:, :, pl.ds(begin, PIECE), :]


def unpack_kernel(s0, s1, s2, s3, *refs):
    outs, whole, bufs, sem = refs[:7], refs[7], refs[8:15], refs[15]
    i1, i2 = places()
    for a, stack in zip((0, *PEERS), (s0, s1, s2, s3)):
        for slot, b in enumerate((0, *PEERS)):
            at = pl.multiple_of((i1 ^ a) * CHUNK + (i2 ^ b) * PIECE, PIECE)
            whole[:, pl.ds(at, PIECE), :] = stack[slot]
    scale = 1.0 / math.sqrt(98304)
    copies = []
    for (name, (begin, count)), out, buf in zip(TABLES.items(), outs, bufs):
        for k in range(2):
            if buf.shape[2] == 128:
                buf[k] = whole[k, begin : begin + count, :].astype(F32) * scale
            else:
                for i in range(count // 128):
                    part = whole[k, begin + 128 * i : begin + 128 * (i + 1), :].astype(F32) * scale
                    buf[k, :, 128 * i : 128 * (i + 1)] = part.T if name == "basis" else part
        copies.append(pltpu.make_async_copy(buf, out, sem.at[len(copies)]))
        copies[-1].start()
    for copy in copies:
        copy.wait()


def shape(*dims, kind=F32):
    return jax.ShapeDtypeStruct(dims, kind)


def vmem(*dims, kind=BF):
    return pltpu.VMEM(dims, kind)


M1, M2, M3, M4, M5 = 12, 20, 12, 12, 8
DMA = pltpu.SemaphoreType.DMA
IN_VMEM = pl.BlockSpec(memory_space=pltpu.VMEM)
ANYWHERE = pl.BlockSpec(memory_space=pl.ANY)


def call(kernel, name, ins, outs, scratch, mib, us):
    return pl.pallas_call(
        kernel,
        out_shape=[o[0] for o in outs],
        in_specs=ins,
        out_specs=[o[1] for o in outs],
        scratch_shapes=scratch,
        compiler_params=pltpu.CompilerParams(vmem_limit_bytes=mib * 1024 * 1024),
        cost_estimate=pl.CostEstimate(
            flops=int(us * 8e8), bytes_accessed=int(us * 1e6), transcendentals=0
        ),
        name=name,
    )


ACTS = (4, 512, ROWS)
KEPT = [(560, ROWS), ACTS, ACTS, (2, 512, ROWS)]
TOP, LOW = PACK - FOURTH, FOURTH


def plus(*parts):
    return sum(part.astype(F32) for part in parts).astype(BF)


def shards(lag, label, entry, second, third, fourth, back, fore, basis, adjoint, left):
    label = label[None, :]
    lag, adjoint, left = lag.T, adjoint.T, left.T
    whole, part = shape(PACK, 128, kind=BF), shape(CHUNK, 128, kind=BF)
    tables = (entry, second, third, fourth, back, fore, basis)
    two, quarter = call(
        functools.partial(pack_kernel, 1), "pack_two", [IN_VMEM] * 7, [(whole, IN_VMEM), (part, IN_VMEM)], [], 60, 2
    )(*tables)
    quarter, *tables = lax.optimization_barrier((quarter, *tables))
    one = call(functools.partial(pack_kernel, 0), "pack_one", [IN_VMEM] * 7, [(whole, IN_VMEM)], [], 60, 2)(*tables)[0]
    quarter = send(quarter, to_x_by_core())
    quarters = [quarter]
    one, quarters[0] = lax.optimization_barrier((one, quarters[0]))
    across = send(one, to_x_by_core())
    quarters += [send(quarters[0], to_first(a)) for a in PEERS]
    across, *quarters = lax.optimization_barrier((across, *quarters))
    slots1 = (one, send(one, to_core()), across, send(across, to_core()))
    across = call(join_kernel, "join", [IN_VMEM] * 4, [(whole, IN_VMEM)], [], M5, 1)(*quarters)[0]
    slots2 = (two, send(two, to_core()), across, send(across, to_core()))
    state1, look1, e1, act1, slope1, theta1 = call(
        first_kernel,
        "forward_one",
        [IN_VMEM] * 6,
        [(shape(336, ROWS), IN_VMEM), (shape(48, ROWS), IN_VMEM)]
        + [(shape(*k, kind=BF), IN_VMEM) for k in KEPT],
        [],
        M1,
        6,
    )(label, lag, *slots1)
    rest, look, g1, mine2, theirs2 = call(
        second_kernel,
        "block_two",
        [IN_VMEM] * 9,
        [(shape(336, ROWS), IN_VMEM), (shape(48, ROWS), IN_VMEM), (shape(336, ROWS), IN_VMEM)]
        + [(shape(2, PACK, 128, kind=BF), IN_VMEM)] * 2,
        [vmem(*k) for k in KEPT],
        M2,
        14,
    )(label, state1, look1, left, adjoint, *slots2)
    got2 = send(theirs2, to_core())
    d_pre, mine1a, theirs1a = call(
        third_kernel,
        "backward_one_heads",
        [IN_VMEM] * 10,
        [(shape(512, ROWS, kind=BF), IN_VMEM)] + [(shape(2, TOP, 128, kind=BF), IN_VMEM)] * 2,
        [],
        M3,
        6,
    )(label, g1, adjoint, *slots1, act1, slope1, theta1)
    got1a = send(theirs1a, to_core())

    def cut(mine, got, name):
        return call(
            functools.partial(cut_kernel, len(mine)),
            name,
            [IN_VMEM] * (2 * len(mine)),
            [(shape(2, CHUNK, 128, kind=BF), IN_VMEM)] * 4,
            [vmem(2, PACK, 128)],
            M5,
            2,
        )(*mine, *got)

    *out2, own2 = cut([mine2], [got2], "cut_two")
    got2 = [send(part, to_first(a)) for part, a in zip(out2, PEERS)]
    d_pre, *out2 = lax.optimization_barrier((d_pre, *out2))
    steep, mine1b, theirs1b = call(
        fourth_kernel,
        "backward_one_layers",
        [IN_VMEM] * 10,
        [(shape(336, ROWS), IN_VMEM)] + [(shape(2, LOW, 128, kind=BF), IN_VMEM)] * 2,
        [],
        M4,
        6,
    )(label, g1, d_pre, *slots1, e1, act1, slope1)
    got1b = send(theirs1b, to_core())
    *out1, own1 = cut([mine1b, mine1a], [got1b, got1a], "cut_one")
    got1 = [send(part, to_first(a)) for part, a in zip(out1, PEERS)]
    *out, own = call(
        piece_kernel,
        "pieces",
        [IN_VMEM] * 8,
        [(shape(2, 2, PIECE, 128, kind=BF), IN_VMEM)] * 4,
        [vmem(2, 2, CHUNK, 128)],
        M5,
        2,
    )(own1, *got1, own2, *got2)
    got = [send(part, to_second(b)) for part, b in zip(out, PEERS)]
    done = plus(own, *got)
    got = [send(done[1], to_x(1)), send(done[1], to_x(3)), send(done[0], to_x(2))]
    done = plus(done[0], *got)
    stack = jnp.stack([done] + [send(done, to_second(b)) for b in PEERS])
    stacks = [stack] + [send(stack, to_first(a)) for a in PEERS]
    outs = (
        (2, 560, 128), (2, 128, 512), (2, 512, 128), (2, 128, 512), (2, 512, 128), (2, 512, 128), (2, 128, 640),
    )
    grads = call(
        unpack_kernel,
        "unpack",
        [IN_VMEM] * 4,
        [(shape(*dims), ANYWHERE) for dims in outs],
        [vmem(2, PACK, 128)] + [vmem(*dims, kind=F32) for dims in outs] + [DMA((7,))],
        16,
        3,
    )(*stacks)
    return (look.T, rest.T, steep.T, *grads)


def solution(mesh):
    windows = P(("dp", "mp"), None)
    columns, rows = P(None, None, "mp"), P(None, "mp", None)
    tables = (columns, rows, columns, rows, columns, columns, rows)
    return jax.shard_map(
        shards,
        mesh=mesh,
        in_specs=(windows, P(("dp", "mp")), *tables, windows, windows),
        out_specs=(windows, windows, windows, *tables),
        check_vma=False,
    )
```

```python
import functools
import math

import jax
import jax.numpy as jnp
from jax import lax
from jax.experimental import pallas as pl
from jax.experimental.pallas import tpu as pltpu
from jax.sharding import PartitionSpec as P

BF = jnp.bfloat16
F32 = jnp.float32
ROWS = 768
ENTRY, SECOND, THIRD, FOURTH, BACK, FORE, BASIS, USED = 0, 560, 1072, 1584, 2096, 2608, 3120, 3760
PACK = 3840
PEERS = (1, 3, 2)
CHUNK, PIECE = PACK // 4, PACK // 16


def place(y, x, z, c):
    y, x, z, c = y % 4, x % 4, z % 4, c % 2
    return ((((y * 2 + x // 2) * 4 + z) * 2) + x % 2) * 2 + c


def pairs(move):
    out = []
    for y in range(4):
        for x in range(4):
            for z in range(4):
                for c in range(2):
                    out.append((place(y, x, z, c), place(*move(y, x, z, c))))
    return tuple(out)


def to_core():
    return pairs(lambda y, x, z, c: (y, x, z, 1 - c))


def to_x(bits):
    return pairs(lambda y, x, z, c: (y, x ^ bits, z, c))


def to_x_by_core():
    return pairs(lambda y, x, z, c: (y, x ^ (1 if c == 0 else 3), z, c))


def to_first(bits):
    return pairs(lambda y, x, z, c: (y ^ bits, x, z, c) if c == 0 else (y, x, z ^ bits, c))


def to_second(bits):
    return pairs(lambda y, x, z, c: (y, x, z ^ bits, c) if c == 0 else (y ^ bits, x, z, c))


def send(values, where):
    return lax.ppermute(values, ("dp", "mp"), where)


def row_of(count, begin=0):
    return lax.broadcasted_iota(jnp.int32, (count, ROWS), 0) + begin


def turn(values, shift):
    return pltpu.roll(values, shift % values.shape[0], 0)


def widen_look(v, label):
    zero = jnp.float32(0)
    e = [label == g for g in range(4)]
    near = turn(v[:56], 2)
    far = turn(v[:128], 2)
    top = row_of(56) < 2
    tip = row_of(8) < 2
    mid = jnp.where(
        top, jnp.where(e[0], v[40:96], zero), jnp.where(e[1], near, zero)
    )
    joint = jnp.where(
        tip, jnp.where(e[1], near[:8], zero), jnp.where(e[2], far[:8], zero)
    )
    return jnp.concatenate(
        [
            jnp.where(e[0], v[:40], zero),
            mid,
            joint,
            jnp.where(e[2], far[8:], zero),
            jnp.where(e[3], v, zero),
        ],
        axis=0,
    )


def pick_look(u, label):
    zero = jnp.float32(0)
    e = [label == g for g in range(4)]
    last = jnp.where(e[3], u[224:560], zero)
    near = turn(u[40:104], -2)
    far = turn(u[96:224], -2)
    row = row_of(56)
    begin = jnp.where(
        e[2],
        far[:56],
        jnp.where(e[1], near[:56], jnp.where(e[0] & (row < 42), u[:56], last[:56])),
    )
    middle = jnp.where(e[2] & (row_of(72, 56) < 126), far[56:], last[56:128])
    return jnp.concatenate([begin, middle, last[128:]], axis=0)


def widen_reach(a, label):
    zero = jnp.float32(0)
    e = [label == g for g in range(4)]
    one = turn(a[:16], 6)
    two = turn(a[:24], 6)
    row = row_of(8)
    return jnp.concatenate(
        [
            jnp.where(row < 6, jnp.where(e[0], a[:8], zero), jnp.where(e[1], one[:8], zero)),
            jnp.where(row < 6, jnp.where(e[1], one[8:], zero), jnp.where(e[2], two[:8], zero)),
            jnp.where(e[2], two[8:], zero),
            jnp.where(e[3], a, zero),
        ],
        axis=0,
    )


def pick_reach(u, label):
    zero = jnp.float32(0)
    e = [label == g for g in range(4)]
    last = jnp.where(e[3], u[32:], zero)
    one = turn(u[:16], -6)
    two = turn(u[8:32], -6)
    row = row_of(8)
    return jnp.concatenate(
        [
            jnp.where(
                e[2],
                two[:8],
                jnp.where(e[1], one[:8], jnp.where(e[0] & (row < 6), u[:8], last[:8])),
            ),
            jnp.where(e[2] & (row_of(16, 8) < 18), two[8:], last[8:24]),
            last[24:],
        ],
        axis=0,
    )


def look_mask(label):
    reach = jnp.where(label == 0, 42, jnp.where(label == 1, 56, jnp.where(label == 2, 126, 336)))
    return row_of(336) < reach


def by_columns(slots, begin, count):
    return jnp.concatenate([slot[begin : begin + count, :] for slot in slots], axis=1)


def by_rows(slots, begin, count):
    return jnp.concatenate(
        [
            jnp.concatenate(
                [slot[begin + 128 * i : begin + 128 * (i + 1), :] for i in range(count)], axis=1
            )
            for slot in slots
        ],
        axis=0,
    )


def dot(a, b):
    return jnp.dot(a, b, preferred_element_type=F32)


def dot_t(a, b):
    return lax.dot_general(a, b, (((1,), (1,)), ((), ())), preferred_element_type=F32)


def t_dot(a, b):
    return lax.dot_general(a, b, (((0,), (0,)), ((), ())), preferred_element_type=F32)


def silu_both(pre):
    s = 0.5 * jnp.tanh(0.5 * pre) + 0.5
    act = pre * s
    return act.astype(BF), (s + act * (1.0 - s)).astype(BF)


TABLES = {
    "entry": (ENTRY, 560),
    "second": (SECOND, 512),
    "third": (THIRD, 512),
    "fourth": (FOURTH, 512),
    "back": (BACK, 512),
    "fore": (FORE, 512),
    "basis": (BASIS, 640),
}


class Weights:
    def __init__(self, slots):
        self.slots = slots

    def get(self, name):
        begin, count = TABLES[name]
        if name in ("second", "fourth"):
            return by_rows(self.slots, begin, 4)
        return by_columns(self.slots, begin, count)


def run_forward(state, label, weights, e_ref, act_ref, slope_ref, theta_ref):
    e_ref[...] = widen_look(state, label).astype(BF)
    act, slope = silu_both(t_dot(weights.get("entry"), e_ref[...]))
    act_ref[0], slope_ref[0] = act, slope
    for i, name in enumerate(("second", "third", "fourth")):
        act, slope = silu_both(t_dot(weights.get(name), act_ref[i]))
        act_ref[i + 1], slope_ref[i + 1] = act, slope
    theta_ref[0] = t_dot(weights.get("back"), act_ref[3]).astype(BF)
    theta_ref[1] = t_dot(weights.get("fore"), act_ref[3]).astype(BF)
    basis = weights.get("basis")
    return dot(basis[:560], theta_ref[0]), dot(basis[560:], theta_ref[1])


class Grads:
    def __init__(self, outs, base=0):
        self.outs, self.base = outs, base

    def put(self, name, grad):
        begin, count = TABLES[name]
        at = begin - self.base
        for slot in range(4):
            out = self.outs[slot % 2]
            out = out[slot // 2] if isinstance(out, tuple) else out.at[slot // 2]
            if name in ("second", "fourth"):
                for i in range(4):
                    out[at + 128 * i : at + 128 * (i + 1), :] = grad[
                        128 * slot : 128 * (slot + 1), 128 * i : 128 * (i + 1)
                    ].astype(BF)
            else:
                out[at : at + count, :] = grad[:, 128 * slot : 128 * (slot + 1)].astype(BF)
        if name == "basis":
            for out in self.outs:
                out[:, USED - self.base : PACK - self.base, :] = jnp.zeros((2, PACK - USED, 128), BF)


def backward_heads(g, fore_wide, label, weights, act_ref, slope_ref, theta_ref, grads):
    d_back = -widen_look(g, label).astype(BF)
    d_fore = fore_wide.astype(BF)
    basis = weights.get("basis")
    d_theta_b = t_dot(basis[:560], d_back).astype(BF)
    d_theta_f = t_dot(basis[560:], d_fore).astype(BF)
    grads.put(
        "basis",
        jnp.concatenate([dot_t(d_back, theta_ref[0]), dot_t(d_fore, theta_ref[1])], axis=0),
    )
    d_act = dot(weights.get("back"), d_theta_b) + dot(weights.get("fore"), d_theta_f)
    grads.put("back", dot_t(act_ref[3], d_theta_b))
    grads.put("fore", dot_t(act_ref[3], d_theta_f))
    d_pre = (d_act * slope_ref[3].astype(F32)).astype(BF)
    grads.put("fourth", dot_t(act_ref[2], d_pre))
    return d_pre


def backward_layers(g, d_pre, label, weights, e_ref, act_ref, slope_ref, grads):
    d_act = dot(weights.get("fourth"), d_pre)
    d_pre = (d_act * slope_ref[2].astype(F32)).astype(BF)
    grads.put("third", dot_t(act_ref[1], d_pre))
    d_act = dot(weights.get("third"), d_pre)
    d_pre = (d_act * slope_ref[1].astype(F32)).astype(BF)
    grads.put("second", dot_t(act_ref[0], d_pre))
    d_act = dot(weights.get("second"), d_pre)
    d_pre = (d_act * slope_ref[0].astype(F32)).astype(BF)
    grads.put("entry", dot_t(e_ref[...], d_pre))
    return g + pick_look(dot(weights.get("entry"), d_pre), label)


def places():
    dp, core = lax.axis_index("dp"), lax.rem(lax.axis_index("mp"), 2)
    y, z = lax.div(dp, 8), lax.rem(dp, 4)
    return jnp.where(core == 0, y, z), jnp.where(core == 0, z, y)


def pack_kernel(k, *refs):
    ins, out, quarter = refs[:7], refs[7], refs[8:]
    entry, second, third, fourth, back, fore, basis = (ref.at[k] for ref in ins)
    out[ENTRY:SECOND, :] = entry[...]
    out[THIRD:FOURTH, :] = third[...]
    out[BACK:FORE, :] = back[...]
    out[FORE:BASIS, :] = fore[...]
    for i in range(4):
        out[SECOND + 128 * i : SECOND + 128 * (i + 1), :] = second[:, 128 * i : 128 * (i + 1)]
        out[FOURTH + 128 * i : FOURTH + 128 * (i + 1), :] = fourth[:, 128 * i : 128 * (i + 1)]
    for i in range(5):
        out[BASIS + 128 * i : BASIS + 128 * (i + 1), :] = basis[:, 128 * i : 128 * (i + 1)].T
    out[USED:PACK, :] = jnp.zeros((PACK - USED, 128), BF)
    if quarter:
        i1, _ = places()
        quarter[0][...] = out[pl.ds(pl.multiple_of(i1 * CHUNK, CHUNK), CHUNK), :]


def join_kernel(q0, q1, q2, q3, out):
    i1, _ = places()
    for bits, quarter in zip((0, *PEERS), (q0, q1, q2, q3)):
        begin = pl.multiple_of((i1 ^ bits) * CHUNK, CHUNK)
        out[pl.ds(begin, CHUNK), :] = quarter[...]


def first_kernel(label, lag, s0, s1, s2, s3, state_out, look_out, e, act, slope, theta):
    weights = Weights((s0, s1, s2, s3))
    labels = label[...]
    state = jnp.where(look_mask(labels), lag[...].astype(F32), 0.0)
    heads, fore = run_forward(state, labels, weights, e, act, slope, theta)
    state_out[...] = state - pick_look(heads, labels)
    look_out[...] = pick_reach(fore, labels)


def second_kernel(
    label, state_in, look_in, left, adjoint, s0, s1, s2, s3, rest, look, g_out, mine, theirs, e, act, slope, theta
):
    weights = Weights((s0, s1, s2, s3))
    labels = label[...]
    heads, fore = run_forward(state_in[...], labels, weights, e, act, slope, theta)
    rest[...] = state_in[...] - pick_look(heads, labels)
    look[...] = look_in[...] + pick_reach(fore, labels)
    grads = Grads((mine, theirs))
    g = left[...].astype(F32)
    fore_wide = widen_reach(adjoint[...].astype(F32), labels)
    d_pre = backward_heads(g, fore_wide, labels, weights, act, slope, theta, grads)
    g_out[...] = backward_layers(g, d_pre, labels, weights, e, act, slope, grads)


def third_kernel(label, g_in, adjoint, s0, s1, s2, s3, act, slope, theta, d_out, mine, theirs):
    grads = Grads((mine, theirs), FOURTH)
    labels = label[...]
    fore_wide = widen_reach(adjoint[...].astype(F32), labels)
    d_out[...] = backward_heads(
        g_in[...], fore_wide, labels, Weights((s0, s1, s2, s3)), act, slope, theta, grads
    )


def fourth_kernel(label, g_in, d_in, s0, s1, s2, s3, e, act, slope, steep, mine, near, far):
    grads = Grads((mine, (near, far)))
    labels = label[...]
    g = backward_layers(g_in[...], d_in[...], labels, Weights((s0, s1, s2, s3)), e, act, slope, grads)
    steep[...] = jnp.where(look_mask(labels), g, 0.0)


def cut_kernel(rows, *refs):
    refs = list(refs)
    mine = [refs.pop(0) for _ in rows]
    got = [(refs.pop(0), refs.pop(0)) if count < 0 else refs.pop(0) for count in rows]
    outs, whole = refs[:4], refs[4]
    i1, _ = places()
    at = 0
    for count, kept, came in zip(rows, mine, got):
        for half in range(2):
            part = came[half] if count < 0 else came.at[half]
            whole[half, at : at + abs(count), :] = (
                kept[half].astype(F32) + part[...].astype(F32)
            ).astype(BF)
        at += abs(count)
    for bits, out in zip((*PEERS, 0), outs):
        begin = pl.multiple_of((i1 ^ bits) * CHUNK, CHUNK)
        out[...] = whole[:, pl.ds(begin, CHUNK), :]


def piece_kernel(*refs):
    chunks, outs, whole = refs[:8], refs[8:12], refs[12]
    _, i2 = places()
    for k in range(2):
        own, a, b, c = (ref[...].astype(F32) for ref in chunks[4 * k : 4 * k + 4])
        whole[:, k] = ((own + a) + (b + c)).astype(BF)
    for bits, out in zip((*PEERS, 0), outs):
        begin = pl.multiple_of((i2 ^ bits) * PIECE, PIECE)
        out[...] = whole[:, :, pl.ds(begin, PIECE), :]


def unpack_kernel(here, s0, s1, s2, s3, *refs):
    outs, whole, bufs, sem = refs[:7], refs[7], refs[8:15], refs[15]
    i1, i2 = places()
    for a, stack in zip((0, *PEERS), (s0, s1, s2, s3)):
        for slot, b in enumerate((0, *PEERS)):
            at = pl.multiple_of((i1 ^ a) * CHUNK + (i2 ^ b) * PIECE, PIECE)
            whole[:, pl.ds(at, PIECE), :] = stack[slot]
    scale = 1.0 / math.sqrt(98304)
    copies = []
    for (name, (begin, count)), out, buf in zip(TABLES.items(), outs, bufs):
        for k in range(2):
            if buf.shape[2] == 128:
                buf[k] = whole[k, begin : begin + count, :].astype(F32) * scale
            else:
                for i in range(count // 128):
                    part = whole[k, begin + 128 * i : begin + 128 * (i + 1), :].astype(F32) * scale
                    buf[k, :, 128 * i : 128 * (i + 1)] = part.T if name == "basis" else part
        copies.append(pltpu.make_async_copy(buf, out, sem.at[len(copies)]))
        copies[-1].start()
    for copy in copies:
        copy.wait()


def shape(*dims, kind=F32):
    return jax.ShapeDtypeStruct(dims, kind)


def vmem(*dims, kind=BF):
    return pltpu.VMEM(dims, kind)


M1, M2, M3, M4, M5 = 12, 20, 12, 12, 8
DMA = pltpu.SemaphoreType.DMA
IN_VMEM = pl.BlockSpec(memory_space=pltpu.VMEM)
ANYWHERE = pl.BlockSpec(memory_space=pl.ANY)


def call(kernel, name, ins, outs, scratch, mib, us):
    return pl.pallas_call(
        kernel,
        out_shape=[o[0] for o in outs],
        in_specs=ins,
        out_specs=[o[1] for o in outs],
        scratch_shapes=scratch,
        compiler_params=pltpu.CompilerParams(vmem_limit_bytes=mib * 1024 * 1024),
        cost_estimate=pl.CostEstimate(
            flops=int(us * 8e8), bytes_accessed=int(us * 1e6), transcendentals=0
        ),
        name=name,
    )


ACTS = (4, 512, ROWS)
KEPT = [(560, ROWS), ACTS, ACTS, (2, 512, ROWS)]
TOP, LOW = PACK - FOURTH, FOURTH


def plus(*parts):
    return sum(part.astype(F32) for part in parts).astype(BF)


def shards(lag, label, entry, second, third, fourth, back, fore, basis, adjoint, left):
    label = label[None, :]
    lag, adjoint, left = lag.T, adjoint.T, left.T
    whole, part = shape(PACK, 128, kind=BF), shape(CHUNK, 128, kind=BF)
    tables = (entry, second, third, fourth, back, fore, basis)
    two, quarter = call(
        functools.partial(pack_kernel, 1), "pack_two", [IN_VMEM] * 7, [(whole, IN_VMEM), (part, IN_VMEM)], [], 60, 2
    )(*tables)
    quarter, *tables = lax.optimization_barrier((quarter, *tables))
    one = call(functools.partial(pack_kernel, 0), "pack_one", [IN_VMEM] * 7, [(whole, IN_VMEM)], [], 60, 2)(*tables)[0]
    quarter = send(quarter, to_x_by_core())
    quarters = [quarter]
    one, quarters[0] = lax.optimization_barrier((one, quarters[0]))
    across = send(one, to_x_by_core())
    quarters += [send(quarters[0], to_first(a)) for a in PEERS]
    across, *quarters = lax.optimization_barrier((across, *quarters))
    slots1 = (one, send(one, to_core()), across, send(across, to_core()))
    across = call(join_kernel, "join", [IN_VMEM] * 4, [(whole, IN_VMEM)], [], M5, 1)(*quarters)[0]
    slots2 = (two, send(two, to_core()), across, send(across, to_core()))
    state1, look1, e1, act1, slope1, theta1 = call(
        first_kernel,
        "forward_one",
        [IN_VMEM] * 6,
        [(shape(336, ROWS), IN_VMEM), (shape(48, ROWS), IN_VMEM)]
        + [(shape(*k, kind=BF), IN_VMEM) for k in KEPT],
        [],
        M1,
        6,
    )(label, lag, *slots1)
    rest, look, g1, mine2, theirs2 = call(
        second_kernel,
        "block_two",
        [IN_VMEM] * 9,
        [(shape(336, ROWS), IN_VMEM), (shape(48, ROWS), IN_VMEM), (shape(336, ROWS), IN_VMEM)]
        + [(shape(2, PACK, 128, kind=BF), IN_VMEM)] * 2,
        [vmem(*k) for k in KEPT],
        M2,
        14,
    )(label, state1, look1, left, adjoint, *slots2)
    got2 = send(theirs2, to_core())
    d_pre, mine1a, theirs1a = call(
        third_kernel,
        "backward_one_heads",
        [IN_VMEM] * 10,
        [(shape(512, ROWS, kind=BF), IN_VMEM)] + [(shape(2, TOP, 128, kind=BF), IN_VMEM)] * 2,
        [],
        M3,
        6,
    )(label, g1, adjoint, *slots1, act1, slope1, theta1)
    got1a = send(theirs1a, to_core())

    def cut(rows, mine, got, name):
        return call(
            functools.partial(cut_kernel, rows),
            name,
            [IN_VMEM] * (len(mine) + len(got)),
            [(shape(2, CHUNK, 128, kind=BF), IN_VMEM)] * 4,
            [vmem(2, PACK, 128)],
            M5,
            2,
        )(*mine, *got)

    *out2, own2 = cut((PACK,), [mine2], [got2], "cut_two")
    got2 = [send(part, to_first(a)) for part, a in zip(out2, PEERS)]
    d_pre, got1a, *out2 = lax.optimization_barrier((d_pre, got1a, *out2))
    steep, mine1b, *theirs1b = call(
        fourth_kernel,
        "backward_one_layers",
        [IN_VMEM] * 10,
        [(shape(336, ROWS), IN_VMEM), (shape(2, LOW, 128, kind=BF), IN_VMEM)]
        + [(shape(LOW, 128, kind=BF), IN_VMEM)] * 2,
        [],
        M4,
        6,
    )(label, g1, d_pre, *slots1, e1, act1, slope1)
    got1b = [send(part, to_core()) for part in theirs1b]
    mine1b, got2[2] = lax.optimization_barrier((mine1b, got2[2]))
    *out1, own1 = cut((-LOW, TOP), [mine1b, mine1a], [*got1b, got1a], "cut_one")
    got1 = [send(part, to_first(a)) for part, a in zip(out1, PEERS)]
    *out, own = call(
        piece_kernel,
        "pieces",
        [IN_VMEM] * 8,
        [(shape(2, 2, PIECE, 128, kind=BF), IN_VMEM)] * 4,
        [vmem(2, 2, CHUNK, 128)],
        M5,
        2,
    )(own1, *got1, own2, *got2)
    got = [send(part, to_second(b)) for part, b in zip(out, PEERS)]
    done = plus(own, *got)
    got = [send(done[1], to_x(1)), send(done[1], to_x(3)), send(done[0], to_x(2))]
    done = plus(done[0], *got)
    stack = jnp.stack([done] + [send(done, to_second(b)) for b in PEERS])
    stack, here = lax.optimization_barrier((stack, send(stack[:, 0, :8], to_core())))
    stacks = [stack] + [send(stack, to_first(a)) for a in PEERS]
    outs = (
        (2, 560, 128), (2, 128, 512), (2, 512, 128), (2, 128, 512), (2, 512, 128), (2, 512, 128), (2, 128, 640),
    )
    grads = call(
        unpack_kernel,
        "unpack",
        [ANYWHERE] + [IN_VMEM] * 4,
        [(shape(*dims), ANYWHERE) for dims in outs],
        [vmem(2, PACK, 128)] + [vmem(*dims, kind=F32) for dims in outs] + [DMA((7,))],
        16,
        3,
    )(here, *stacks)
    return (look.T, rest.T, steep.T, *grads)


def solution(mesh):
    windows = P(("dp", "mp"), None)
    columns, rows = P(None, None, "mp"), P(None, "mp", None)
    tables = (columns, rows, columns, rows, columns, columns, rows)
    return jax.shard_map(
        shards,
        mesh=mesh,
        in_specs=(windows, P(("dp", "mp")), *tables, windows, windows),
        out_specs=(windows, windows, windows, *tables),
        check_vma=False,
    )
```

```python
import functools
import math

import jax
import jax.numpy as jnp
from jax import lax
from jax.experimental import pallas as pl
from jax.experimental.pallas import tpu as pltpu
from jax.sharding import PartitionSpec as P

BF = jnp.bfloat16
F32 = jnp.float32
ROWS = 768
ENTRY, SECOND, THIRD, FOURTH, BACK, FORE, BASIS, USED = 0, 560, 1072, 1584, 2096, 2608, 3120, 3760
PACK = 3840
PEERS = (1, 3, 2)
CHUNK, PIECE = PACK // 4, PACK // 16


def place(y, x, z, c):
    y, x, z, c = y % 4, x % 4, z % 4, c % 2
    return ((((y * 2 + x // 2) * 4 + z) * 2) + x % 2) * 2 + c


def pairs(move):
    out = []
    for y in range(4):
        for x in range(4):
            for z in range(4):
                for c in range(2):
                    out.append((place(y, x, z, c), place(*move(y, x, z, c))))
    return tuple(out)


def to_core():
    return pairs(lambda y, x, z, c: (y, x, z, 1 - c))


def to_x(bits):
    return pairs(lambda y, x, z, c: (y, x ^ bits, z, c))


def to_x_by_core():
    return pairs(lambda y, x, z, c: (y, x ^ (1 if c == 0 else 3), z, c))


def to_first(bits):
    return pairs(lambda y, x, z, c: (y ^ bits, x, z, c) if c == 0 else (y, x, z ^ bits, c))


def to_second(bits):
    return pairs(lambda y, x, z, c: (y, x, z ^ bits, c) if c == 0 else (y ^ bits, x, z, c))


def send(values, where):
    return lax.ppermute(values, ("dp", "mp"), where)


def row_of(count, begin=0):
    return lax.broadcasted_iota(jnp.int32, (count, ROWS), 0) + begin


def turn(values, shift):
    return pltpu.roll(values, shift % values.shape[0], 0)


def widen_look(v, label):
    zero = jnp.float32(0)
    e = [label == g for g in range(4)]
    near = turn(v[:56], 2)
    far = turn(v[:128], 2)
    top = row_of(56) < 2
    tip = row_of(8) < 2
    mid = jnp.where(
        top, jnp.where(e[0], v[40:96], zero), jnp.where(e[1], near, zero)
    )
    joint = jnp.where(
        tip, jnp.where(e[1], near[:8], zero), jnp.where(e[2], far[:8], zero)
    )
    return jnp.concatenate(
        [
            jnp.where(e[0], v[:40], zero),
            mid,
            joint,
            jnp.where(e[2], far[8:], zero),
            jnp.where(e[3], v, zero),
        ],
        axis=0,
    )


def pick_look(u, label):
    zero = jnp.float32(0)
    e = [label == g for g in range(4)]
    last = jnp.where(e[3], u[224:560], zero)
    near = turn(u[40:104], -2)
    far = turn(u[96:224], -2)
    row = row_of(56)
    begin = jnp.where(
        e[2],
        far[:56],
        jnp.where(e[1], near[:56], jnp.where(e[0] & (row < 42), u[:56], last[:56])),
    )
    middle = jnp.where(e[2] & (row_of(72, 56) < 126), far[56:], last[56:128])
    return jnp.concatenate([begin, middle, last[128:]], axis=0)


def widen_reach(a, label):
    zero = jnp.float32(0)
    e = [label == g for g in range(4)]
    one = turn(a[:16], 6)
    two = turn(a[:24], 6)
    row = row_of(8)
    return jnp.concatenate(
        [
            jnp.where(row < 6, jnp.where(e[0], a[:8], zero), jnp.where(e[1], one[:8], zero)),
            jnp.where(row < 6, jnp.where(e[1], one[8:], zero), jnp.where(e[2], two[:8], zero)),
            jnp.where(e[2], two[8:], zero),
            jnp.where(e[3], a, zero),
        ],
        axis=0,
    )


def pick_reach(u, label):
    zero = jnp.float32(0)
    e = [label == g for g in range(4)]
    last = jnp.where(e[3], u[32:], zero)
    one = turn(u[:16], -6)
    two = turn(u[8:32], -6)
    row = row_of(8)
    return jnp.concatenate(
        [
            jnp.where(
                e[2],
                two[:8],
                jnp.where(e[1], one[:8], jnp.where(e[0] & (row < 6), u[:8], last[:8])),
            ),
            jnp.where(e[2] & (row_of(16, 8) < 18), two[8:], last[8:24]),
            last[24:],
        ],
        axis=0,
    )


def look_mask(label):
    reach = jnp.where(label == 0, 42, jnp.where(label == 1, 56, jnp.where(label == 2, 126, 336)))
    return row_of(336) < reach


def by_columns(slots, begin, count):
    return jnp.concatenate([slot[begin : begin + count, :] for slot in slots], axis=1)


def by_rows(slots, begin, count):
    return jnp.concatenate(
        [
            jnp.concatenate(
                [slot[begin + 128 * i : begin + 128 * (i + 1), :] for i in range(count)], axis=1
            )
            for slot in slots
        ],
        axis=0,
    )


def dot(a, b):
    return jnp.dot(a, b, preferred_element_type=F32)


def dot_t(a, b):
    return lax.dot_general(a, b, (((1,), (1,)), ((), ())), preferred_element_type=F32)


def t_dot(a, b):
    return lax.dot_general(a, b, (((0,), (0,)), ((), ())), preferred_element_type=F32)


def silu_both(pre):
    s = 0.5 * jnp.tanh(0.5 * pre) + 0.5
    act = pre * s
    return act.astype(BF), (s + act * (1.0 - s)).astype(BF)


TABLES = {
    "entry": (ENTRY, 560),
    "second": (SECOND, 512),
    "third": (THIRD, 512),
    "fourth": (FOURTH, 512),
    "back": (BACK, 512),
    "fore": (FORE, 512),
    "basis": (BASIS, 640),
}


class Weights:
    def __init__(self, slots):
        self.slots = slots

    def get(self, name):
        begin, count = TABLES[name]
        if name in ("second", "fourth"):
            return by_rows(self.slots, begin, 4)
        return by_columns(self.slots, begin, count)


def run_forward(state, label, weights, e_ref, act_ref, slope_ref, theta_ref):
    e_ref[...] = widen_look(state, label).astype(BF)
    act, slope = silu_both(t_dot(weights.get("entry"), e_ref[...]))
    act_ref[0], slope_ref[0] = act, slope
    for i, name in enumerate(("second", "third", "fourth")):
        act, slope = silu_both(t_dot(weights.get(name), act_ref[i]))
        act_ref[i + 1], slope_ref[i + 1] = act, slope
    theta_ref[0] = t_dot(weights.get("back"), act_ref[3]).astype(BF)
    theta_ref[1] = t_dot(weights.get("fore"), act_ref[3]).astype(BF)
    basis = weights.get("basis")
    return dot(basis[:560], theta_ref[0]), dot(basis[560:], theta_ref[1])


class Grads:
    def __init__(self, outs, base=0):
        self.outs, self.base = outs, base

    def put(self, name, grad):
        begin, count = TABLES[name]
        at = begin - self.base
        for slot in range(4):
            out = self.outs[slot % 2]
            out = out[slot // 2] if isinstance(out, tuple) else out.at[slot // 2]
            if name in ("second", "fourth"):
                for i in range(4):
                    out[at + 128 * i : at + 128 * (i + 1), :] = grad[
                        128 * slot : 128 * (slot + 1), 128 * i : 128 * (i + 1)
                    ].astype(BF)
            else:
                out[at : at + count, :] = grad[:, 128 * slot : 128 * (slot + 1)].astype(BF)
        if name == "basis":
            for out in self.outs:
                out[:, USED - self.base : PACK - self.base, :] = jnp.zeros((2, PACK - USED, 128), BF)


def backward_heads(g, fore_wide, label, weights, act_ref, slope_ref, theta_ref, grads):
    d_back = -widen_look(g, label).astype(BF)
    d_fore = fore_wide.astype(BF)
    basis = weights.get("basis")
    d_theta_b = t_dot(basis[:560], d_back).astype(BF)
    d_theta_f = t_dot(basis[560:], d_fore).astype(BF)
    grads.put(
        "basis",
        jnp.concatenate([dot_t(d_back, theta_ref[0]), dot_t(d_fore, theta_ref[1])], axis=0),
    )
    d_act = dot(weights.get("back"), d_theta_b) + dot(weights.get("fore"), d_theta_f)
    grads.put("back", dot_t(act_ref[3], d_theta_b))
    grads.put("fore", dot_t(act_ref[3], d_theta_f))
    d_pre = (d_act * slope_ref[3].astype(F32)).astype(BF)
    grads.put("fourth", dot_t(act_ref[2], d_pre))
    return d_pre


def backward_layers(g, d_pre, label, weights, e_ref, act_ref, slope_ref, grads):
    d_act = dot(weights.get("fourth"), d_pre)
    d_pre = (d_act * slope_ref[2].astype(F32)).astype(BF)
    grads.put("third", dot_t(act_ref[1], d_pre))
    d_act = dot(weights.get("third"), d_pre)
    d_pre = (d_act * slope_ref[1].astype(F32)).astype(BF)
    grads.put("second", dot_t(act_ref[0], d_pre))
    d_act = dot(weights.get("second"), d_pre)
    d_pre = (d_act * slope_ref[0].astype(F32)).astype(BF)
    grads.put("entry", dot_t(e_ref[...], d_pre))
    return g + pick_look(dot(weights.get("entry"), d_pre), label)


def places():
    dp, core = lax.axis_index("dp"), lax.rem(lax.axis_index("mp"), 2)
    y, z = lax.div(dp, 8), lax.rem(dp, 4)
    return jnp.where(core == 0, y, z), jnp.where(core == 0, z, y)


def pack_kernel(k, *refs):
    ins, out, quarter = refs[:7], refs[7], refs[8:]
    entry, second, third, fourth, back, fore, basis = (ref.at[k] for ref in ins)
    out[ENTRY:SECOND, :] = entry[...]
    out[THIRD:FOURTH, :] = third[...]
    out[BACK:FORE, :] = back[...]
    out[FORE:BASIS, :] = fore[...]
    for i in range(4):
        out[SECOND + 128 * i : SECOND + 128 * (i + 1), :] = second[:, 128 * i : 128 * (i + 1)]
        out[FOURTH + 128 * i : FOURTH + 128 * (i + 1), :] = fourth[:, 128 * i : 128 * (i + 1)]
    for i in range(5):
        out[BASIS + 128 * i : BASIS + 128 * (i + 1), :] = basis[:, 128 * i : 128 * (i + 1)].T
    out[USED:PACK, :] = jnp.zeros((PACK - USED, 128), BF)
    if quarter:
        i1, _ = places()
        quarter[0][...] = out[pl.ds(pl.multiple_of(i1 * CHUNK, CHUNK), CHUNK), :]


def join_kernel(q0, q1, q2, q3, out):
    i1, _ = places()
    for bits, quarter in zip((0, *PEERS), (q0, q1, q2, q3)):
        begin = pl.multiple_of((i1 ^ bits) * CHUNK, CHUNK)
        out[pl.ds(begin, CHUNK), :] = quarter[...]


def first_kernel(label, lag, s0, s1, s2, s3, state_out, look_out, e, act, slope, theta):
    weights = Weights((s0, s1, s2, s3))
    labels = label[...]
    state = jnp.where(look_mask(labels), lag[...].astype(F32), 0.0)
    heads, fore = run_forward(state, labels, weights, e, act, slope, theta)
    state_out[...] = state - pick_look(heads, labels)
    look_out[...] = pick_reach(fore, labels)


def second_kernel(
    label, state_in, look_in, left, adjoint, s0, s1, s2, s3, rest, look, g_out, mine, theirs, e, act, slope, theta
):
    weights = Weights((s0, s1, s2, s3))
    labels = label[...]
    heads, fore = run_forward(state_in[...], labels, weights, e, act, slope, theta)
    rest[...] = state_in[...] - pick_look(heads, labels)
    look[...] = look_in[...] + pick_reach(fore, labels)
    grads = Grads((mine, theirs))
    g = left[...].astype(F32)
    fore_wide = widen_reach(adjoint[...].astype(F32), labels)
    d_pre = backward_heads(g, fore_wide, labels, weights, act, slope, theta, grads)
    g_out[...] = backward_layers(g, d_pre, labels, weights, e, act, slope, grads)


def third_kernel(label, g_in, adjoint, s0, s1, s2, s3, act, slope, theta, d_out, mine, theirs):
    grads = Grads((mine, theirs), FOURTH)
    labels = label[...]
    fore_wide = widen_reach(adjoint[...].astype(F32), labels)
    d_out[...] = backward_heads(
        g_in[...], fore_wide, labels, Weights((s0, s1, s2, s3)), act, slope, theta, grads
    )


def fourth_kernel(label, g_in, d_in, s0, s1, s2, s3, e, act, slope, steep, mine, near, far):
    grads = Grads((mine, (near, far)))
    labels = label[...]
    g = backward_layers(g_in[...], d_in[...], labels, Weights((s0, s1, s2, s3)), e, act, slope, grads)
    steep[...] = jnp.where(look_mask(labels), g, 0.0)


def cut_kernel(rows, *refs):
    refs = list(refs)
    mine = [refs.pop(0) for _ in rows]
    got = [(refs.pop(0), refs.pop(0)) if count < 0 else refs.pop(0) for count in rows]
    outs, whole = refs[:4], refs[4]
    i1, _ = places()
    at = 0
    for count, kept, came in zip(rows, mine, got):
        for half in range(2):
            part = came[half] if count < 0 else came.at[half]
            whole[half, at : at + abs(count), :] = (
                kept[half].astype(F32) + part[...].astype(F32)
            ).astype(BF)
        at += abs(count)
    for bits, out in zip((*PEERS, 0), outs):
        begin = pl.multiple_of((i1 ^ bits) * CHUNK, CHUNK)
        out[...] = whole[:, pl.ds(begin, CHUNK), :]


def piece_kernel(own, a, b, c, *refs):
    before, outs, whole = refs[:-5], refs[-5:-1], refs[-1]
    _, i2 = places()
    own, a, b, c = (ref[...].astype(F32) for ref in (own, a, b, c))
    whole[...] = ((own + a) + (b + c)).astype(BF)
    for n, (bits, out) in enumerate(zip((*PEERS, 0), outs)):
        begin = pl.multiple_of((i2 ^ bits) * PIECE, PIECE)
        if before:
            out[:, 0] = whole[:, pl.ds(begin, PIECE), :]
            out[:, 1] = before[n][...]
        else:
            out[...] = whole[:, pl.ds(begin, PIECE), :]


def unpack_kernel(k, *refs):
    stacks, outs, whole, bufs, sem = refs[:4], refs[-16:-9], refs[-9], refs[-8:-1], refs[-1]
    i1, i2 = places()
    for a, stack in zip((0, *PEERS), stacks):
        for slot, b in enumerate((0, *PEERS)):
            at = pl.multiple_of((i1 ^ a) * CHUNK + (i2 ^ b) * PIECE, PIECE)
            whole[pl.ds(at, PIECE), :] = stack[slot]
    scale = 1.0 / math.sqrt(98304)
    copies = []
    for (name, (begin, count)), out, buf in zip(TABLES.items(), outs, bufs):
        if buf.shape[1] == 128:
            buf[...] = whole[begin : begin + count, :].astype(F32) * scale
        else:
            for i in range(count // 128):
                part = whole[begin + 128 * i : begin + 128 * (i + 1), :].astype(F32) * scale
                buf[:, 128 * i : 128 * (i + 1)] = part.T if name == "basis" else part
        copies.append(pltpu.make_async_copy(buf, out.at[k], sem.at[len(copies)]))
        copies[-1].start()
    for copy in copies:
        copy.wait()


def shape(*dims, kind=F32):
    return jax.ShapeDtypeStruct(dims, kind)


def vmem(*dims, kind=BF):
    return pltpu.VMEM(dims, kind)


M1, M2, M3, M4, M5 = 12, 20, 12, 12, 8
DMA = pltpu.SemaphoreType.DMA
IN_VMEM = pl.BlockSpec(memory_space=pltpu.VMEM)
ANYWHERE = pl.BlockSpec(memory_space=pl.ANY)


def call(kernel, name, ins, outs, scratch, mib, us, aliases={}):
    return pl.pallas_call(
        kernel,
        out_shape=[o[0] for o in outs],
        in_specs=ins,
        out_specs=[o[1] for o in outs],
        scratch_shapes=scratch,
        compiler_params=pltpu.CompilerParams(vmem_limit_bytes=mib * 1024 * 1024),
        cost_estimate=pl.CostEstimate(
            flops=int(us * 8e8), bytes_accessed=int(us * 1e6), transcendentals=0
        ),
        name=name,
        input_output_aliases=aliases,
    )


ACTS = (4, 512, ROWS)
KEPT = [(560, ROWS), ACTS, ACTS, (2, 512, ROWS)]
TOP, LOW = PACK - FOURTH, FOURTH


def plus(*parts):
    return sum(part.astype(F32) for part in parts).astype(BF)


def shards(lag, label, entry, second, third, fourth, back, fore, basis, adjoint, left):
    label = label[None, :]
    lag, adjoint, left = lag.T, adjoint.T, left.T
    whole, part = shape(PACK, 128, kind=BF), shape(CHUNK, 128, kind=BF)
    tables = (entry, second, third, fourth, back, fore, basis)
    two, quarter = call(
        functools.partial(pack_kernel, 1), "pack_two", [IN_VMEM] * 7, [(whole, IN_VMEM), (part, IN_VMEM)], [], 60, 2
    )(*tables)
    quarter, *tables = lax.optimization_barrier((quarter, *tables))
    one = call(functools.partial(pack_kernel, 0), "pack_one", [IN_VMEM] * 7, [(whole, IN_VMEM)], [], 60, 2)(*tables)[0]
    quarter = send(quarter, to_x_by_core())
    quarters = [quarter]
    one, quarters[0] = lax.optimization_barrier((one, quarters[0]))
    across = send(one, to_x_by_core())
    quarters += [send(quarters[0], to_first(a)) for a in PEERS]
    across, *quarters = lax.optimization_barrier((across, *quarters))
    slots1 = (one, send(one, to_core()), across, send(across, to_core()))
    across = call(join_kernel, "join", [IN_VMEM] * 4, [(whole, IN_VMEM)], [], M5, 1)(*quarters)[0]
    slots2 = (two, send(two, to_core()), across, send(across, to_core()))
    state1, look1, e1, act1, slope1, theta1 = call(
        first_kernel,
        "forward_one",
        [IN_VMEM] * 6,
        [(shape(336, ROWS), IN_VMEM), (shape(48, ROWS), IN_VMEM)]
        + [(shape(*k, kind=BF), IN_VMEM) for k in KEPT],
        [],
        M1,
        6,
    )(label, lag, *slots1)
    rest, look, g1, mine2, theirs2 = call(
        second_kernel,
        "block_two",
        [IN_VMEM] * 9,
        [(shape(336, ROWS), IN_VMEM), (shape(48, ROWS), IN_VMEM), (shape(336, ROWS), IN_VMEM)]
        + [(shape(2, PACK, 128, kind=BF), IN_VMEM)] * 2,
        [vmem(*k) for k in KEPT],
        M2,
        14,
    )(label, state1, look1, left, adjoint, *slots2)
    got2 = send(theirs2, to_core())
    d_pre, mine1a, theirs1a = call(
        third_kernel,
        "backward_one_heads",
        [IN_VMEM] * 10,
        [(shape(512, ROWS, kind=BF), IN_VMEM)] + [(shape(2, TOP, 128, kind=BF), IN_VMEM)] * 2,
        [],
        M3,
        6,
    )(label, g1, adjoint, *slots1, act1, slope1, theta1)
    got1a = send(theirs1a, to_core())

    def cut(rows, mine, got, name):
        return call(
            functools.partial(cut_kernel, rows),
            name,
            [IN_VMEM] * (len(mine) + len(got)),
            [(shape(2, CHUNK, 128, kind=BF), IN_VMEM)] * 4,
            [vmem(2, PACK, 128)],
            M5,
            2,
        )(*mine, *got)

    *out2, own2 = cut((PACK,), [mine2], [got2], "cut_two")
    got2 = [send(part, to_first(a)) for part, a in zip(out2, PEERS)]
    d_pre, got1a, *out2 = lax.optimization_barrier((d_pre, got1a, *out2))
    steep, mine1b, *theirs1b = call(
        fourth_kernel,
        "backward_one_layers",
        [IN_VMEM] * 10,
        [(shape(336, ROWS), IN_VMEM), (shape(2, LOW, 128, kind=BF), IN_VMEM)]
        + [(shape(LOW, 128, kind=BF), IN_VMEM)] * 2,
        [],
        M4,
        6,
    )(label, g1, d_pre, *slots1, e1, act1, slope1)
    got1b = [send(part, to_core()) for part in theirs1b]
    mine1b, got2[2] = lax.optimization_barrier((mine1b, got2[2]))
    *out1, own1 = cut((-LOW, TOP), [mine1b, mine1a], [*got1b, got1a], "cut_one")
    got1 = [send(part, to_first(a)) for part, a in zip(out1, PEERS)]

    def pieces(own, got, before, dims):
        return call(
            piece_kernel,
            "pieces",
            [IN_VMEM] * (4 + len(before)),
            [(shape(2, *dims, PIECE, 128, kind=BF), IN_VMEM)] * 4,
            [vmem(2, CHUNK, 128)],
            M5,
            1,
        )(own, *got, *before)

    *out, own = pieces(own1, got1, pieces(own2, got2, (), ()), (2,))
    got = [send(part, to_second(b)) for part, b in zip(out, PEERS)]
    done = plus(own, *got)
    got = [send(done[1], to_x(1)), send(done[1], to_x(3)), send(done[0], to_x(2))]
    done = plus(done[0], *got)
    stack = jnp.stack([done] + [send(done, to_second(b)) for b in PEERS], axis=1)
    grads = ()
    for k in (1, 0):
        stacks = [stack[k]] + [send(stack[k], to_first(a)) for a in PEERS]
        outs = (
            (560, 128), (128, 512), (512, 128), (128, 512), (512, 128), (512, 128), (128, 640),
        )
        grads = call(
            functools.partial(unpack_kernel, k),
            "unpack",
            [IN_VMEM] * 4 + [ANYWHERE] * (len(grads)),
            [(shape(2, *dims), ANYWHERE) for dims in outs],
            [vmem(PACK, 128)] + [vmem(*dims, kind=F32) for dims in outs] + [DMA((7,))],
            16,
            2,
            {4 + n: n for n in range(len(grads))},
        )(*stacks, *grads)
    return (look.T, rest.T, steep.T, *grads)


def solution(mesh):
    windows = P(("dp", "mp"), None)
    columns, rows = P(None, None, "mp"), P(None, "mp", None)
    tables = (columns, rows, columns, rows, columns, columns, rows)
    return jax.shard_map(
        shards,
        mesh=mesh,
        in_specs=(windows, P(("dp", "mp")), *tables, windows, windows),
        out_specs=(windows, windows, windows, *tables),
        check_vma=False,
    )
```

```python
import functools
import math

import jax
import jax.numpy as jnp
from jax import lax
from jax.experimental import pallas as pl
from jax.experimental.pallas import tpu as pltpu
from jax.sharding import PartitionSpec as P

BF = jnp.bfloat16
F32 = jnp.float32
ROWS = 768
ENTRY, SECOND, THIRD, FOURTH, BACK, FORE, BASIS, USED = 0, 560, 1072, 1584, 2096, 2608, 3120, 3760
PACK = 3840
PEERS = (1, 3, 2)
FAR_FIRST = (2, 3, 1)
CHUNK, PIECE = PACK // 4, PACK // 16


def place(y, x, z, c):
    y, x, z, c = y % 4, x % 4, z % 4, c % 2
    return ((((y * 2 + x // 2) * 4 + z) * 2) + x % 2) * 2 + c


def pairs(move):
    out = []
    for y in range(4):
        for x in range(4):
            for z in range(4):
                for c in range(2):
                    out.append((place(y, x, z, c), place(*move(y, x, z, c))))
    return tuple(out)


def to_core():
    return pairs(lambda y, x, z, c: (y, x, z, 1 - c))


def to_x(bits):
    return pairs(lambda y, x, z, c: (y, x ^ bits, z, c))


def to_x_by_core():
    return pairs(lambda y, x, z, c: (y, x ^ (1 if c == 0 else 3), z, c))


def to_first(bits):
    return pairs(lambda y, x, z, c: (y ^ bits, x, z, c) if c == 0 else (y, x, z ^ bits, c))


def to_second(bits):
    return pairs(lambda y, x, z, c: (y, x, z ^ bits, c) if c == 0 else (y ^ bits, x, z, c))


def send(values, where):
    return lax.ppermute(values, ("dp", "mp"), where)


def row_of(count, begin=0):
    return lax.broadcasted_iota(jnp.int32, (count, ROWS), 0) + begin


def turn(values, shift):
    return pltpu.roll(values, shift % values.shape[0], 0)


def widen_look(v, label):
    zero = jnp.float32(0)
    e = [label == g for g in range(4)]
    near = turn(v[:56], 2)
    far = turn(v[:128], 2)
    top = row_of(56) < 2
    tip = row_of(8) < 2
    mid = jnp.where(
        top, jnp.where(e[0], v[40:96], zero), jnp.where(e[1], near, zero)
    )
    joint = jnp.where(
        tip, jnp.where(e[1], near[:8], zero), jnp.where(e[2], far[:8], zero)
    )
    return jnp.concatenate(
        [
            jnp.where(e[0], v[:40], zero),
            mid,
            joint,
            jnp.where(e[2], far[8:], zero),
            jnp.where(e[3], v, zero),
        ],
        axis=0,
    )


def pick_look(u, label):
    zero = jnp.float32(0)
    e = [label == g for g in range(4)]
    last = jnp.where(e[3], u[224:560], zero)
    near = turn(u[40:104], -2)
    far = turn(u[96:224], -2)
    row = row_of(56)
    begin = jnp.where(
        e[2],
        far[:56],
        jnp.where(e[1], near[:56], jnp.where(e[0] & (row < 42), u[:56], last[:56])),
    )
    middle = jnp.where(e[2] & (row_of(72, 56) < 126), far[56:], last[56:128])
    return jnp.concatenate([begin, middle, last[128:]], axis=0)


def widen_reach(a, label):
    zero = jnp.float32(0)
    e = [label == g for g in range(4)]
    one = turn(a[:16], 6)
    two = turn(a[:24], 6)
    row = row_of(8)
    return jnp.concatenate(
        [
            jnp.where(row < 6, jnp.where(e[0], a[:8], zero), jnp.where(e[1], one[:8], zero)),
            jnp.where(row < 6, jnp.where(e[1], one[8:], zero), jnp.where(e[2], two[:8], zero)),
            jnp.where(e[2], two[8:], zero),
            jnp.where(e[3], a, zero),
        ],
        axis=0,
    )


def pick_reach(u, label):
    zero = jnp.float32(0)
    e = [label == g for g in range(4)]
    last = jnp.where(e[3], u[32:], zero)
    one = turn(u[:16], -6)
    two = turn(u[8:32], -6)
    row = row_of(8)
    return jnp.concatenate(
        [
            jnp.where(
                e[2],
                two[:8],
                jnp.where(e[1], one[:8], jnp.where(e[0] & (row < 6), u[:8], last[:8])),
            ),
            jnp.where(e[2] & (row_of(16, 8) < 18), two[8:], last[8:24]),
            last[24:],
        ],
        axis=0,
    )


def look_mask(label):
    reach = jnp.where(label == 0, 42, jnp.where(label == 1, 56, jnp.where(label == 2, 126, 336)))
    return row_of(336) < reach


def by_columns(slots, begin, count):
    return jnp.concatenate([slot[begin : begin + count, :] for slot in slots], axis=1)


def by_rows(slots, begin, count):
    return jnp.concatenate(
        [
            jnp.concatenate(
                [slot[begin + 128 * i : begin + 128 * (i + 1), :] for i in range(count)], axis=1
            )
            for slot in slots
        ],
        axis=0,
    )


def dot(a, b):
    return jnp.dot(a, b, preferred_element_type=F32)


def dot_t(a, b):
    return lax.dot_general(a, b, (((1,), (1,)), ((), ())), preferred_element_type=F32)


def t_dot(a, b):
    return lax.dot_general(a, b, (((0,), (0,)), ((), ())), preferred_element_type=F32)


def silu_both(pre):
    s = 0.5 * jnp.tanh(0.5 * pre) + 0.5
    act = pre * s
    return act.astype(BF), (s + act * (1.0 - s)).astype(BF)


TABLES = {
    "entry": (ENTRY, 560),
    "second": (SECOND, 512),
    "third": (THIRD, 512),
    "fourth": (FOURTH, 512),
    "back": (BACK, 512),
    "fore": (FORE, 512),
    "basis": (BASIS, 640),
}


class Weights:
    def __init__(self, slots):
        self.slots = slots

    def get(self, name):
        begin, count = TABLES[name]
        if name in ("second", "fourth"):
            return by_rows(self.slots, begin, 4)
        return by_columns(self.slots, begin, count)


def run_forward(state, label, weights, e_ref, act_ref, slope_ref, theta_ref):
    e_ref[...] = widen_look(state, label).astype(BF)
    act, slope = silu_both(t_dot(weights.get("entry"), e_ref[...]))
    act_ref[0], slope_ref[0] = act, slope
    for i, name in enumerate(("second", "third", "fourth")):
        act, slope = silu_both(t_dot(weights.get(name), act_ref[i]))
        act_ref[i + 1], slope_ref[i + 1] = act, slope
    theta_ref[0] = t_dot(weights.get("back"), act_ref[3]).astype(BF)
    theta_ref[1] = t_dot(weights.get("fore"), act_ref[3]).astype(BF)
    basis = weights.get("basis")
    return dot(basis[:560], theta_ref[0]), dot(basis[560:], theta_ref[1])


class Grads:
    def __init__(self, outs, base=0):
        self.outs, self.base = outs, base

    def put(self, name, grad):
        begin, count = TABLES[name]
        at = begin - self.base
        for slot in range(4):
            out = self.outs[slot % 2]
            out = out[slot // 2] if isinstance(out, tuple) else out.at[slot // 2]
            if name in ("second", "fourth"):
                for i in range(4):
                    out[at + 128 * i : at + 128 * (i + 1), :] = grad[
                        128 * slot : 128 * (slot + 1), 128 * i : 128 * (i + 1)
                    ].astype(BF)
            else:
                out[at : at + count, :] = grad[:, 128 * slot : 128 * (slot + 1)].astype(BF)
        if name == "basis":
            for out in self.outs:
                out[:, USED - self.base : PACK - self.base, :] = jnp.zeros((2, PACK - USED, 128), BF)


def backward_heads(g, fore_wide, label, weights, act_ref, slope_ref, theta_ref, grads):
    d_back = -widen_look(g, label).astype(BF)
    d_fore = fore_wide.astype(BF)
    basis = weights.get("basis")
    d_theta_b = t_dot(basis[:560], d_back).astype(BF)
    d_theta_f = t_dot(basis[560:], d_fore).astype(BF)
    grads.put(
        "basis",
        jnp.concatenate([dot_t(d_back, theta_ref[0]), dot_t(d_fore, theta_ref[1])], axis=0),
    )
    d_act = dot(weights.get("back"), d_theta_b) + dot(weights.get("fore"), d_theta_f)
    grads.put("back", dot_t(act_ref[3], d_theta_b))
    grads.put("fore", dot_t(act_ref[3], d_theta_f))
    d_pre = (d_act * slope_ref[3].astype(F32)).astype(BF)
    grads.put("fourth", dot_t(act_ref[2], d_pre))
    return d_pre


def backward_layers(g, d_pre, label, weights, e_ref, act_ref, slope_ref, grads):
    d_act = dot(weights.get("fourth"), d_pre)
    d_pre = (d_act * slope_ref[2].astype(F32)).astype(BF)
    grads.put("third", dot_t(act_ref[1], d_pre))
    d_act = dot(weights.get("third"), d_pre)
    d_pre = (d_act * slope_ref[1].astype(F32)).astype(BF)
    grads.put("second", dot_t(act_ref[0], d_pre))
    d_act = dot(weights.get("second"), d_pre)
    d_pre = (d_act * slope_ref[0].astype(F32)).astype(BF)
    grads.put("entry", dot_t(e_ref[...], d_pre))
    return g + pick_look(dot(weights.get("entry"), d_pre), label)


def places():
    dp, core = lax.axis_index("dp"), lax.rem(lax.axis_index("mp"), 2)
    y, z = lax.div(dp, 8), lax.rem(dp, 4)
    return jnp.where(core == 0, y, z), jnp.where(core == 0, z, y)


def pack_kernel(*refs):
    tables, both, one = refs[:7], refs[7], refs[8]
    for k in range(2):
        for (name, (begin, count)), table in zip(TABLES.items(), tables):
            if table.shape[2] == 128:
                both[k, begin : begin + count, :] = table[k]
                continue
            for i in range(count // 128):
                block = table[k, :, 128 * i : 128 * (i + 1)]
                both[k, begin + 128 * i : begin + 128 * (i + 1), :] = block.T if name == "basis" else block
        both[k, USED:PACK, :] = jnp.zeros((PACK - USED, 128), BF)
    one[...] = both[0]


def quarter_kernel(*refs):
    tables, out, turned, sem = refs[:7], refs[7], refs[8], refs[9]
    i1, _ = places()
    for n in range(4):

        @pl.when(i1 == n)
        def _():
            copies = []

            def copy(source, target):
                copies.append(pltpu.make_async_copy(source, target, sem.at[len(copies)]))
                copies[-1].start()

            for (name, (begin, count)), table in zip(TABLES.items(), tables):
                step = 128 if table.shape[2] > 128 else count
                for at in range(begin, begin + count, step):
                    low, high = max(at, n * CHUNK), min(at + step, (n + 1) * CHUNK)
                    if low >= high or name == "basis":
                        continue
                    columns = at - begin if step == 128 else 0
                    copy(
                        table.at[1, pl.ds(low - at, high - low), pl.ds(columns, 128)],
                        out.at[pl.ds(low - n * CHUNK, high - low)],
                    )
            if n == 3:
                copy(tables[6].at[1], turned)
                out[USED - n * CHUNK :, :] = jnp.zeros((PACK - USED, 128), BF)
            for c in copies:
                c.wait()
            if n == 3:
                for i in range(5):
                    at = BASIS - n * CHUNK + 128 * i
                    out[at : at + 128, :] = turned[:, 128 * i : 128 * (i + 1)].T


def join_kernel(q0, q1, q2, q3, out):
    i1, _ = places()
    for bits, quarter in zip((0, *PEERS), (q0, q1, q2, q3)):
        begin = pl.multiple_of((i1 ^ bits) * CHUNK, CHUNK)
        out[pl.ds(begin, CHUNK), :] = quarter[...]


def first_kernel(label, lag, s0, s1, s2, s3, state_out, look_out, e, act, slope, theta):
    weights = Weights((s0.at[0], s1.at[0], s2, s3))
    labels = label[...]
    state = jnp.where(look_mask(labels), lag[...].astype(F32), 0.0)
    heads, fore = run_forward(state, labels, weights, e, act, slope, theta)
    state_out[...] = state - pick_look(heads, labels)
    look_out[...] = pick_reach(fore, labels)


def second_kernel(
    label, state_in, look_in, left, adjoint, s0, s1, s2, s3, rest, look, g_out, mine, theirs, e, act, slope, theta
):
    weights = Weights((s0.at[1], s1.at[1], s2, s3))
    labels = label[...]
    heads, fore = run_forward(state_in[...], labels, weights, e, act, slope, theta)
    rest[...] = state_in[...] - pick_look(heads, labels)
    look[...] = look_in[...] + pick_reach(fore, labels)
    grads = Grads((mine, theirs))
    g = left[...].astype(F32)
    fore_wide = widen_reach(adjoint[...].astype(F32), labels)
    d_pre = backward_heads(g, fore_wide, labels, weights, act, slope, theta, grads)
    g_out[...] = backward_layers(g, d_pre, labels, weights, e, act, slope, grads)


def third_kernel(label, g_in, adjoint, s0, s1, s2, s3, act, slope, theta, d_out, mine, theirs):
    grads = Grads((mine, theirs), FOURTH)
    labels = label[...]
    fore_wide = widen_reach(adjoint[...].astype(F32), labels)
    d_out[...] = backward_heads(
        g_in[...], fore_wide, labels, Weights((s0.at[0], s1.at[0], s2, s3)), act, slope, theta, grads
    )


def fourth_kernel(label, g_in, d_in, s0, s1, s2, s3, e, act, slope, steep, mine, near, far):
    grads = Grads((mine, (near, far)))
    labels = label[...]
    g = backward_layers(g_in[...], d_in[...], labels, Weights((s0.at[0], s1.at[0], s2, s3)), e, act, slope, grads)
    steep[...] = jnp.where(look_mask(labels), g, 0.0)


def cut_kernel(rows, *refs):
    refs = list(refs)
    mine = [refs.pop(0) for _ in rows]
    got = [(refs.pop(0), refs.pop(0)) if count < 0 else refs.pop(0) for count in rows]
    outs, whole = refs[:4], refs[4]
    i1, _ = places()
    at = 0
    for count, kept, came in zip(rows, mine, got):
        for half in range(2):
            part = came[half] if count < 0 else came.at[half]
            whole[half, at : at + abs(count), :] = (
                kept[half].astype(F32) + part[...].astype(F32)
            ).astype(BF)
        at += abs(count)
    for bits, out in zip((*PEERS, 0), outs):
        begin = pl.multiple_of((i1 ^ bits) * CHUNK, CHUNK)
        out[...] = whole[:, pl.ds(begin, CHUNK), :]


def total(refs):
    a, b, c, d = (ref[...].astype(F32) for ref in refs)
    return ((a + b) + (c + d)).astype(BF)


def fold_kernel(own, a, b, c, near, far):
    near[...], far[...] = total((own, a, b, c))


def piece_kernel(own, a, b, c, near, came, *refs):
    outs, whole = refs[:4], refs[4]
    _, i2 = places()
    whole[0], whole[2] = total((own, a, b, c))
    whole[1] = (near[...].astype(F32) + came[...].astype(F32)).astype(BF)
    for bits, out in zip((*PEERS, 0), outs):
        begin = pl.multiple_of((i2 ^ bits) * PIECE, PIECE)
        out[...] = whole[:, pl.ds(begin, PIECE), :]


def sum_kernel(own, a, b, c, near, far):
    sums = total((own, a, b, c))
    near[...] = sums[:2]
    far[...] = sums[2]


def across_kernel(near, a, b, c, out):
    both = near[...].astype(F32) + a[...].astype(F32)
    out[0] = (both[0] + (b[...].astype(F32) + c[...].astype(F32))).astype(BF)
    out[1] = both[1].astype(BF)


def stack_kernel(*refs):
    for k in range(2):
        for n in range(4):
            refs[4 + k][n] = refs[n][k]


def unpack_kernel(k, *refs):
    stacks, outs, whole, bufs, sem = refs[:4], refs[-16:-9], refs[-9], refs[-8:-1], refs[-1]
    i1, i2 = places()
    for a, stack in zip((0, *FAR_FIRST), stacks):
        for slot, b in enumerate((0, *FAR_FIRST)):
            at = pl.multiple_of((i1 ^ a) * CHUNK + (i2 ^ b) * PIECE, PIECE)
            whole[pl.ds(at, PIECE), :] = stack[slot]
    scale = 1.0 / math.sqrt(98304)
    copies = []
    for (name, (begin, count)), out, buf in zip(TABLES.items(), outs, bufs):
        if buf.shape[1] == 128:
            buf[...] = whole[begin : begin + count, :].astype(F32) * scale
        else:
            for i in range(count // 128):
                part = whole[begin + 128 * i : begin + 128 * (i + 1), :].astype(F32) * scale
                buf[:, 128 * i : 128 * (i + 1)] = part.T if name == "basis" else part
        copies.append(pltpu.make_async_copy(buf, out.at[k], sem.at[len(copies)]))
        copies[-1].start()
    for copy in copies:
        copy.wait()


def shape(*dims, kind=F32):
    return jax.ShapeDtypeStruct(dims, kind)


def vmem(*dims, kind=BF):
    return pltpu.VMEM(dims, kind)


M1, M2, M3, M4, M5 = 12, 20, 12, 12, 8
DMA = pltpu.SemaphoreType.DMA
IN_VMEM = pl.BlockSpec(memory_space=pltpu.VMEM)
ANYWHERE = pl.BlockSpec(memory_space=pl.ANY)


def call(kernel, name, ins, outs, scratch, mib, us, aliases={}):
    return pl.pallas_call(
        kernel,
        out_shape=[o[0] for o in outs],
        in_specs=ins,
        out_specs=[o[1] for o in outs],
        scratch_shapes=scratch,
        compiler_params=pltpu.CompilerParams(vmem_limit_bytes=mib * 1024 * 1024),
        cost_estimate=pl.CostEstimate(
            flops=int(us * 8e8), bytes_accessed=int(us * 1e6), transcendentals=0
        ),
        name=name,
        input_output_aliases=aliases,
    )


ACTS = (4, 512, ROWS)
KEPT = [(560, ROWS), ACTS, ACTS, (2, 512, ROWS)]
TOP, LOW = PACK - FOURTH, FOURTH


def plus(*parts):
    return sum(part.astype(F32) for part in parts).astype(BF)


def shards(lag, label, entry, second, third, fourth, back, fore, basis, adjoint, left):
    label = label[None, :]
    lag, adjoint, left = lag.T, adjoint.T, left.T
    whole, part = shape(PACK, 128, kind=BF), shape(CHUNK, 128, kind=BF)
    tables = (entry, second, third, fourth, back, fore, basis)
    quarter = call(
        quarter_kernel,
        "pack_quarter",
        [ANYWHERE] * 7,
        [(part, IN_VMEM)],
        [vmem(128, 640), DMA((8,))],
        60,
        1,
    )(*tables)[0]
    quarter, *tables = lax.optimization_barrier((quarter, *tables))
    both, one = call(
        pack_kernel,
        "pack",
        [IN_VMEM] * 7,
        [(shape(2, PACK, 128, kind=BF), IN_VMEM), (whole, IN_VMEM)],
        [],
        60,
        3,
    )(*tables)
    quarter = send(quarter, to_x_by_core())
    one, quarter = lax.optimization_barrier((one, quarter))
    across = send(one, to_x_by_core())
    quarters = [quarter] + [send(quarter, to_first(a)) for a in PEERS]
    other = send(both, to_core())
    across, *quarters = lax.optimization_barrier((across, *quarters))
    slots1 = (both, other, across, send(across, to_core()))
    across = call(join_kernel, "join", [IN_VMEM] * 4, [(whole, IN_VMEM)], [], M5, 1)(*quarters)[0]
    slots2 = (both, other, across, send(across, to_core()))
    state1, look1, e1, act1, slope1, theta1 = call(
        first_kernel,
        "forward_one",
        [IN_VMEM] * 6,
        [(shape(336, ROWS), IN_VMEM), (shape(48, ROWS), IN_VMEM)]
        + [(shape(*k, kind=BF), IN_VMEM) for k in KEPT],
        [],
        M1,
        6,
    )(label, lag, *slots1)
    rest, look, g1, mine2, theirs2 = call(
        second_kernel,
        "block_two",
        [IN_VMEM] * 9,
        [(shape(336, ROWS), IN_VMEM), (shape(48, ROWS), IN_VMEM), (shape(336, ROWS), IN_VMEM)]
        + [(shape(2, PACK, 128, kind=BF), IN_VMEM)] * 2,
        [vmem(*k) for k in KEPT],
        M2,
        14,
    )(label, state1, look1, left, adjoint, *slots2)
    got2 = send(theirs2, to_core())
    d_pre, mine1a, theirs1a = call(
        third_kernel,
        "backward_one_heads",
        [IN_VMEM] * 10,
        [(shape(512, ROWS, kind=BF), IN_VMEM)] + [(shape(2, TOP, 128, kind=BF), IN_VMEM)] * 2,
        [],
        M3,
        6,
    )(label, g1, adjoint, *slots1, act1, slope1, theta1)
    got1a = send(theirs1a, to_core())

    def cut(rows, mine, got, name):
        return call(
            functools.partial(cut_kernel, rows),
            name,
            [IN_VMEM] * (len(mine) + len(got)),
            [(shape(2, CHUNK, 128, kind=BF), IN_VMEM)] * 4,
            [vmem(2, PACK, 128)],
            M5,
            2,
        )(*mine, *got)

    *out2, own2 = cut((PACK,), [mine2], [got2], "cut_two")
    got2 = [send(part, to_first(a)) for part, a in zip(out2, PEERS)]
    d_pre, got1a, *out2 = lax.optimization_barrier((d_pre, got1a, *out2))
    steep, mine1b, *theirs1b = call(
        fourth_kernel,
        "backward_one_layers",
        [IN_VMEM] * 10,
        [(shape(336, ROWS), IN_VMEM), (shape(2, LOW, 128, kind=BF), IN_VMEM)]
        + [(shape(LOW, 128, kind=BF), IN_VMEM)] * 2,
        [],
        M4,
        6,
    )(label, g1, d_pre, *slots1, e1, act1, slope1)
    got1b = [send(part, to_core()) for part in theirs1b]
    mine1b, got2[2] = lax.optimization_barrier((mine1b, got2[2]))
    *out1, own1 = cut((-LOW, TOP), [mine1b, mine1a], [*got1b, got1a], "cut_one")
    got1 = [send(part, to_first(a)) for part, a in zip(out1, PEERS)]

    def small(kernel, name, outs, *args, scratch=()):
        return call(
            kernel,
            name,
            [IN_VMEM] * len(args),
            [(shape(*dims, 128, kind=BF), IN_VMEM) for dims in outs],
            scratch,
            M5,
            1,
        )(*args)

    near2, far2 = small(fold_kernel, "fold", [(CHUNK,)] * 2, own2, *got2)
    *out, own = small(
        piece_kernel,
        "pieces",
        [(3, PIECE)] * 4,
        own1,
        *got1,
        near2,
        send(far2, to_x_by_core()),
        scratch=[vmem(3, CHUNK, 128)],
    )
    got = [send(part, to_second(b)) for part, b in zip(out, PEERS)]
    near, far = small(sum_kernel, "sums", [(2, PIECE), (PIECE,)], own, *got)
    got = [send(near, to_x(2)), send(far, to_x(3)), send(far, to_x(1))]
    done = small(across_kernel, "across", [(2, PIECE)], near, *got)[0]
    got = [send(done, to_second(b)) for b in FAR_FIRST]
    stack = small(stack_kernel, "stack", [(4, PIECE)] * 2, done, *got)
    grads = ()
    for k in (1, 0):
        stacks = [stack[k]] + [send(stack[k], to_first(a)) for a in FAR_FIRST]
        outs = (
            (560, 128), (128, 512), (512, 128), (128, 512), (512, 128), (512, 128), (128, 640),
        )
        grads = call(
            functools.partial(unpack_kernel, k),
            "unpack",
            [IN_VMEM] * 4 + [ANYWHERE] * (len(grads)),
            [(shape(2, *dims), ANYWHERE) for dims in outs],
            [vmem(PACK, 128)] + [vmem(*dims, kind=F32) for dims in outs] + [DMA((7,))],
            16,
            2,
            {4 + n: n for n in range(len(grads))},
        )(*stacks, *grads)
    return (look.T, rest.T, steep.T, *grads)


def solution(mesh):
    windows = P(("dp", "mp"), None)
    columns, rows = P(None, None, "mp"), P(None, "mp", None)
    tables = (columns, rows, columns, rows, columns, columns, rows)
    return jax.shard_map(
        shards,
        mesh=mesh,
        in_specs=(windows, P(("dp", "mp")), *tables, windows, windows),
        out_specs=(windows, windows, windows, *tables),
        check_vma=False,
    )
```

```python
import functools
import math

import jax
import jax.numpy as jnp
from jax import lax
from jax.experimental import pallas as pl
from jax.experimental.pallas import tpu as pltpu
from jax.sharding import PartitionSpec as P

BF = jnp.bfloat16
F32 = jnp.float32
ROWS = 768
ENTRY, SECOND, THIRD, FOURTH, BACK, FORE, BASIS, USED = 0, 560, 1072, 1584, 2096, 2608, 3120, 3760
PACK = 3840
PEERS = (1, 3, 2)
EARLY, EARLY_PACK, LATE = 1712, 1792, 2048
EARLY_CHUNK, LATE_CHUNK = EARLY_PACK // 4, LATE // 4
EARLY_PIECE, LATE_PIECE = EARLY_PACK // 16, LATE // 16
FAR_FIRST = (1, 3, 2)
CHUNK, PIECE = PACK // 4, PACK // 16


def place(y, x, z, c):
    y, x, z, c = y % 4, x % 4, z % 4, c % 2
    return ((((y * 2 + x // 2) * 4 + z) * 2) + x % 2) * 2 + c


def pairs(move):
    out = []
    for y in range(4):
        for x in range(4):
            for z in range(4):
                for c in range(2):
                    out.append((place(y, x, z, c), place(*move(y, x, z, c))))
    return tuple(out)


def to_core():
    return pairs(lambda y, x, z, c: (y, x, z, 1 - c))


def to_x(bits):
    return pairs(lambda y, x, z, c: (y, x ^ bits, z, c))


def to_x_by_core():
    return pairs(lambda y, x, z, c: (y, x ^ (1 if c == 0 else 3), z, c))


def to_first(bits):
    return pairs(lambda y, x, z, c: (y ^ bits, x, z, c) if c == 0 else (y, x, z ^ bits, c))


def to_second(bits):
    return pairs(lambda y, x, z, c: (y, x, z ^ bits, c) if c == 0 else (y ^ bits, x, z, c))


def send(values, where):
    return lax.ppermute(values, ("dp", "mp"), where)


def row_of(count, begin=0):
    return lax.broadcasted_iota(jnp.int32, (count, ROWS), 0) + begin


def turn(values, shift):
    return pltpu.roll(values, shift % values.shape[0], 0)


def widen_look(v, label):
    zero = jnp.float32(0)
    e = [label == g for g in range(4)]
    near = turn(v[:56], 2)
    far = turn(v[:128], 2)
    top = row_of(56) < 2
    tip = row_of(8) < 2
    mid = jnp.where(
        top, jnp.where(e[0], v[40:96], zero), jnp.where(e[1], near, zero)
    )
    joint = jnp.where(
        tip, jnp.where(e[1], near[:8], zero), jnp.where(e[2], far[:8], zero)
    )
    return jnp.concatenate(
        [
            jnp.where(e[0], v[:40], zero),
            mid,
            joint,
            jnp.where(e[2], far[8:], zero),
            jnp.where(e[3], v, zero),
        ],
        axis=0,
    )


def pick_look(u, label):
    zero = jnp.float32(0)
    e = [label == g for g in range(4)]
    last = jnp.where(e[3], u[224:560], zero)
    near = turn(u[40:104], -2)
    far = turn(u[96:224], -2)
    row = row_of(56)
    begin = jnp.where(
        e[2],
        far[:56],
        jnp.where(e[1], near[:56], jnp.where(e[0] & (row < 42), u[:56], last[:56])),
    )
    middle = jnp.where(e[2] & (row_of(72, 56) < 126), far[56:], last[56:128])
    return jnp.concatenate([begin, middle, last[128:]], axis=0)


def widen_reach(a, label):
    zero = jnp.float32(0)
    e = [label == g for g in range(4)]
    one = turn(a[:16], 6)
    two = turn(a[:24], 6)
    row = row_of(8)
    return jnp.concatenate(
        [
            jnp.where(row < 6, jnp.where(e[0], a[:8], zero), jnp.where(e[1], one[:8], zero)),
            jnp.where(row < 6, jnp.where(e[1], one[8:], zero), jnp.where(e[2], two[:8], zero)),
            jnp.where(e[2], two[8:], zero),
            jnp.where(e[3], a, zero),
        ],
        axis=0,
    )


def pick_reach(u, label):
    zero = jnp.float32(0)
    e = [label == g for g in range(4)]
    last = jnp.where(e[3], u[32:], zero)
    one = turn(u[:16], -6)
    two = turn(u[8:32], -6)
    row = row_of(8)
    return jnp.concatenate(
        [
            jnp.where(
                e[2],
                two[:8],
                jnp.where(e[1], one[:8], jnp.where(e[0] & (row < 6), u[:8], last[:8])),
            ),
            jnp.where(e[2] & (row_of(16, 8) < 18), two[8:], last[8:24]),
            last[24:],
        ],
        axis=0,
    )


def look_mask(label):
    reach = jnp.where(label == 0, 42, jnp.where(label == 1, 56, jnp.where(label == 2, 126, 336)))
    return row_of(336) < reach


def by_columns(slots, begin, count):
    return jnp.concatenate([slot[begin : begin + count, :] for slot in slots], axis=1)


def by_rows(slots, begin, count):
    return jnp.concatenate(
        [
            jnp.concatenate(
                [slot[begin + 128 * i : begin + 128 * (i + 1), :] for i in range(count)], axis=1
            )
            for slot in slots
        ],
        axis=0,
    )


def dot(a, b):
    return jnp.dot(a, b, preferred_element_type=F32)


def dot_t(a, b):
    return lax.dot_general(a, b, (((1,), (1,)), ((), ())), preferred_element_type=F32)


def t_dot(a, b):
    return lax.dot_general(a, b, (((0,), (0,)), ((), ())), preferred_element_type=F32)


def silu_both(pre):
    s = 0.5 * jnp.tanh(0.5 * pre) + 0.5
    act = pre * s
    return act.astype(BF), (s + act * (1.0 - s)).astype(BF)


TABLES = {
    "entry": (ENTRY, 560),
    "second": (SECOND, 512),
    "third": (THIRD, 512),
    "fourth": (FOURTH, 512),
    "back": (BACK, 512),
    "fore": (FORE, 512),
    "basis": (BASIS, 640),
}


class Weights:
    def __init__(self, slots):
        self.slots = slots

    def get(self, name):
        begin, count = TABLES[name]
        if name in ("second", "fourth"):
            return by_rows(self.slots, begin, 4)
        return by_columns(self.slots, begin, count)


def run_forward(state, label, weights, e_ref, act_ref, slope_ref, theta_ref):
    e_ref[...] = widen_look(state, label).astype(BF)
    act, slope = silu_both(t_dot(weights.get("entry"), e_ref[...]))
    act_ref[0], slope_ref[0] = act, slope
    for i, name in enumerate(("second", "third", "fourth")):
        act, slope = silu_both(t_dot(weights.get(name), act_ref[i]))
        act_ref[i + 1], slope_ref[i + 1] = act, slope
    theta_ref[0] = t_dot(weights.get("back"), act_ref[3]).astype(BF)
    theta_ref[1] = t_dot(weights.get("fore"), act_ref[3]).astype(BF)
    basis = weights.get("basis")
    return dot(basis[:560], theta_ref[0]), dot(basis[560:], theta_ref[1])


class Grads:
    def __init__(self, outs, base=0):
        self.outs, self.base = outs, base

    def put(self, name, grad):
        begin, count = TABLES[name]
        at = begin - self.base
        for slot in range(4):
            out = self.outs[slot % 2]
            out = out[slot // 2] if isinstance(out, tuple) else out.at[slot // 2]
            if name in ("second", "fourth"):
                for i in range(4):
                    out[at + 128 * i : at + 128 * (i + 1), :] = grad[
                        128 * slot : 128 * (slot + 1), 128 * i : 128 * (i + 1)
                    ].astype(BF)
            else:
                out[at : at + count, :] = grad[:, 128 * slot : 128 * (slot + 1)].astype(BF)
        if name == "basis" and not self.base:
            for out in self.outs:
                out[:, USED:PACK, :] = jnp.zeros((2, PACK - USED, 128), BF)


def backward_heads(g, fore_wide, label, weights, act_ref, slope_ref, theta_ref, grads):
    d_back = -widen_look(g, label).astype(BF)
    d_fore = fore_wide.astype(BF)
    basis = weights.get("basis")
    d_theta_b = t_dot(basis[:560], d_back).astype(BF)
    d_theta_f = t_dot(basis[560:], d_fore).astype(BF)
    grads.put(
        "basis",
        jnp.concatenate([dot_t(d_back, theta_ref[0]), dot_t(d_fore, theta_ref[1])], axis=0),
    )
    d_act = dot(weights.get("back"), d_theta_b) + dot(weights.get("fore"), d_theta_f)
    grads.put("back", dot_t(act_ref[3], d_theta_b))
    grads.put("fore", dot_t(act_ref[3], d_theta_f))
    d_pre = (d_act * slope_ref[3].astype(F32)).astype(BF)
    grads.put("fourth", dot_t(act_ref[2], d_pre))
    return d_pre


def backward_layers(g, d_pre, label, weights, e_ref, act_ref, slope_ref, grads):
    d_act = dot(weights.get("fourth"), d_pre)
    d_pre = (d_act * slope_ref[2].astype(F32)).astype(BF)
    grads.put("third", dot_t(act_ref[1], d_pre))
    d_act = dot(weights.get("third"), d_pre)
    d_pre = (d_act * slope_ref[1].astype(F32)).astype(BF)
    grads.put("second", dot_t(act_ref[0], d_pre))
    d_act = dot(weights.get("second"), d_pre)
    d_pre = (d_act * slope_ref[0].astype(F32)).astype(BF)
    grads.put("entry", dot_t(e_ref[...], d_pre))
    return g + pick_look(dot(weights.get("entry"), d_pre), label)


def places():
    dp, core = lax.axis_index("dp"), lax.rem(lax.axis_index("mp"), 2)
    y, z = lax.div(dp, 8), lax.rem(dp, 4)
    return jnp.where(core == 0, y, z), jnp.where(core == 0, z, y)


def pack_kernel(*refs):
    tables, both, one = refs[:7], refs[7], refs[8]
    for k in range(2):
        for (name, (begin, count)), table in zip(TABLES.items(), tables):
            if table.shape[2] == 128:
                both[k, begin : begin + count, :] = table[k]
                continue
            for i in range(count // 128):
                block = table[k, :, 128 * i : 128 * (i + 1)]
                both[k, begin + 128 * i : begin + 128 * (i + 1), :] = block.T if name == "basis" else block
        both[k, USED:PACK, :] = jnp.zeros((PACK - USED, 128), BF)
    one[...] = both[0]


def quarter_kernel(*refs):
    tables, out, turned, sem = refs[:7], refs[7], refs[8], refs[9]
    i1, _ = places()
    for n in range(4):

        @pl.when(i1 == n)
        def _():
            copies = []

            def copy(source, target):
                copies.append(pltpu.make_async_copy(source, target, sem.at[len(copies)]))
                copies[-1].start()

            for (name, (begin, count)), table in zip(TABLES.items(), tables):
                step = 128 if table.shape[2] > 128 else count
                for at in range(begin, begin + count, step):
                    low, high = max(at, n * CHUNK), min(at + step, (n + 1) * CHUNK)
                    if low >= high or name == "basis":
                        continue
                    columns = at - begin if step == 128 else 0
                    copy(
                        table.at[1, pl.ds(low - at, high - low), pl.ds(columns, 128)],
                        out.at[pl.ds(low - n * CHUNK, high - low)],
                    )
            if n == 3:
                copy(tables[6].at[1], turned)
                out[USED - n * CHUNK :, :] = jnp.zeros((PACK - USED, 128), BF)
            for c in copies:
                c.wait()
            if n == 3:
                for i in range(5):
                    at = BASIS - n * CHUNK + 128 * i
                    out[at : at + 128, :] = turned[:, 128 * i : 128 * (i + 1)].T


def join_kernel(q0, q1, q2, q3, out):
    i1, _ = places()
    for bits, quarter in zip((0, *PEERS), (q0, q1, q2, q3)):
        begin = pl.multiple_of((i1 ^ bits) * CHUNK, CHUNK)
        out[pl.ds(begin, CHUNK), :] = quarter[...]


def first_kernel(label, lag, s0, s1, s2, s3, state_out, look_out, e, act, slope, theta):
    weights = Weights((s0.at[0], s1.at[0], s2, s3))
    labels = label[...]
    state = jnp.where(look_mask(labels), lag[...].astype(F32), 0.0)
    heads, fore = run_forward(state, labels, weights, e, act, slope, theta)
    state_out[...] = state - pick_look(heads, labels)
    look_out[...] = pick_reach(fore, labels)


def second_kernel(
    label, state_in, look_in, left, adjoint, s0, s1, s2, s3, rest, look, g_out, mine, theirs, e, act, slope, theta
):
    weights = Weights((s0.at[1], s1.at[1], s2, s3))
    labels = label[...]
    heads, fore = run_forward(state_in[...], labels, weights, e, act, slope, theta)
    rest[...] = state_in[...] - pick_look(heads, labels)
    look[...] = look_in[...] + pick_reach(fore, labels)
    grads = Grads((mine, theirs))
    g = left[...].astype(F32)
    fore_wide = widen_reach(adjoint[...].astype(F32), labels)
    d_pre = backward_heads(g, fore_wide, labels, weights, act, slope, theta, grads)
    g_out[...] = backward_layers(g, d_pre, labels, weights, e, act, slope, grads)


def third_kernel(label, g_in, adjoint, s0, s1, s2, s3, act, slope, theta, d_out, mine, theirs):
    grads = Grads((mine, theirs), FOURTH)
    labels = label[...]
    fore_wide = widen_reach(adjoint[...].astype(F32), labels)
    d_out[...] = backward_heads(
        g_in[...], fore_wide, labels, Weights((s0.at[0], s1.at[0], s2, s3)), act, slope, theta, grads
    )


def fourth_kernel(label, g_in, d_in, s0, s1, s2, s3, e, act, slope, steep, mine, near, far):
    grads = Grads((mine, (near, far)))
    labels = label[...]
    g = backward_layers(g_in[...], d_in[...], labels, Weights((s0.at[0], s1.at[0], s2, s3)), e, act, slope, grads)
    steep[...] = jnp.where(look_mask(labels), g, 0.0)


def cut_kernel(mine, got, *refs):
    outs, whole = refs[:4], refs[4]
    i1, _ = places()
    whole[...] = (mine[...].astype(F32) + got[...].astype(F32)).astype(BF)
    for bits, out in zip((*PEERS, 0), outs):
        begin = pl.multiple_of((i1 ^ bits) * CHUNK, CHUNK)
        out[...] = whole[:, pl.ds(begin, CHUNK), :]


def fold_heads_kernel(mine, got, near, rest, far):
    sums = (mine[...].astype(F32) + got[...].astype(F32)).astype(BF)
    near[...] = sums[0]
    rest[...] = sums[1, : EARLY - FOURTH]
    far[...] = sums[1, EARLY - FOURTH :]


def cut_one_kernel(mine, got0, got1, near, rest, came, *refs):
    outs, early, late = refs[:4], refs[4], refs[5]
    i1, _ = places()
    for half, got in enumerate((got0, got1)):
        early[half, :LOW] = (mine[half].astype(F32) + got[...].astype(F32)).astype(BF)
    early[0, LOW:EARLY] = near[: EARLY - LOW, :]
    early[1, LOW:EARLY] = rest[...]
    early[:, EARLY:] = jnp.zeros((2, EARLY_PACK - EARLY, 128), BF)
    late[...] = (near[EARLY - LOW :, :].astype(F32) + came[...].astype(F32)).astype(BF)
    for bits, out in zip((*PEERS, 0), outs):
        begin = pl.multiple_of((i1 ^ bits) * EARLY_CHUNK, EARLY_CHUNK)
        for half in range(2):
            out[half * EARLY_CHUNK : (half + 1) * EARLY_CHUNK, :] = early[half, pl.ds(begin, EARLY_CHUNK), :]
        begin = pl.multiple_of((i1 ^ bits) * LATE_CHUNK, LATE_CHUNK)
        out[2 * EARLY_CHUNK :, :] = late[pl.ds(begin, LATE_CHUNK), :]


def total(refs):
    a, b, c, d = (ref[...].astype(F32) for ref in refs)
    return ((a + b) + (c + d)).astype(BF)


def fold_kernel(own, a, b, c, near, far):
    near[...], far[...] = total((own, a, b, c))


def piece_kernel(own, a, b, c, near, came, *refs):
    outs, one, two = refs[:4], refs[4], refs[5]
    _, i2 = places()
    one[...] = total((own, a, b, c))
    two[...] = (near[...].astype(F32) + came[...].astype(F32)).astype(BF)
    for bits, out in zip((*PEERS, 0), outs):
        at = 0
        for ref, base, count in (
            (one, 0, EARLY_PIECE),
            (one, 2 * EARLY_CHUNK, LATE_PIECE),
            (two, 0, PIECE),
            (one, EARLY_CHUNK, EARLY_PIECE),
        ):
            begin = pl.multiple_of(base + (i2 ^ bits) * count, 16)
            out[at : at + count, :] = ref[pl.ds(begin, count), :]
            at += count


def sum_kernel(own, a, b, c, near, far):
    sums = total((own, a, b, c))
    near[0] = sums[:PIECE]
    near[1] = sums[PIECE : 2 * PIECE]
    far[...] = sums[2 * PIECE :]


def across_kernel(near, a, b, c, out):
    both = near[...].astype(F32) + a[...].astype(F32)
    add = b[...].astype(F32) + c[...].astype(F32)
    out[0, :EARLY_PIECE] = (both[0, :EARLY_PIECE] + add).astype(BF)
    out[0, EARLY_PIECE:] = both[0, EARLY_PIECE:].astype(BF)
    out[1] = both[1].astype(BF)


def stack_kernel(*refs):
    for k in range(2):
        for n in range(4):
            refs[4 + k][n] = refs[n][k]
    refs[6][...] = refs[3][0, :16]


def unpack_kernel(k, *refs):
    stacks, outs, whole, bufs, sem = refs[:4], refs[-16:-9], refs[-9], refs[-8:-1], refs[-1]
    i1, i2 = places()
    parts = ((0, EARLY_CHUNK, EARLY_PIECE), (EARLY_PACK, LATE_CHUNK, LATE_PIECE)) if k == 0 else ((0, CHUNK, PIECE),)
    for a, stack in zip((0, *FAR_FIRST), stacks):
        for slot, b in enumerate((0, *FAR_FIRST)):
            row = 0
            for base, chunk, piece in parts:
                at = pl.multiple_of(base + (i1 ^ a) * chunk + (i2 ^ b) * piece, 16)
                whole[pl.ds(at, piece), :] = stack[slot, row : row + piece, :]
                row += piece

    def rows(begin, count):
        if k == 0 and begin >= EARLY:
            begin += EARLY_PACK - EARLY
        return whole[begin : begin + count, :].astype(F32) * scale

    scale = 1.0 / math.sqrt(98304)
    copies = []
    for (name, (begin, count)), out, buf in zip(TABLES.items(), outs, bufs):
        if buf.shape[1] == 128:
            buf[...] = rows(begin, count)
        else:
            for i in range(count // 128):
                part = rows(begin + 128 * i, 128)
                buf[:, 128 * i : 128 * (i + 1)] = part.T if name == "basis" else part
        copies.append(pltpu.make_async_copy(buf, out.at[k], sem.at[len(copies)]))
        copies[-1].start()
    for copy in copies:
        copy.wait()


def shape(*dims, kind=F32):
    return jax.ShapeDtypeStruct(dims, kind)


def vmem(*dims, kind=BF):
    return pltpu.VMEM(dims, kind)


M1, M2, M3, M4, M5 = 12, 20, 12, 12, 8
DMA = pltpu.SemaphoreType.DMA
IN_VMEM = pl.BlockSpec(memory_space=pltpu.VMEM)
ANYWHERE = pl.BlockSpec(memory_space=pl.ANY)


def call(kernel, name, ins, outs, scratch, mib, us, aliases={}):
    return pl.pallas_call(
        kernel,
        out_shape=[o[0] for o in outs],
        in_specs=ins,
        out_specs=[o[1] for o in outs],
        scratch_shapes=scratch,
        compiler_params=pltpu.CompilerParams(vmem_limit_bytes=mib * 1024 * 1024),
        cost_estimate=pl.CostEstimate(
            flops=int(us * 8e8), bytes_accessed=int(us * 1e6), transcendentals=0
        ),
        name=name,
        input_output_aliases=aliases,
    )


ACTS = (4, 512, ROWS)
KEPT = [(560, ROWS), ACTS, ACTS, (2, 512, ROWS)]
TOP, LOW = USED - FOURTH, FOURTH


def plus(*parts):
    return sum(part.astype(F32) for part in parts).astype(BF)


def shards(lag, label, entry, second, third, fourth, back, fore, basis, adjoint, left):
    label = label[None, :]
    lag, adjoint, left = lag.T, adjoint.T, left.T
    whole, part = shape(PACK, 128, kind=BF), shape(CHUNK, 128, kind=BF)
    tables = (entry, second, third, fourth, back, fore, basis)
    quarter = call(
        quarter_kernel,
        "pack_quarter",
        [ANYWHERE] * 7,
        [(part, IN_VMEM)],
        [vmem(128, 640), DMA((8,))],
        60,
        1,
    )(*tables)[0]
    quarter, *tables = lax.optimization_barrier((quarter, *tables))
    both, one = call(
        pack_kernel,
        "pack",
        [IN_VMEM] * 7,
        [(shape(2, PACK, 128, kind=BF), IN_VMEM), (whole, IN_VMEM)],
        [],
        60,
        3,
    )(*tables)
    quarter = send(quarter, to_x_by_core())
    one, quarter = lax.optimization_barrier((one, quarter))
    across = send(one, to_x_by_core())
    quarters = [quarter] + [send(quarter, to_first(a)) for a in PEERS]
    other = send(both, to_core())
    across, *quarters = lax.optimization_barrier((across, *quarters))
    slots1 = (both, other, across, send(across, to_core()))
    across = call(join_kernel, "join", [IN_VMEM] * 4, [(whole, IN_VMEM)], [], M5, 1)(*quarters)[0]
    slots2 = (both, other, across, send(across, to_core()))
    state1, look1, e1, act1, slope1, theta1 = call(
        first_kernel,
        "forward_one",
        [IN_VMEM] * 6,
        [(shape(336, ROWS), IN_VMEM), (shape(48, ROWS), IN_VMEM)]
        + [(shape(*k, kind=BF), IN_VMEM) for k in KEPT],
        [],
        M1,
        6,
    )(label, lag, *slots1)
    rest, look, g1, mine2, theirs2 = call(
        second_kernel,
        "block_two",
        [IN_VMEM] * 9,
        [(shape(336, ROWS), IN_VMEM), (shape(48, ROWS), IN_VMEM), (shape(336, ROWS), IN_VMEM)]
        + [(shape(2, PACK, 128, kind=BF), IN_VMEM)] * 2,
        [vmem(*k) for k in KEPT],
        M2,
        14,
    )(label, state1, look1, left, adjoint, *slots2)
    got2 = send(theirs2, to_core())
    d_pre, mine1a, theirs1a = call(
        third_kernel,
        "backward_one_heads",
        [IN_VMEM] * 10,
        [(shape(512, ROWS, kind=BF), IN_VMEM)] + [(shape(2, TOP, 128, kind=BF), IN_VMEM)] * 2,
        [],
        M3,
        6,
    )(label, g1, adjoint, *slots1, act1, slope1, theta1)
    got1a = send(theirs1a, to_core())

    def small(kernel, name, outs, *args, scratch=()):
        return call(
            kernel,
            name,
            [IN_VMEM] * len(args),
            [(shape(*dims, 128, kind=BF), IN_VMEM) for dims in outs],
            scratch,
            M5,
            1,
        )(*args)

    *out2, own2 = small(cut_kernel, "cut_two", [(2, CHUNK)] * 4, mine2, got2, scratch=[vmem(2, PACK, 128)])
    got2 = [send(part, to_first(a)) for part, a in zip(out2, PEERS)]
    near1, rest1, far1 = small(
        fold_heads_kernel, "fold_heads", [(TOP,), (EARLY - FOURTH,), (LATE,)], mine1a, got1a
    )
    d_pre, far1, *out2 = lax.optimization_barrier((d_pre, far1, *out2))
    came1 = send(far1, to_x_by_core())
    steep, mine1b, *theirs1b = call(
        fourth_kernel,
        "backward_one_layers",
        [IN_VMEM] * 10,
        [(shape(336, ROWS), IN_VMEM), (shape(2, LOW, 128, kind=BF), IN_VMEM)]
        + [(shape(LOW, 128, kind=BF), IN_VMEM)] * 2,
        [],
        M4,
        6,
    )(label, g1, d_pre, *slots1, e1, act1, slope1)
    got1b = [send(part, to_core()) for part in theirs1b]
    mine1b, got2[2] = lax.optimization_barrier((mine1b, got2[2]))
    *out1, own1 = small(
        cut_one_kernel,
        "cut_one",
        [(2 * EARLY_CHUNK + LATE_CHUNK,)] * 4,
        mine1b,
        *got1b,
        near1,
        rest1,
        came1,
        scratch=[vmem(2, EARLY_PACK, 128), vmem(LATE, 128)],
    )
    got1 = [send(part, to_first(a)) for part, a in zip(out1, PEERS)]

    near2, far2 = small(fold_kernel, "fold", [(CHUNK,)] * 2, own2, *got2)
    *out, own = small(
        piece_kernel,
        "pieces",
        [(2 * PIECE + EARLY_PIECE,)] * 4,
        own1,
        *got1,
        near2,
        send(far2, to_x_by_core()),
        scratch=[vmem(2 * EARLY_CHUNK + LATE_CHUNK, 128), vmem(CHUNK, 128)],
    )
    got = [send(part, to_second(b)) for part, b in zip(out, PEERS)]
    near, far = small(sum_kernel, "sums", [(2, PIECE), (EARLY_PIECE,)], own, *got)
    x1, x3 = send(far, to_x(1)), send(far, to_x(3))
    got = [send(near, to_x(2)), x3, x1]
    done = small(across_kernel, "across", [(2, PIECE)], near, *got)[0]
    got = [send(done, to_second(b)) for b in FAR_FIRST]
    *stack, here = small(stack_kernel, "stack", [(4, PIECE)] * 2 + [(16,)], done, *got)
    *stack, here = lax.optimization_barrier((*stack, send(here, to_core())))
    grads = ()
    for k in (1, 0):
        stacks = [stack[k]] + [send(stack[k], to_first(a)) for a in FAR_FIRST]
        outs = (
            (560, 128), (128, 512), (512, 128), (128, 512), (512, 128), (512, 128), (128, 640),
        )
        grads = call(
            functools.partial(unpack_kernel, k),
            "unpack",
            [IN_VMEM] * 4 + [ANYWHERE] * (len(grads) + 1),
            [(shape(2, *dims), ANYWHERE) for dims in outs],
            [vmem(PACK, 128)] + [vmem(*dims, kind=F32) for dims in outs] + [DMA((7,))],
            16,
            2,
            {4 + n: n for n in range(len(grads))},
        )(*stacks, *grads, here)
    return (look.T, rest.T, steep.T, *grads)


def solution(mesh):
    windows = P(("dp", "mp"), None)
    columns, rows = P(None, None, "mp"), P(None, "mp", None)
    tables = (columns, rows, columns, rows, columns, columns, rows)
    return jax.shard_map(
        shards,
        mesh=mesh,
        in_specs=(windows, P(("dp", "mp")), *tables, windows, windows),
        out_specs=(windows, windows, windows, *tables),
        check_vma=False,
    )
```

```python
import functools
import math

import jax
import jax.numpy as jnp
from jax import lax
from jax.experimental import pallas as pl
from jax.experimental.pallas import tpu as pltpu
from jax.sharding import PartitionSpec as P

BF = jnp.bfloat16
F32 = jnp.float32
ROWS = 768
ENTRY, SECOND, THIRD, FOURTH, BACK, FORE, BASIS, USED = 0, 560, 1072, 1584, 2096, 2608, 3120, 3760
PACK = 3840
PEERS = (1, 3, 2)
SECOND_STEP = (2, 3, 1)
EARLY, EARLY_PACK, LATE = 1712, 1792, 2048
EARLY_CHUNK, LATE_CHUNK = EARLY_PACK // 4, LATE // 4
EARLY_PIECE, LATE_PIECE = EARLY_PACK // 16, LATE // 16
FAR_FIRST = (1, 3, 2)
CHUNK, PIECE = PACK // 4, PACK // 16


def place(y, x, z, c):
    y, x, z, c = y % 4, x % 4, z % 4, c % 2
    return ((((y * 2 + x // 2) * 4 + z) * 2) + x % 2) * 2 + c


def pairs(move):
    out = []
    for y in range(4):
        for x in range(4):
            for z in range(4):
                for c in range(2):
                    out.append((place(y, x, z, c), place(*move(y, x, z, c))))
    return tuple(out)


def to_core():
    return pairs(lambda y, x, z, c: (y, x, z, 1 - c))


def to_x(bits):
    return pairs(lambda y, x, z, c: (y, x ^ bits, z, c))


def to_x_by_core():
    return pairs(lambda y, x, z, c: (y, x ^ (1 if c == 0 else 3), z, c))


def to_first(bits):
    return pairs(lambda y, x, z, c: (y ^ bits, x, z, c) if c == 0 else (y, x, z ^ bits, c))


def to_second(bits):
    return pairs(lambda y, x, z, c: (y, x, z ^ bits, c) if c == 0 else (y ^ bits, x, z, c))


def send(values, where):
    return lax.ppermute(values, ("dp", "mp"), where)


def row_of(count, begin=0):
    return lax.broadcasted_iota(jnp.int32, (count, ROWS), 0) + begin


def turn(values, shift):
    return pltpu.roll(values, shift % values.shape[0], 0)


def widen_look(v, label):
    zero = jnp.float32(0)
    e = [label == g for g in range(4)]
    near = turn(v[:56], 2)
    far = turn(v[:128], 2)
    top = row_of(56) < 2
    tip = row_of(8) < 2
    mid = jnp.where(
        top, jnp.where(e[0], v[40:96], zero), jnp.where(e[1], near, zero)
    )
    joint = jnp.where(
        tip, jnp.where(e[1], near[:8], zero), jnp.where(e[2], far[:8], zero)
    )
    return jnp.concatenate(
        [
            jnp.where(e[0], v[:40], zero),
            mid,
            joint,
            jnp.where(e[2], far[8:], zero),
            jnp.where(e[3], v, zero),
        ],
        axis=0,
    )


def pick_look(u, label):
    zero = jnp.float32(0)
    e = [label == g for g in range(4)]
    last = jnp.where(e[3], u[224:560], zero)
    near = turn(u[40:104], -2)
    far = turn(u[96:224], -2)
    row = row_of(56)
    begin = jnp.where(
        e[2],
        far[:56],
        jnp.where(e[1], near[:56], jnp.where(e[0] & (row < 42), u[:56], last[:56])),
    )
    middle = jnp.where(e[2] & (row_of(72, 56) < 126), far[56:], last[56:128])
    return jnp.concatenate([begin, middle, last[128:]], axis=0)


def widen_reach(a, label):
    zero = jnp.float32(0)
    e = [label == g for g in range(4)]
    one = turn(a[:16], 6)
    two = turn(a[:24], 6)
    row = row_of(8)
    return jnp.concatenate(
        [
            jnp.where(row < 6, jnp.where(e[0], a[:8], zero), jnp.where(e[1], one[:8], zero)),
            jnp.where(row < 6, jnp.where(e[1], one[8:], zero), jnp.where(e[2], two[:8], zero)),
            jnp.where(e[2], two[8:], zero),
            jnp.where(e[3], a, zero),
        ],
        axis=0,
    )


def pick_reach(u, label):
    zero = jnp.float32(0)
    e = [label == g for g in range(4)]
    last = jnp.where(e[3], u[32:], zero)
    one = turn(u[:16], -6)
    two = turn(u[8:32], -6)
    row = row_of(8)
    return jnp.concatenate(
        [
            jnp.where(
                e[2],
                two[:8],
                jnp.where(e[1], one[:8], jnp.where(e[0] & (row < 6), u[:8], last[:8])),
            ),
            jnp.where(e[2] & (row_of(16, 8) < 18), two[8:], last[8:24]),
            last[24:],
        ],
        axis=0,
    )


def look_mask(label):
    reach = jnp.where(label == 0, 42, jnp.where(label == 1, 56, jnp.where(label == 2, 126, 336)))
    return row_of(336) < reach


def by_columns(slots, begin, count):
    return jnp.concatenate([slot[begin : begin + count, :] for slot in slots], axis=1)


def by_rows(slots, begin, count):
    return jnp.concatenate(
        [
            jnp.concatenate(
                [slot[begin + 128 * i : begin + 128 * (i + 1), :] for i in range(count)], axis=1
            )
            for slot in slots
        ],
        axis=0,
    )


def dot(a, b):
    return jnp.dot(a, b, preferred_element_type=F32)


def dot_t(a, b):
    return lax.dot_general(a, b, (((1,), (1,)), ((), ())), preferred_element_type=F32)


def t_dot(a, b):
    return lax.dot_general(a, b, (((0,), (0,)), ((), ())), preferred_element_type=F32)


def silu_both(pre):
    s = 0.5 * jnp.tanh(0.5 * pre) + 0.5
    act = pre * s
    return act.astype(BF), (s + act * (1.0 - s)).astype(BF)


TABLES = {
    "entry": (ENTRY, 560),
    "second": (SECOND, 512),
    "third": (THIRD, 512),
    "fourth": (FOURTH, 512),
    "back": (BACK, 512),
    "fore": (FORE, 512),
    "basis": (BASIS, 640),
}


class Weights:
    def __init__(self, slots):
        self.slots = slots

    def get(self, name):
        begin, count = TABLES[name]
        if name in ("second", "fourth"):
            return by_rows(self.slots, begin, 4)
        return by_columns(self.slots, begin, count)


def run_forward(state, label, weights, e_ref, act_ref, slope_ref, theta_ref):
    e_ref[...] = widen_look(state, label).astype(BF)
    act, slope = silu_both(t_dot(weights.get("entry"), e_ref[...]))
    act_ref[0], slope_ref[0] = act, slope
    for i, name in enumerate(("second", "third", "fourth")):
        act, slope = silu_both(t_dot(weights.get(name), act_ref[i]))
        act_ref[i + 1], slope_ref[i + 1] = act, slope
    theta_ref[0] = t_dot(weights.get("back"), act_ref[3]).astype(BF)
    theta_ref[1] = t_dot(weights.get("fore"), act_ref[3]).astype(BF)
    basis = weights.get("basis")
    return dot(basis[:560], theta_ref[0]), dot(basis[560:], theta_ref[1])


class Grads:
    def __init__(self, outs, base=0):
        self.outs, self.base = outs, base

    def put(self, name, grad):
        begin, count = TABLES[name]
        at = begin - self.base
        for slot in range(4):
            out = self.outs[slot % 2]
            out = out[slot // 2] if isinstance(out, tuple) else out.at[slot // 2]
            if name in ("second", "fourth"):
                for i in range(4):
                    out[at + 128 * i : at + 128 * (i + 1), :] = grad[
                        128 * slot : 128 * (slot + 1), 128 * i : 128 * (i + 1)
                    ].astype(BF)
            else:
                out[at : at + count, :] = grad[:, 128 * slot : 128 * (slot + 1)].astype(BF)
        if name == "basis" and not self.base:
            for out in self.outs:
                out[:, USED:PACK, :] = jnp.zeros((2, PACK - USED, 128), BF)


def backward_heads(g, fore_wide, label, weights, act_ref, slope_ref, theta_ref, grads):
    d_back = -widen_look(g, label).astype(BF)
    d_fore = fore_wide.astype(BF)
    basis = weights.get("basis")
    d_theta_b = t_dot(basis[:560], d_back).astype(BF)
    d_theta_f = t_dot(basis[560:], d_fore).astype(BF)
    grads.put(
        "basis",
        jnp.concatenate([dot_t(d_back, theta_ref[0]), dot_t(d_fore, theta_ref[1])], axis=0),
    )
    d_act = dot(weights.get("back"), d_theta_b) + dot(weights.get("fore"), d_theta_f)
    grads.put("back", dot_t(act_ref[3], d_theta_b))
    grads.put("fore", dot_t(act_ref[3], d_theta_f))
    d_pre = (d_act * slope_ref[3].astype(F32)).astype(BF)
    grads.put("fourth", dot_t(act_ref[2], d_pre))
    return d_pre


def backward_layers(g, d_pre, label, weights, e_ref, act_ref, slope_ref, grads):
    d_act = dot(weights.get("fourth"), d_pre)
    d_pre = (d_act * slope_ref[2].astype(F32)).astype(BF)
    grads.put("third", dot_t(act_ref[1], d_pre))
    d_act = dot(weights.get("third"), d_pre)
    d_pre = (d_act * slope_ref[1].astype(F32)).astype(BF)
    grads.put("second", dot_t(act_ref[0], d_pre))
    d_act = dot(weights.get("second"), d_pre)
    d_pre = (d_act * slope_ref[0].astype(F32)).astype(BF)
    grads.put("entry", dot_t(e_ref[...], d_pre))
    return g + pick_look(dot(weights.get("entry"), d_pre), label)


def places():
    dp, core = lax.axis_index("dp"), lax.rem(lax.axis_index("mp"), 2)
    y, z = lax.div(dp, 8), lax.rem(dp, 4)
    return jnp.where(core == 0, y, z), jnp.where(core == 0, z, y)


def pack_kernel(*refs):
    tables, both, one = refs[:7], refs[7], refs[8]
    for k in range(2):
        for (name, (begin, count)), table in zip(TABLES.items(), tables):
            if table.shape[2] == 128:
                both[k, begin : begin + count, :] = table[k]
                continue
            for i in range(count // 128):
                block = table[k, :, 128 * i : 128 * (i + 1)]
                both[k, begin + 128 * i : begin + 128 * (i + 1), :] = block.T if name == "basis" else block
        both[k, USED:PACK, :] = jnp.zeros((PACK - USED, 128), BF)
    one[...] = both[0]


def quarter_kernel(*refs):
    tables, out, turned, sem = refs[:7], refs[7], refs[8], refs[9]
    i1, _ = places()
    for n in range(4):

        @pl.when(i1 == n)
        def _():
            copies = []

            def copy(source, target):
                copies.append(pltpu.make_async_copy(source, target, sem.at[len(copies)]))
                copies[-1].start()

            for (name, (begin, count)), table in zip(TABLES.items(), tables):
                step = 128 if table.shape[2] > 128 else count
                for at in range(begin, begin + count, step):
                    low, high = max(at, n * CHUNK), min(at + step, (n + 1) * CHUNK)
                    if low >= high or name == "basis":
                        continue
                    columns = at - begin if step == 128 else 0
                    copy(
                        table.at[1, pl.ds(low - at, high - low), pl.ds(columns, 128)],
                        out.at[pl.ds(low - n * CHUNK, high - low)],
                    )
            if n == 3:
                copy(tables[6].at[1], turned)
                out[USED - n * CHUNK :, :] = jnp.zeros((PACK - USED, 128), BF)
            for c in copies:
                c.wait()
            if n == 3:
                for i in range(5):
                    at = BASIS - n * CHUNK + 128 * i
                    out[at : at + 128, :] = turned[:, 128 * i : 128 * (i + 1)].T


def join_kernel(q0, q1, q2, q3, out):
    i1, _ = places()
    for bits, quarter in zip((0, *PEERS), (q0, q1, q2, q3)):
        begin = pl.multiple_of((i1 ^ bits) * CHUNK, CHUNK)
        out[pl.ds(begin, CHUNK), :] = quarter[...]


def first_kernel(label, lag, s0, s1, s2, s3, state_out, look_out, e, act, slope, theta):
    weights = Weights((s0.at[0], s1.at[0], s2, s3))
    labels = label[...]
    state = jnp.where(look_mask(labels), lag[...].astype(F32), 0.0)
    heads, fore = run_forward(state, labels, weights, e, act, slope, theta)
    state_out[...] = state - pick_look(heads, labels)
    look_out[...] = pick_reach(fore, labels)


def second_kernel(
    label, state_in, look_in, left, adjoint, s0, s1, s2, s3, rest, look, g_out, mine, theirs, e, act, slope, theta
):
    weights = Weights((s0.at[1], s1.at[1], s2, s3))
    labels = label[...]
    heads, fore = run_forward(state_in[...], labels, weights, e, act, slope, theta)
    rest[...] = state_in[...] - pick_look(heads, labels)
    look[...] = look_in[...] + pick_reach(fore, labels)
    grads = Grads((mine, theirs))
    g = left[...].astype(F32)
    fore_wide = widen_reach(adjoint[...].astype(F32), labels)
    d_pre = backward_heads(g, fore_wide, labels, weights, act, slope, theta, grads)
    g_out[...] = backward_layers(g, d_pre, labels, weights, e, act, slope, grads)


def third_kernel(label, g_in, adjoint, s0, s1, s2, s3, act, slope, theta, d_out, mine, theirs):
    grads = Grads((mine, theirs), FOURTH)
    labels = label[...]
    fore_wide = widen_reach(adjoint[...].astype(F32), labels)
    d_out[...] = backward_heads(
        g_in[...], fore_wide, labels, Weights((s0.at[0], s1.at[0], s2, s3)), act, slope, theta, grads
    )


def fourth_kernel(label, g_in, d_in, s0, s1, s2, s3, e, act, slope, steep, mine, near, far):
    grads = Grads((mine, (near, far)))
    labels = label[...]
    g = backward_layers(g_in[...], d_in[...], labels, Weights((s0.at[0], s1.at[0], s2, s3)), e, act, slope, grads)
    steep[...] = jnp.where(look_mask(labels), g, 0.0)


def cut_kernel(mine, got, *outs):
    i1, _ = places()
    for bits, out in zip((*PEERS, 0), outs):
        rows = pl.ds(pl.multiple_of((i1 ^ bits) * CHUNK, CHUNK), CHUNK)
        out[...] = (mine[:, rows, :].astype(F32) + got[:, rows, :].astype(F32)).astype(BF)


def fold_heads_kernel(mine, got, near, rest, far):
    sums = (mine[...].astype(F32) + got[...].astype(F32)).astype(BF)
    near[...] = sums[0]
    rest[...] = sums[1, : EARLY - FOURTH]
    far[...] = sums[1, EARLY - FOURTH :]


def cut_one_kernel(mine, got0, got1, near, rest, came, *refs):
    outs, early, late = refs[:4], refs[4], refs[5]
    i1, _ = places()
    for half, got in enumerate((got0, got1)):
        early[half, :LOW] = (mine[half].astype(F32) + got[...].astype(F32)).astype(BF)
    early[0, LOW:EARLY] = near[: EARLY - LOW, :]
    early[1, LOW:EARLY] = rest[...]
    early[:, EARLY:] = jnp.zeros((2, EARLY_PACK - EARLY, 128), BF)
    late[...] = (near[EARLY - LOW :, :].astype(F32) + came[...].astype(F32)).astype(BF)
    for bits, out in zip((*PEERS, 0), outs):
        begin = pl.multiple_of((i1 ^ bits) * EARLY_CHUNK, EARLY_CHUNK)
        for half in range(2):
            out[half * EARLY_CHUNK : (half + 1) * EARLY_CHUNK, :] = early[half, pl.ds(begin, EARLY_CHUNK), :]
        begin = pl.multiple_of((i1 ^ bits) * LATE_CHUNK, LATE_CHUNK)
        out[2 * EARLY_CHUNK :, :] = late[pl.ds(begin, LATE_CHUNK), :]


def total(refs):
    a, b, c, d = (ref[...].astype(F32) for ref in refs)
    return ((a + b) + (c + d)).astype(BF)


def fold_kernel(own, a, b, c, near, far):
    near[...], far[...] = total((own, a, b, c))


def piece_kernel(own, a, b, c, near, came, *refs):
    outs, one, two = refs[:4], refs[4], refs[5]
    _, i2 = places()
    one[...] = total((own, a, b, c))
    two[...] = (near[...].astype(F32) + came[...].astype(F32)).astype(BF)
    for bits, out in zip((*SECOND_STEP, 0), outs):
        at = 0
        for ref, base, count in (
            (one, 0, EARLY_PIECE),
            (one, 2 * EARLY_CHUNK, LATE_PIECE),
            (two, 0, PIECE),
            (one, EARLY_CHUNK, EARLY_PIECE),
        ):
            begin = pl.multiple_of(base + (i2 ^ bits) * count, 16)
            out[at : at + count, :] = ref[pl.ds(begin, count), :]
            at += count


def sum_kernel(own, a, b, c, near, far):
    sums = total((own, a, b, c))
    near[0] = sums[:PIECE]
    near[1] = sums[PIECE : 2 * PIECE]
    far[...] = sums[2 * PIECE :]


def across_kernel(near, a, b, c, out):
    both = near[...].astype(F32) + a[...].astype(F32)
    add = b[...].astype(F32) + c[...].astype(F32)
    out[0, :EARLY_PIECE] = (both[0, :EARLY_PIECE] + add).astype(BF)
    out[0, EARLY_PIECE:] = both[0, EARLY_PIECE:].astype(BF)
    out[1] = both[1].astype(BF)


def stack_kernel(*refs):
    for k in range(2):
        for n in range(4):
            refs[4 + k][n] = refs[n][k]
    refs[6][...] = refs[3][0, :16]


def unpack_kernel(k, *refs):
    stacks, outs, whole, bufs, sem = refs[:4], refs[-16:-9], refs[-9], refs[-8:-1], refs[-1]
    i1, i2 = places()
    parts = ((0, EARLY_CHUNK, EARLY_PIECE), (EARLY_PACK, LATE_CHUNK, LATE_PIECE)) if k == 0 else ((0, CHUNK, PIECE),)
    for a, stack in zip((0, *FAR_FIRST), stacks):
        for slot, b in enumerate((0, *FAR_FIRST)):
            row = 0
            for base, chunk, piece in parts:
                at = pl.multiple_of(base + (i1 ^ a) * chunk + (i2 ^ b) * piece, 16)
                whole[pl.ds(at, piece), :] = stack[slot, row : row + piece, :]
                row += piece

    def rows(begin, count):
        if k == 0 and begin >= EARLY:
            begin += EARLY_PACK - EARLY
        return whole[begin : begin + count, :].astype(F32) * scale

    scale = 1.0 / math.sqrt(98304)
    copies = []
    for (name, (begin, count)), out, buf in zip(TABLES.items(), outs, bufs):
        if buf.shape[1] == 128:
            buf[...] = rows(begin, count)
        else:
            for i in range(count // 128):
                part = rows(begin + 128 * i, 128)
                buf[:, 128 * i : 128 * (i + 1)] = part.T if name == "basis" else part
        copies.append(pltpu.make_async_copy(buf, out.at[k], sem.at[len(copies)]))
        copies[-1].start()
    for copy in copies:
        copy.wait()


def shape(*dims, kind=F32):
    return jax.ShapeDtypeStruct(dims, kind)


def vmem(*dims, kind=BF):
    return pltpu.VMEM(dims, kind)


M1, M2, M3, M4, M5 = 12, 20, 12, 12, 8
DMA = pltpu.SemaphoreType.DMA
IN_VMEM = pl.BlockSpec(memory_space=pltpu.VMEM)
ANYWHERE = pl.BlockSpec(memory_space=pl.ANY)


def call(kernel, name, ins, outs, scratch, mib, us, aliases={}):
    return pl.pallas_call(
        kernel,
        out_shape=[o[0] for o in outs],
        in_specs=ins,
        out_specs=[o[1] for o in outs],
        scratch_shapes=scratch,
        compiler_params=pltpu.CompilerParams(vmem_limit_bytes=mib * 1024 * 1024),
        cost_estimate=pl.CostEstimate(
            flops=int(us * 8e8), bytes_accessed=int(us * 1e6), transcendentals=0
        ),
        name=name,
        input_output_aliases=aliases,
    )


ACTS = (4, 512, ROWS)
KEPT = [(560, ROWS), ACTS, ACTS, (2, 512, ROWS)]
TOP, LOW = USED - FOURTH, FOURTH


def plus(*parts):
    return sum(part.astype(F32) for part in parts).astype(BF)


def shards(lag, label, entry, second, third, fourth, back, fore, basis, adjoint, left):
    label = label[None, :]
    lag, adjoint, left = lag.T, adjoint.T, left.T
    whole, part = shape(PACK, 128, kind=BF), shape(CHUNK, 128, kind=BF)
    tables = (entry, second, third, fourth, back, fore, basis)
    quarter = call(
        quarter_kernel,
        "pack_quarter",
        [ANYWHERE] * 7,
        [(part, IN_VMEM)],
        [vmem(128, 640), DMA((8,))],
        60,
        1,
    )(*tables)[0]
    quarter, *tables = lax.optimization_barrier((quarter, *tables))
    both, one = call(
        pack_kernel,
        "pack",
        [IN_VMEM] * 7,
        [(shape(2, PACK, 128, kind=BF), IN_VMEM), (whole, IN_VMEM)],
        [],
        60,
        3,
    )(*tables)
    quarter = send(quarter, to_x_by_core())
    one, quarter = lax.optimization_barrier((one, quarter))
    across = send(one, to_x_by_core())
    quarters = [quarter] + [send(quarter, to_first(a)) for a in PEERS]
    other = send(both, to_core())
    across, *quarters = lax.optimization_barrier((across, *quarters))
    slots1 = (both, other, across, send(across, to_core()))
    across = call(join_kernel, "join", [IN_VMEM] * 4, [(whole, IN_VMEM)], [], M5, 1)(*quarters)[0]
    slots2 = (both, other, across, send(across, to_core()))
    state1, look1, e1, act1, slope1, theta1 = call(
        first_kernel,
        "forward_one",
        [IN_VMEM] * 6,
        [(shape(336, ROWS), IN_VMEM), (shape(48, ROWS), IN_VMEM)]
        + [(shape(*k, kind=BF), IN_VMEM) for k in KEPT],
        [],
        M1,
        6,
    )(label, lag, *slots1)
    rest, look, g1, mine2, theirs2 = call(
        second_kernel,
        "block_two",
        [IN_VMEM] * 9,
        [(shape(336, ROWS), IN_VMEM), (shape(48, ROWS), IN_VMEM), (shape(336, ROWS), IN_VMEM)]
        + [(shape(2, PACK, 128, kind=BF), IN_VMEM)] * 2,
        [vmem(*k) for k in KEPT],
        M2,
        14,
    )(label, state1, look1, left, adjoint, *slots2)
    got2 = send(theirs2, to_core())
    d_pre, mine1a, theirs1a = call(
        third_kernel,
        "backward_one_heads",
        [IN_VMEM] * 10,
        [(shape(512, ROWS, kind=BF), IN_VMEM)] + [(shape(2, TOP, 128, kind=BF), IN_VMEM)] * 2,
        [],
        M3,
        6,
    )(label, g1, adjoint, *slots1, act1, slope1, theta1)
    got1a = send(theirs1a, to_core())

    def small(kernel, name, outs, *args, scratch=()):
        return call(
            kernel,
            name,
            [IN_VMEM] * len(args),
            [(shape(*dims, 128, kind=BF), IN_VMEM) for dims in outs],
            scratch,
            M5,
            1,
        )(*args)

    *out2, own2 = small(cut_kernel, "cut_two", [(2, CHUNK)] * 4, mine2, got2)
    got2 = [send(part, to_first(a)) for part, a in zip(out2, PEERS)]
    near1, rest1, far1 = small(
        fold_heads_kernel, "fold_heads", [(TOP,), (EARLY - FOURTH,), (LATE,)], mine1a, got1a
    )
    d_pre, far1, *out2 = lax.optimization_barrier((d_pre, far1, *out2))
    came1 = send(far1, to_x_by_core())
    steep, mine1b, *theirs1b = call(
        fourth_kernel,
        "backward_one_layers",
        [IN_VMEM] * 10,
        [(shape(336, ROWS), IN_VMEM), (shape(2, LOW, 128, kind=BF), IN_VMEM)]
        + [(shape(LOW, 128, kind=BF), IN_VMEM)] * 2,
        [],
        M4,
        6,
    )(label, g1, d_pre, *slots1, e1, act1, slope1)
    got1b = [send(part, to_core()) for part in theirs1b]
    mine1b, got2[2] = lax.optimization_barrier((mine1b, got2[2]))
    *out1, own1 = small(
        cut_one_kernel,
        "cut_one",
        [(2 * EARLY_CHUNK + LATE_CHUNK,)] * 4,
        mine1b,
        *got1b,
        near1,
        rest1,
        came1,
        scratch=[vmem(2, EARLY_PACK, 128), vmem(LATE, 128)],
    )
    got1 = [send(part, to_first(a)) for part, a in zip(out1, PEERS)]

    near2, far2 = small(fold_kernel, "fold", [(CHUNK,)] * 2, own2, *got2)
    *out, own = small(
        piece_kernel,
        "pieces",
        [(2 * PIECE + EARLY_PIECE,)] * 4,
        own1,
        *got1,
        near2,
        send(far2, to_x_by_core()),
        scratch=[vmem(2 * EARLY_CHUNK + LATE_CHUNK, 128), vmem(CHUNK, 128)],
    )
    got = [send(part, to_second(b)) for part, b in zip(out, SECOND_STEP)]
    near, far = small(sum_kernel, "sums", [(2, PIECE), (EARLY_PIECE,)], own, *got)
    x1, x3 = send(far, to_x(1)), send(far, to_x(3))
    got = [send(near, to_x(2)), x3, x1]
    done = small(across_kernel, "across", [(2, PIECE)], near, *got)[0]
    got = [send(done, to_second(b)) for b in FAR_FIRST]
    *stack, here = small(stack_kernel, "stack", [(4, PIECE)] * 2 + [(16,)], done, *got)
    *stack, here = lax.optimization_barrier((*stack, send(here, to_core())))
    grads = ()
    for k in (1, 0):
        stacks = [stack[k]] + [send(stack[k], to_first(a)) for a in FAR_FIRST]
        outs = (
            (560, 128), (128, 512), (512, 128), (128, 512), (512, 128), (512, 128), (128, 640),
        )
        grads = call(
            functools.partial(unpack_kernel, k),
            "unpack",
            [IN_VMEM] * 4 + [ANYWHERE] * (len(grads) + 1),
            [(shape(2, *dims), ANYWHERE) for dims in outs],
            [vmem(PACK, 128)] + [vmem(*dims, kind=F32) for dims in outs] + [DMA((7,))],
            16,
            2,
            {4 + n: n for n in range(len(grads))},
        )(*stacks, *grads, here)
    return (look.T, rest.T, steep.T, *grads)


def solution(mesh):
    windows = P(("dp", "mp"), None)
    columns, rows = P(None, None, "mp"), P(None, "mp", None)
    tables = (columns, rows, columns, rows, columns, columns, rows)
    return jax.shard_map(
        shards,
        mesh=mesh,
        in_specs=(windows, P(("dp", "mp")), *tables, windows, windows),
        out_specs=(windows, windows, windows, *tables),
        check_vma=False,
    )
```

```python
import functools
import math

import jax
import jax.numpy as jnp
from jax import lax
from jax.experimental import pallas as pl
from jax.experimental.pallas import tpu as pltpu
from jax.sharding import PartitionSpec as P

BF = jnp.bfloat16
F32 = jnp.float32
ROWS = 768
ENTRY, SECOND, THIRD, FOURTH, BACK, FORE, BASIS, USED = 0, 560, 1072, 1584, 2096, 2608, 3120, 3760
PACK = 3840
PEERS = (1, 3, 2)
SECOND_STEP = (2, 3, 1)
EARLY, EARLY_PACK, LATE = 1712, 1792, 2048
EARLY_CHUNK, LATE_CHUNK = EARLY_PACK // 4, LATE // 4
EARLY_PIECE, LATE_PIECE = EARLY_PACK // 16, LATE // 16
FAR_FIRST = (1, 3, 2)
CHUNK, PIECE = PACK // 4, PACK // 16


def place(y, x, z, c):
    y, x, z, c = y % 4, x % 4, z % 4, c % 2
    return ((((y * 2 + x // 2) * 4 + z) * 2) + x % 2) * 2 + c


def pairs(move):
    out = []
    for y in range(4):
        for x in range(4):
            for z in range(4):
                for c in range(2):
                    out.append((place(y, x, z, c), place(*move(y, x, z, c))))
    return tuple(out)


def to_core():
    return pairs(lambda y, x, z, c: (y, x, z, 1 - c))


def to_x(bits):
    return pairs(lambda y, x, z, c: (y, x ^ bits, z, c))


def to_x_by_core():
    return pairs(lambda y, x, z, c: (y, x ^ (1 if c == 0 else 3), z, c))


def to_first(bits):
    return pairs(lambda y, x, z, c: (y ^ bits, x, z, c) if c == 0 else (y, x, z ^ bits, c))


def to_second(bits):
    return pairs(lambda y, x, z, c: (y, x, z ^ bits, c) if c == 0 else (y ^ bits, x, z, c))


def send(values, where):
    return lax.ppermute(values, ("dp", "mp"), where)


def row_of(count, begin=0):
    return lax.broadcasted_iota(jnp.int32, (count, ROWS), 0) + begin


def turn(values, shift):
    return pltpu.roll(values, shift % values.shape[0], 0)


def widen_look(v, label):
    zero = jnp.float32(0)
    e = [label == g for g in range(4)]
    near = turn(v[:56], 2)
    far = turn(v[:128], 2)
    top = row_of(56) < 2
    tip = row_of(8) < 2
    mid = jnp.where(
        top, jnp.where(e[0], v[40:96], zero), jnp.where(e[1], near, zero)
    )
    joint = jnp.where(
        tip, jnp.where(e[1], near[:8], zero), jnp.where(e[2], far[:8], zero)
    )
    return jnp.concatenate(
        [
            jnp.where(e[0], v[:40], zero),
            mid,
            joint,
            jnp.where(e[2], far[8:], zero),
            jnp.where(e[3], v, zero),
        ],
        axis=0,
    )


def pick_look(u, label):
    zero = jnp.float32(0)
    e = [label == g for g in range(4)]
    last = jnp.where(e[3], u[224:560], zero)
    near = turn(u[40:104], -2)
    far = turn(u[96:224], -2)
    row = row_of(56)
    begin = jnp.where(
        e[2],
        far[:56],
        jnp.where(e[1], near[:56], jnp.where(e[0] & (row < 42), u[:56], last[:56])),
    )
    middle = jnp.where(e[2] & (row_of(72, 56) < 126), far[56:], last[56:128])
    return jnp.concatenate([begin, middle, last[128:]], axis=0)


def widen_reach(a, label):
    zero = jnp.float32(0)
    e = [label == g for g in range(4)]
    one = turn(a[:16], 6)
    two = turn(a[:24], 6)
    row = row_of(8)
    return jnp.concatenate(
        [
            jnp.where(row < 6, jnp.where(e[0], a[:8], zero), jnp.where(e[1], one[:8], zero)),
            jnp.where(row < 6, jnp.where(e[1], one[8:], zero), jnp.where(e[2], two[:8], zero)),
            jnp.where(e[2], two[8:], zero),
            jnp.where(e[3], a, zero),
        ],
        axis=0,
    )


def pick_reach(u, label):
    zero = jnp.float32(0)
    e = [label == g for g in range(4)]
    last = jnp.where(e[3], u[32:], zero)
    one = turn(u[:16], -6)
    two = turn(u[8:32], -6)
    row = row_of(8)
    return jnp.concatenate(
        [
            jnp.where(
                e[2],
                two[:8],
                jnp.where(e[1], one[:8], jnp.where(e[0] & (row < 6), u[:8], last[:8])),
            ),
            jnp.where(e[2] & (row_of(16, 8) < 18), two[8:], last[8:24]),
            last[24:],
        ],
        axis=0,
    )


def look_mask(label):
    reach = jnp.where(label == 0, 42, jnp.where(label == 1, 56, jnp.where(label == 2, 126, 336)))
    return row_of(336) < reach


def by_columns(slots, begin, count):
    return jnp.concatenate([slot[begin : begin + count, :] for slot in slots], axis=1)


def by_rows(slots, begin, count):
    return jnp.concatenate(
        [
            jnp.concatenate(
                [slot[begin + 128 * i : begin + 128 * (i + 1), :] for i in range(count)], axis=1
            )
            for slot in slots
        ],
        axis=0,
    )


def dot(a, b):
    return jnp.dot(a, b, preferred_element_type=F32)


def dot_t(a, b):
    return lax.dot_general(a, b, (((1,), (1,)), ((), ())), preferred_element_type=F32)


def t_dot(a, b):
    return lax.dot_general(a, b, (((0,), (0,)), ((), ())), preferred_element_type=F32)


def silu_both(pre):
    s = jax.nn.sigmoid(pre)
    act = pre * s
    return act.astype(BF), (s + act * (1.0 - s)).astype(BF)


TABLES = {
    "entry": (ENTRY, 560),
    "second": (SECOND, 512),
    "third": (THIRD, 512),
    "fourth": (FOURTH, 512),
    "back": (BACK, 512),
    "fore": (FORE, 512),
    "basis": (BASIS, 640),
}


class Weights:
    def __init__(self, slots):
        self.slots = slots

    def get(self, name):
        begin, count = TABLES[name]
        if name in ("second", "fourth"):
            return by_rows(self.slots, begin, 4)
        return by_columns(self.slots, begin, count)


def run_forward(state, label, weights, e_ref, act_ref, slope_ref, theta_ref):
    e_ref[...] = widen_look(state, label).astype(BF)
    act, slope = silu_both(t_dot(weights.get("entry"), e_ref[...]))
    act_ref[0], slope_ref[0] = act, slope
    for i, name in enumerate(("second", "third", "fourth")):
        act, slope = silu_both(t_dot(weights.get(name), act_ref[i]))
        act_ref[i + 1], slope_ref[i + 1] = act, slope
    theta_ref[0] = t_dot(weights.get("back"), act_ref[3]).astype(BF)
    theta_ref[1] = t_dot(weights.get("fore"), act_ref[3]).astype(BF)
    basis = weights.get("basis")
    return dot(basis[:560], theta_ref[0]), dot(basis[560:], theta_ref[1])


class Grads:
    def __init__(self, outs, base=0):
        self.outs, self.base = outs, base

    def put(self, name, grad):
        begin, count = TABLES[name]
        at = begin - self.base
        for slot in range(4):
            out = self.outs[slot % 2]
            out = out[slot // 2] if isinstance(out, tuple) else out.at[slot // 2]
            if name in ("second", "fourth"):
                for i in range(4):
                    out[at + 128 * i : at + 128 * (i + 1), :] = grad[
                        128 * slot : 128 * (slot + 1), 128 * i : 128 * (i + 1)
                    ].astype(BF)
            else:
                out[at : at + count, :] = grad[:, 128 * slot : 128 * (slot + 1)].astype(BF)
        if name == "basis" and not self.base:
            for out in self.outs:
                out[:, USED:PACK, :] = jnp.zeros((2, PACK - USED, 128), BF)


def backward_heads(g, fore_wide, label, weights, act_ref, slope_ref, theta_ref, grads):
    d_back = -widen_look(g, label).astype(BF)
    d_fore = fore_wide.astype(BF)
    basis = weights.get("basis")
    d_theta_b = t_dot(basis[:560], d_back).astype(BF)
    d_theta_f = t_dot(basis[560:], d_fore).astype(BF)
    grads.put(
        "basis",
        jnp.concatenate([dot_t(d_back, theta_ref[0]), dot_t(d_fore, theta_ref[1])], axis=0),
    )
    d_act = dot(weights.get("back"), d_theta_b) + dot(weights.get("fore"), d_theta_f)
    grads.put("back", dot_t(act_ref[3], d_theta_b))
    grads.put("fore", dot_t(act_ref[3], d_theta_f))
    d_pre = (d_act * slope_ref[3].astype(F32)).astype(BF)
    grads.put("fourth", dot_t(act_ref[2], d_pre))
    return d_pre


def backward_layers(g, d_pre, label, weights, e_ref, act_ref, slope_ref, grads):
    d_act = dot(weights.get("fourth"), d_pre)
    d_pre = (d_act * slope_ref[2].astype(F32)).astype(BF)
    grads.put("third", dot_t(act_ref[1], d_pre))
    d_act = dot(weights.get("third"), d_pre)
    d_pre = (d_act * slope_ref[1].astype(F32)).astype(BF)
    grads.put("second", dot_t(act_ref[0], d_pre))
    d_act = dot(weights.get("second"), d_pre)
    d_pre = (d_act * slope_ref[0].astype(F32)).astype(BF)
    grads.put("entry", dot_t(e_ref[...], d_pre))
    return g + pick_look(dot(weights.get("entry"), d_pre), label)


def places():
    dp, core = lax.axis_index("dp"), lax.rem(lax.axis_index("mp"), 2)
    y, z = lax.div(dp, 8), lax.rem(dp, 4)
    return jnp.where(core == 0, y, z), jnp.where(core == 0, z, y)


def pack_kernel(*refs):
    tables, both, one = refs[:7], refs[7], refs[8]
    for k in range(2):
        for (name, (begin, count)), table in zip(TABLES.items(), tables):
            if table.shape[2] == 128:
                both[k, begin : begin + count, :] = table[k]
                continue
            for i in range(count // 128):
                block = table[k, :, 128 * i : 128 * (i + 1)]
                both[k, begin + 128 * i : begin + 128 * (i + 1), :] = block.T if name == "basis" else block
        both[k, USED:PACK, :] = jnp.zeros((PACK - USED, 128), BF)
    one[...] = both[0]


def quarter_kernel(*refs):
    tables, out, turned, sem = refs[:7], refs[7], refs[8], refs[9]
    i1, _ = places()
    for n in range(4):

        @pl.when(i1 == n)
        def _():
            copies = []

            def copy(source, target):
                copies.append(pltpu.make_async_copy(source, target, sem.at[len(copies)]))
                copies[-1].start()

            for (name, (begin, count)), table in zip(TABLES.items(), tables):
                step = 128 if table.shape[2] > 128 else count
                for at in range(begin, begin + count, step):
                    low, high = max(at, n * CHUNK), min(at + step, (n + 1) * CHUNK)
                    if low >= high or name == "basis":
                        continue
                    columns = at - begin if step == 128 else 0
                    copy(
                        table.at[1, pl.ds(low - at, high - low), pl.ds(columns, 128)],
                        out.at[pl.ds(low - n * CHUNK, high - low)],
                    )
            if n == 3:
                copy(tables[6].at[1], turned)
                out[USED - n * CHUNK :, :] = jnp.zeros((PACK - USED, 128), BF)
            for c in copies:
                c.wait()
            if n == 3:
                for i in range(5):
                    at = BASIS - n * CHUNK + 128 * i
                    out[at : at + 128, :] = turned[:, 128 * i : 128 * (i + 1)].T


def join_kernel(q0, q1, q2, q3, out):
    i1, _ = places()
    for bits, quarter in zip((0, *PEERS), (q0, q1, q2, q3)):
        begin = pl.multiple_of((i1 ^ bits) * CHUNK, CHUNK)
        out[pl.ds(begin, CHUNK), :] = quarter[...]


def first_kernel(label, lag, s0, s1, s2, s3, state_out, look_out, e, act, slope, theta):
    weights = Weights((s0.at[0], s1.at[0], s2, s3))
    labels = label[...]
    state = jnp.where(look_mask(labels), lag[...].astype(F32), 0.0)
    heads, fore = run_forward(state, labels, weights, e, act, slope, theta)
    state_out[...] = state - pick_look(heads, labels)
    look_out[...] = pick_reach(fore, labels)


def second_kernel(
    label, state_in, look_in, left, adjoint, s0, s1, s2, s3, rest, look, g_out, mine, theirs, e, act, slope, theta
):
    weights = Weights((s0.at[1], s1.at[1], s2, s3))
    labels = label[...]
    heads, fore = run_forward(state_in[...], labels, weights, e, act, slope, theta)
    rest[...] = state_in[...] - pick_look(heads, labels)
    look[...] = look_in[...] + pick_reach(fore, labels)
    grads = Grads((mine, theirs))
    g = left[...].astype(F32)
    fore_wide = widen_reach(adjoint[...].astype(F32), labels)
    d_pre = backward_heads(g, fore_wide, labels, weights, act, slope, theta, grads)
    g_out[...] = backward_layers(g, d_pre, labels, weights, e, act, slope, grads)


def third_kernel(label, g_in, adjoint, s0, s1, s2, s3, act, slope, theta, d_out, mine, theirs):
    grads = Grads((mine, theirs), FOURTH)
    labels = label[...]
    fore_wide = widen_reach(adjoint[...].astype(F32), labels)
    d_out[...] = backward_heads(
        g_in[...], fore_wide, labels, Weights((s0.at[0], s1.at[0], s2, s3)), act, slope, theta, grads
    )


def fourth_kernel(label, g_in, d_in, s0, s1, s2, s3, e, act, slope, steep, mine, near, far):
    grads = Grads((mine, (near, far)))
    labels = label[...]
    g = backward_layers(g_in[...], d_in[...], labels, Weights((s0.at[0], s1.at[0], s2, s3)), e, act, slope, grads)
    steep[...] = jnp.where(look_mask(labels), g, 0.0)


def cut_kernel(mine, got, *outs):
    i1, _ = places()
    for bits, out in zip((*PEERS, 0), outs):
        rows = pl.ds(pl.multiple_of((i1 ^ bits) * CHUNK, CHUNK), CHUNK)
        out[...] = (mine[:, rows, :].astype(F32) + got[:, rows, :].astype(F32)).astype(BF)


def fold_heads_kernel(mine, got, near, rest, far):
    sums = (mine[...].astype(F32) + got[...].astype(F32)).astype(BF)
    near[...] = sums[0]
    rest[...] = sums[1, : EARLY - FOURTH]
    far[...] = sums[1, EARLY - FOURTH :]


def cut_one_kernel(mine, got0, got1, near, rest, came, *refs):
    outs, early, late = refs[:4], refs[4], refs[5]
    i1, _ = places()
    for half, got in enumerate((got0, got1)):
        early[half, :LOW] = (mine[half].astype(F32) + got[...].astype(F32)).astype(BF)
    early[0, LOW:EARLY] = near[: EARLY - LOW, :]
    early[1, LOW:EARLY] = rest[...]
    early[:, EARLY:] = jnp.zeros((2, EARLY_PACK - EARLY, 128), BF)
    late[...] = (near[EARLY - LOW :, :].astype(F32) + came[...].astype(F32)).astype(BF)
    for bits, out in zip((*PEERS, 0), outs):
        begin = pl.multiple_of((i1 ^ bits) * EARLY_CHUNK, EARLY_CHUNK)
        for half in range(2):
            out[half * EARLY_CHUNK : (half + 1) * EARLY_CHUNK, :] = early[half, pl.ds(begin, EARLY_CHUNK), :]
        begin = pl.multiple_of((i1 ^ bits) * LATE_CHUNK, LATE_CHUNK)
        out[2 * EARLY_CHUNK :, :] = late[pl.ds(begin, LATE_CHUNK), :]


def total(refs):
    a, b, c, d = (ref[...].astype(F32) for ref in refs)
    return ((a + b) + (c + d)).astype(BF)


def fold_kernel(own, a, b, c, near, far):
    near[...], far[...] = total((own, a, b, c))


def piece_kernel(own, a, b, c, near, came, *refs):
    outs, one, two = refs[:4], refs[4], refs[5]
    _, i2 = places()
    one[...] = total((own, a, b, c))
    two[...] = (near[...].astype(F32) + came[...].astype(F32)).astype(BF)
    for bits, out in zip((*SECOND_STEP, 0), outs):
        at = 0
        for ref, base, count in (
            (one, 0, EARLY_PIECE),
            (one, 2 * EARLY_CHUNK, LATE_PIECE),
            (two, 0, PIECE),
            (one, EARLY_CHUNK, EARLY_PIECE),
        ):
            begin = pl.multiple_of(base + (i2 ^ bits) * count, 16)
            out[at : at + count, :] = ref[pl.ds(begin, count), :]
            at += count


def sum_kernel(own, a, b, c, near, far):
    sums = total((own, a, b, c))
    near[0] = sums[:PIECE]
    near[1] = sums[PIECE : 2 * PIECE]
    far[...] = sums[2 * PIECE :]


def across_kernel(near, a, b, c, out):
    both = near[...].astype(F32) + a[...].astype(F32)
    add = b[...].astype(F32) + c[...].astype(F32)
    out[0, :EARLY_PIECE] = (both[0, :EARLY_PIECE] + add).astype(BF)
    out[0, EARLY_PIECE:] = both[0, EARLY_PIECE:].astype(BF)
    out[1] = both[1].astype(BF)


def stack_kernel(*refs):
    for k in range(2):
        for n in range(4):
            refs[4 + k][n] = refs[n][k]
    refs[6][...] = refs[3][0, :16]


def unpack_kernel(k, *refs):
    stacks, outs, whole, bufs, sem = refs[:4], refs[-16:-9], refs[-9], refs[-8:-1], refs[-1]
    i1, i2 = places()
    parts = ((0, EARLY_CHUNK, EARLY_PIECE), (EARLY_PACK, LATE_CHUNK, LATE_PIECE)) if k == 0 else ((0, CHUNK, PIECE),)
    for a, stack in zip((0, *FAR_FIRST), stacks):
        for slot, b in enumerate((0, *FAR_FIRST)):
            row = 0
            for base, chunk, piece in parts:
                at = pl.multiple_of(base + (i1 ^ a) * chunk + (i2 ^ b) * piece, 16)
                whole[pl.ds(at, piece), :] = stack[slot, row : row + piece, :]
                row += piece

    def rows(begin, count):
        if k == 0 and begin >= EARLY:
            begin += EARLY_PACK - EARLY
        return whole[begin : begin + count, :].astype(F32) * scale

    scale = 1.0 / math.sqrt(98304)
    copies = []
    for (name, (begin, count)), out, buf in zip(TABLES.items(), outs, bufs):
        if buf.shape[1] == 128:
            buf[...] = rows(begin, count)
        else:
            for i in range(count // 128):
                part = rows(begin + 128 * i, 128)
                buf[:, 128 * i : 128 * (i + 1)] = part.T if name == "basis" else part
        copies.append(pltpu.make_async_copy(buf, out.at[k], sem.at[len(copies)]))
        copies[-1].start()
    for copy in copies:
        copy.wait()


def shape(*dims, kind=F32):
    return jax.ShapeDtypeStruct(dims, kind)


def vmem(*dims, kind=BF):
    return pltpu.VMEM(dims, kind)


M1, M2, M3, M4, M5 = 12, 20, 12, 12, 8
DMA = pltpu.SemaphoreType.DMA
IN_VMEM = pl.BlockSpec(memory_space=pltpu.VMEM)
ANYWHERE = pl.BlockSpec(memory_space=pl.ANY)


def call(kernel, name, ins, outs, scratch, mib, us, aliases={}):
    return pl.pallas_call(
        kernel,
        out_shape=[o[0] for o in outs],
        in_specs=ins,
        out_specs=[o[1] for o in outs],
        scratch_shapes=scratch,
        compiler_params=pltpu.CompilerParams(vmem_limit_bytes=mib * 1024 * 1024),
        cost_estimate=pl.CostEstimate(
            flops=int(us * 8e8), bytes_accessed=int(us * 1e6), transcendentals=0
        ),
        name=name,
        input_output_aliases=aliases,
    )


ACTS = (4, 512, ROWS)
KEPT = [(560, ROWS), ACTS, ACTS, (2, 512, ROWS)]
TOP, LOW = USED - FOURTH, FOURTH


def plus(*parts):
    return sum(part.astype(F32) for part in parts).astype(BF)


def shards(lag, label, entry, second, third, fourth, back, fore, basis, adjoint, left):
    label = label[None, :]
    lag, adjoint, left = lag.T, adjoint.T, left.T
    whole, part = shape(PACK, 128, kind=BF), shape(CHUNK, 128, kind=BF)
    tables = (entry, second, third, fourth, back, fore, basis)
    quarter = call(
        quarter_kernel,
        "pack_quarter",
        [ANYWHERE] * 7,
        [(part, IN_VMEM)],
        [vmem(128, 640), DMA((8,))],
        60,
        1,
    )(*tables)[0]
    quarter, *tables = lax.optimization_barrier((quarter, *tables))
    both, one = call(
        pack_kernel,
        "pack",
        [IN_VMEM] * 7,
        [(shape(2, PACK, 128, kind=BF), IN_VMEM), (whole, IN_VMEM)],
        [],
        60,
        3,
    )(*tables)
    quarter = send(quarter, to_x_by_core())
    one, quarter = lax.optimization_barrier((one, quarter))
    across = send(one, to_x_by_core())
    quarters = [quarter] + [send(quarter, to_first(a)) for a in PEERS]
    other = send(both, to_core())
    across, *quarters = lax.optimization_barrier((across, *quarters))
    slots1 = (both, other, across, send(across, to_core()))
    across = call(join_kernel, "join", [IN_VMEM] * 4, [(whole, IN_VMEM)], [], M5, 1)(*quarters)[0]
    slots2 = (both, other, across, send(across, to_core()))
    state1, look1, e1, act1, slope1, theta1 = call(
        first_kernel,
        "forward_one",
        [IN_VMEM] * 6,
        [(shape(336, ROWS), IN_VMEM), (shape(48, ROWS), IN_VMEM)]
        + [(shape(*k, kind=BF), IN_VMEM) for k in KEPT],
        [],
        M1,
        6,
    )(label, lag, *slots1)
    rest, look, g1, mine2, theirs2 = call(
        second_kernel,
        "block_two",
        [IN_VMEM] * 9,
        [(shape(336, ROWS), IN_VMEM), (shape(48, ROWS), IN_VMEM), (shape(336, ROWS), IN_VMEM)]
        + [(shape(2, PACK, 128, kind=BF), IN_VMEM)] * 2,
        [vmem(*k) for k in KEPT],
        M2,
        14,
    )(label, state1, look1, left, adjoint, *slots2)
    got2 = send(theirs2, to_core())
    d_pre, mine1a, theirs1a = call(
        third_kernel,
        "backward_one_heads",
        [IN_VMEM] * 10,
        [(shape(512, ROWS, kind=BF), IN_VMEM)] + [(shape(2, TOP, 128, kind=BF), IN_VMEM)] * 2,
        [],
        M3,
        6,
    )(label, g1, adjoint, *slots1, act1, slope1, theta1)
    got1a = send(theirs1a, to_core())

    def small(kernel, name, outs, *args, scratch=()):
        return call(
            kernel,
            name,
            [IN_VMEM] * len(args),
            [(shape(*dims, 128, kind=BF), IN_VMEM) for dims in outs],
            scratch,
            M5,
            1,
        )(*args)

    *out2, own2 = small(cut_kernel, "cut_two", [(2, CHUNK)] * 4, mine2, got2)
    got2 = [send(part, to_first(a)) for part, a in zip(out2, PEERS)]
    near1, rest1, far1 = small(
        fold_heads_kernel, "fold_heads", [(TOP,), (EARLY - FOURTH,), (LATE,)], mine1a, got1a
    )
    d_pre, far1, *out2 = lax.optimization_barrier((d_pre, far1, *out2))
    came1 = send(far1, to_x_by_core())
    steep, mine1b, *theirs1b = call(
        fourth_kernel,
        "backward_one_layers",
        [IN_VMEM] * 10,
        [(shape(336, ROWS), IN_VMEM), (shape(2, LOW, 128, kind=BF), IN_VMEM)]
        + [(shape(LOW, 128, kind=BF), IN_VMEM)] * 2,
        [],
        M4,
        6,
    )(label, g1, d_pre, *slots1, e1, act1, slope1)
    got1b = [send(part, to_core()) for part in theirs1b]
    mine1b, got2[2] = lax.optimization_barrier((mine1b, got2[2]))
    *out1, own1 = small(
        cut_one_kernel,
        "cut_one",
        [(2 * EARLY_CHUNK + LATE_CHUNK,)] * 4,
        mine1b,
        *got1b,
        near1,
        rest1,
        came1,
        scratch=[vmem(2, EARLY_PACK, 128), vmem(LATE, 128)],
    )
    got1 = [send(part, to_first(a)) for part, a in zip(out1, PEERS)]

    near2, far2 = small(fold_kernel, "fold", [(CHUNK,)] * 2, own2, *got2)
    *out, own = small(
        piece_kernel,
        "pieces",
        [(2 * PIECE + EARLY_PIECE,)] * 4,
        own1,
        *got1,
        near2,
        send(far2, to_x_by_core()),
        scratch=[vmem(2 * EARLY_CHUNK + LATE_CHUNK, 128), vmem(CHUNK, 128)],
    )
    got = [send(part, to_second(b)) for part, b in zip(out, SECOND_STEP)]
    near, far = small(sum_kernel, "sums", [(2, PIECE), (EARLY_PIECE,)], own, *got)
    x1, x3 = send(far, to_x(1)), send(far, to_x(3))
    got = [send(near, to_x(2)), x3, x1]
    done = small(across_kernel, "across", [(2, PIECE)], near, *got)[0]
    got = [send(done, to_second(b)) for b in FAR_FIRST]
    *stack, here = small(stack_kernel, "stack", [(4, PIECE)] * 2 + [(16,)], done, *got)
    *stack, here = lax.optimization_barrier((*stack, send(here, to_core())))
    grads = ()
    for k in (1, 0):
        stacks = [stack[k]] + [send(stack[k], to_first(a)) for a in FAR_FIRST]
        outs = (
            (560, 128), (128, 512), (512, 128), (128, 512), (512, 128), (512, 128), (128, 640),
        )
        grads = call(
            functools.partial(unpack_kernel, k),
            "unpack",
            [IN_VMEM] * 4 + [ANYWHERE] * (len(grads) + 1),
            [(shape(2, *dims), ANYWHERE) for dims in outs],
            [vmem(PACK, 128)] + [vmem(*dims, kind=F32) for dims in outs] + [DMA((7,))],
            16,
            2,
            {4 + n: n for n in range(len(grads))},
        )(*stacks, *grads, here)
    return (look.T, rest.T, steep.T, *grads)


def solution(mesh):
    windows = P(("dp", "mp"), None)
    columns, rows = P(None, None, "mp"), P(None, "mp", None)
    tables = (columns, rows, columns, rows, columns, columns, rows)
    return jax.shard_map(
        shards,
        mesh=mesh,
        in_specs=(windows, P(("dp", "mp")), *tables, windows, windows),
        out_specs=(windows, windows, windows, *tables),
        check_vma=False,
    )
```

```python
import functools
import math

import jax
import jax.numpy as jnp
from jax import lax
from jax.experimental import pallas as pl
from jax.experimental.pallas import tpu as pltpu
from jax.sharding import PartitionSpec as P

BF = jnp.bfloat16
F32 = jnp.float32
ROWS = 768
ENTRY, SECOND, THIRD, FOURTH, BACK, FORE, BASIS, USED = 0, 560, 1072, 1584, 2096, 2608, 3120, 3760
PACK = 3840
PEERS = (1, 3, 2)
SECOND_STEP = (2, 3, 1)
EARLY, EARLY_PACK, LATE = 1712, 1792, 2048
EARLY_CHUNK, LATE_CHUNK = EARLY_PACK // 4, LATE // 4
EARLY_PIECE, LATE_PIECE = EARLY_PACK // 16, LATE // 16
FAR_FIRST = (1, 3, 2)
CHUNK, PIECE = PACK // 4, PACK // 16


def place(y, x, z, c):
    y, x, z, c = y % 4, x % 4, z % 4, c % 2
    return ((((y * 2 + x // 2) * 4 + z) * 2) + x % 2) * 2 + c


def pairs(move):
    out = []
    for y in range(4):
        for x in range(4):
            for z in range(4):
                for c in range(2):
                    out.append((place(y, x, z, c), place(*move(y, x, z, c))))
    return tuple(out)


def to_core():
    return pairs(lambda y, x, z, c: (y, x, z, 1 - c))


def to_x(bits):
    return pairs(lambda y, x, z, c: (y, x ^ bits, z, c))


def to_x_by_core():
    return pairs(lambda y, x, z, c: (y, x ^ (1 if c == 0 else 3), z, c))


def to_first(bits):
    return pairs(lambda y, x, z, c: (y ^ bits, x, z, c) if c == 0 else (y, x, z ^ bits, c))


def to_second(bits):
    return pairs(lambda y, x, z, c: (y, x, z ^ bits, c) if c == 0 else (y ^ bits, x, z, c))


def send(values, where):
    return lax.ppermute(values, ("dp", "mp"), where)


def row_of(count, begin=0):
    return lax.broadcasted_iota(jnp.int32, (count, ROWS), 0) + begin


def turn(values, shift):
    return pltpu.roll(values, shift % values.shape[0], 0)


def widen_look(v, label):
    zero = jnp.float32(0)
    e = [label == g for g in range(4)]
    near = turn(v[:56], 2)
    far = turn(v[:128], 2)
    top = row_of(56) < 2
    tip = row_of(8) < 2
    mid = jnp.where(
        top, jnp.where(e[0], v[40:96], zero), jnp.where(e[1], near, zero)
    )
    joint = jnp.where(
        tip, jnp.where(e[1], near[:8], zero), jnp.where(e[2], far[:8], zero)
    )
    return jnp.concatenate(
        [
            jnp.where(e[0], v[:40], zero),
            mid,
            joint,
            jnp.where(e[2], far[8:], zero),
            jnp.where(e[3], v, zero),
        ],
        axis=0,
    )


def pick_look(u, label):
    zero = jnp.float32(0)
    e = [label == g for g in range(4)]
    last = jnp.where(e[3], u[224:560], zero)
    near = turn(u[40:104], -2)
    far = turn(u[96:224], -2)
    row = row_of(56)
    begin = jnp.where(
        e[2],
        far[:56],
        jnp.where(e[1], near[:56], jnp.where(e[0] & (row < 42), u[:56], last[:56])),
    )
    middle = jnp.where(e[2] & (row_of(72, 56) < 126), far[56:], last[56:128])
    return jnp.concatenate([begin, middle, last[128:]], axis=0)


def widen_reach(a, label):
    zero = jnp.float32(0)
    e = [label == g for g in range(4)]
    one = turn(a[:16], 6)
    two = turn(a[:24], 6)
    row = row_of(8)
    return jnp.concatenate(
        [
            jnp.where(row < 6, jnp.where(e[0], a[:8], zero), jnp.where(e[1], one[:8], zero)),
            jnp.where(row < 6, jnp.where(e[1], one[8:], zero), jnp.where(e[2], two[:8], zero)),
            jnp.where(e[2], two[8:], zero),
            jnp.where(e[3], a, zero),
        ],
        axis=0,
    )


def pick_reach(u, label):
    zero = jnp.float32(0)
    e = [label == g for g in range(4)]
    last = jnp.where(e[3], u[32:], zero)
    one = turn(u[:16], -6)
    two = turn(u[8:32], -6)
    row = row_of(8)
    return jnp.concatenate(
        [
            jnp.where(
                e[2],
                two[:8],
                jnp.where(e[1], one[:8], jnp.where(e[0] & (row < 6), u[:8], last[:8])),
            ),
            jnp.where(e[2] & (row_of(16, 8) < 18), two[8:], last[8:24]),
            last[24:],
        ],
        axis=0,
    )


def look_mask(label):
    reach = jnp.where(label == 0, 42, jnp.where(label == 1, 56, jnp.where(label == 2, 126, 336)))
    return row_of(336) < reach


def by_columns(slots, begin, count):
    return jnp.concatenate([slot[begin : begin + count, :] for slot in slots], axis=1)


def by_rows(slots, begin, count):
    return jnp.concatenate(
        [
            jnp.concatenate(
                [slot[begin + 128 * i : begin + 128 * (i + 1), :] for i in range(count)], axis=1
            )
            for slot in slots
        ],
        axis=0,
    )


def dot(a, b):
    return jnp.dot(a, b, preferred_element_type=F32)


def dot_t(a, b):
    return lax.dot_general(a, b, (((1,), (1,)), ((), ())), preferred_element_type=F32)


def t_dot(a, b):
    return lax.dot_general(a, b, (((0,), (0,)), ((), ())), preferred_element_type=F32)


def silu_both(pre):
    s = jax.nn.sigmoid(pre)
    act = pre * s
    return act.astype(BF), (s + act * (1.0 - s)).astype(BF)


TABLES = {
    "entry": (ENTRY, 560),
    "second": (SECOND, 512),
    "third": (THIRD, 512),
    "fourth": (FOURTH, 512),
    "back": (BACK, 512),
    "fore": (FORE, 512),
    "basis": (BASIS, 640),
}


class Weights:
    def __init__(self, slots):
        self.slots = slots

    def get(self, name):
        begin, count = TABLES[name]
        if name in ("second", "fourth"):
            return by_rows(self.slots, begin, 4)
        return by_columns(self.slots, begin, count)


def run_forward(state, label, weights, e_ref, act_ref, slope_ref, theta_ref):
    e_ref[...] = widen_look(state, label).astype(BF)
    act, slope = silu_both(t_dot(weights.get("entry"), e_ref[...]))
    act_ref[0], slope_ref[0] = act, slope
    for i, name in enumerate(("second", "third", "fourth")):
        act, slope = silu_both(t_dot(weights.get(name), act_ref[i]))
        act_ref[i + 1], slope_ref[i + 1] = act, slope
    theta_ref[0] = t_dot(weights.get("back"), act_ref[3]).astype(BF)
    theta_ref[1] = t_dot(weights.get("fore"), act_ref[3]).astype(BF)
    basis = weights.get("basis")
    return dot(basis[:560], theta_ref[0]), dot(basis[560:], theta_ref[1])


class Grads:
    def __init__(self, outs, base=0):
        self.outs, self.base = outs, base

    def put(self, name, grad):
        begin, count = TABLES[name]
        at = begin - self.base
        for slot in range(4):
            out = self.outs[slot % 2]
            out = out[slot // 2] if isinstance(out, tuple) else out.at[slot // 2]
            if name in ("second", "fourth"):
                for i in range(4):
                    out[at + 128 * i : at + 128 * (i + 1), :] = grad[
                        128 * slot : 128 * (slot + 1), 128 * i : 128 * (i + 1)
                    ].astype(BF)
            else:
                out[at : at + count, :] = grad[:, 128 * slot : 128 * (slot + 1)].astype(BF)
        if name == "basis" and not self.base:
            for out in self.outs:
                out[:, USED:PACK, :] = jnp.zeros((2, PACK - USED, 128), BF)


def backward_heads(g, fore_wide, label, weights, act_ref, slope_ref, theta_ref, grads):
    d_back = -widen_look(g, label).astype(BF)
    d_fore = fore_wide.astype(BF)
    basis = weights.get("basis")
    d_theta_b = t_dot(basis[:560], d_back).astype(BF)
    d_theta_f = t_dot(basis[560:], d_fore).astype(BF)
    grads.put(
        "basis",
        jnp.concatenate([dot_t(d_back, theta_ref[0]), dot_t(d_fore, theta_ref[1])], axis=0),
    )
    d_act = dot(weights.get("back"), d_theta_b) + dot(weights.get("fore"), d_theta_f)
    grads.put("back", dot_t(act_ref[3], d_theta_b))
    grads.put("fore", dot_t(act_ref[3], d_theta_f))
    d_pre = (d_act * slope_ref[3].astype(F32)).astype(BF)
    grads.put("fourth", dot_t(act_ref[2], d_pre))
    return d_pre


def backward_layers(g, d_pre, label, weights, e_ref, act_ref, slope_ref, grads, take=None):
    d_act = dot(weights.get("fourth"), d_pre)
    d_pre = (d_act * slope_ref[2].astype(F32)).astype(BF)
    grads.put("third", dot_t(act_ref[1], d_pre))
    d_act = dot(weights.get("third"), d_pre)
    d_pre = (d_act * slope_ref[1].astype(F32)).astype(BF)
    grads.put("second", dot_t(act_ref[0], d_pre))
    d_act = dot(weights.get("second"), d_pre)
    d_pre = (d_act * slope_ref[0].astype(F32)).astype(BF)
    if take:
        take(g + pick_look(dot(weights.get("entry"), d_pre), label))
    grads.put("entry", dot_t(e_ref[...], d_pre))
    if not take:
        return g + pick_look(dot(weights.get("entry"), d_pre), label)


def places():
    dp, core = lax.axis_index("dp"), lax.rem(lax.axis_index("mp"), 2)
    y, z = lax.div(dp, 8), lax.rem(dp, 4)
    return jnp.where(core == 0, y, z), jnp.where(core == 0, z, y)


def pack_kernel(*refs):
    tables, both, one = refs[:7], refs[7], refs[8]
    for k in range(2):
        for (name, (begin, count)), table in zip(TABLES.items(), tables):
            if table.shape[2] == 128:
                both[k, begin : begin + count, :] = table[k]
                continue
            for i in range(count // 128):
                block = table[k, :, 128 * i : 128 * (i + 1)]
                both[k, begin + 128 * i : begin + 128 * (i + 1), :] = block.T if name == "basis" else block
        both[k, USED:PACK, :] = jnp.zeros((PACK - USED, 128), BF)
    one[...] = both[0]


def quarter_kernel(*refs):
    tables, out, turned, sem = refs[:7], refs[7], refs[8], refs[9]
    i1, _ = places()
    for n in range(4):

        @pl.when(i1 == n)
        def _():
            copies = []

            def copy(source, target):
                copies.append(pltpu.make_async_copy(source, target, sem.at[len(copies)]))
                copies[-1].start()

            for (name, (begin, count)), table in zip(TABLES.items(), tables):
                step = 128 if table.shape[2] > 128 else count
                for at in range(begin, begin + count, step):
                    low, high = max(at, n * CHUNK), min(at + step, (n + 1) * CHUNK)
                    if low >= high or name == "basis":
                        continue
                    columns = at - begin if step == 128 else 0
                    copy(
                        table.at[1, pl.ds(low - at, high - low), pl.ds(columns, 128)],
                        out.at[pl.ds(low - n * CHUNK, high - low)],
                    )
            if n == 3:
                copy(tables[6].at[1], turned)
                out[USED - n * CHUNK :, :] = jnp.zeros((PACK - USED, 128), BF)
            for c in copies:
                c.wait()
            if n == 3:
                for i in range(5):
                    at = BASIS - n * CHUNK + 128 * i
                    out[at : at + 128, :] = turned[:, 128 * i : 128 * (i + 1)].T


def join_kernel(q0, q1, q2, q3, out):
    i1, _ = places()
    for bits, quarter in zip((0, *PEERS), (q0, q1, q2, q3)):
        begin = pl.multiple_of((i1 ^ bits) * CHUNK, CHUNK)
        out[pl.ds(begin, CHUNK), :] = quarter[...]


def first_kernel(label, lag, s0, s1, s2, s3, state_out, look_out, e, act, slope, theta):
    weights = Weights((s0.at[0], s1.at[0], s2, s3))
    labels = label[...]
    state = jnp.where(look_mask(labels), lag[...].astype(F32), 0.0)
    heads, fore = run_forward(state, labels, weights, e, act, slope, theta)
    state_out[...] = state - pick_look(heads, labels)
    look_out[...] = pick_reach(fore, labels)


def second_kernel(
    label, state_in, look_in, left, adjoint, s0, s1, s2, s3, rest, look, g_out, mine, theirs, e, act, slope, theta
):
    weights = Weights((s0.at[1], s1.at[1], s2, s3))
    labels = label[...]
    heads, fore = run_forward(state_in[...], labels, weights, e, act, slope, theta)
    rest[...] = state_in[...] - pick_look(heads, labels)
    look[...] = look_in[...] + pick_reach(fore, labels)
    grads = Grads((mine, theirs))
    g = left[...].astype(F32)
    fore_wide = widen_reach(adjoint[...].astype(F32), labels)
    d_pre = backward_heads(g, fore_wide, labels, weights, act, slope, theta, grads)
    g_out[...] = backward_layers(g, d_pre, labels, weights, e, act, slope, grads)


def third_kernel(label, g_in, adjoint, s0, s1, s2, s3, act, slope, theta, d_out, mine, theirs):
    grads = Grads((mine, theirs), FOURTH)
    labels = label[...]
    fore_wide = widen_reach(adjoint[...].astype(F32), labels)
    d_out[...] = backward_heads(
        g_in[...], fore_wide, labels, Weights((s0.at[0], s1.at[0], s2, s3)), act, slope, theta, grads
    )


def fourth_kernel(
    label, g_in, d_in, s0, s1, s2, s3, e, act, slope, steep_out, mine, near, far, steep, sem
):
    grads = Grads((mine, (near, far)))
    labels = label[...]
    weights = Weights((s0.at[0], s1.at[0], s2, s3))
    copy = pltpu.make_async_copy(steep, steep_out, sem)

    def take(new):
        steep[...] = jnp.where(look_mask(labels), new, 0.0)
        copy.start()

    backward_layers(g_in[...], d_in[...], labels, weights, e, act, slope, grads, take)
    copy.wait()


def cut_kernel(mine, got, *outs):
    i1, _ = places()
    for bits, out in zip((*PEERS, 0), outs):
        rows = pl.ds(pl.multiple_of((i1 ^ bits) * CHUNK, CHUNK), CHUNK)
        out[...] = (mine[:, rows, :].astype(F32) + got[:, rows, :].astype(F32)).astype(BF)


def fold_heads_kernel(mine, got, near, rest, far):
    sums = (mine[...].astype(F32) + got[...].astype(F32)).astype(BF)
    near[...] = sums[0]
    rest[...] = sums[1, : EARLY - FOURTH]
    far[...] = sums[1, EARLY - FOURTH :]


def cut_one_kernel(mine, got0, got1, near, rest, came, *refs):
    outs, early, late = refs[:4], refs[4], refs[5]
    i1, _ = places()
    for half, got in enumerate((got0, got1)):
        early[half, :LOW] = (mine[half].astype(F32) + got[...].astype(F32)).astype(BF)
    early[0, LOW:EARLY] = near[: EARLY - LOW, :]
    early[1, LOW:EARLY] = rest[...]
    early[:, EARLY:] = jnp.zeros((2, EARLY_PACK - EARLY, 128), BF)
    late[...] = (near[EARLY - LOW :, :].astype(F32) + came[...].astype(F32)).astype(BF)
    for bits, out in zip((*PEERS, 0), outs):
        begin = pl.multiple_of((i1 ^ bits) * EARLY_CHUNK, EARLY_CHUNK)
        for half in range(2):
            out[half * EARLY_CHUNK : (half + 1) * EARLY_CHUNK, :] = early[half, pl.ds(begin, EARLY_CHUNK), :]
        begin = pl.multiple_of((i1 ^ bits) * LATE_CHUNK, LATE_CHUNK)
        out[2 * EARLY_CHUNK :, :] = late[pl.ds(begin, LATE_CHUNK), :]


def total(refs):
    a, b, c, d = (ref[...].astype(F32) for ref in refs)
    return ((a + b) + (c + d)).astype(BF)


def fold_kernel(own, a, b, c, near, far):
    near[...], far[...] = total((own, a, b, c))


def piece_kernel(own, a, b, c, near, came, *refs):
    outs, one, two = refs[:4], refs[4], refs[5]
    _, i2 = places()
    one[...] = total((own, a, b, c))
    two[...] = (near[...].astype(F32) + came[...].astype(F32)).astype(BF)
    for bits, out in zip((*SECOND_STEP, 0), outs):
        at = 0
        for ref, base, count in (
            (one, 0, EARLY_PIECE),
            (one, 2 * EARLY_CHUNK, LATE_PIECE),
            (two, 0, PIECE),
            (one, EARLY_CHUNK, EARLY_PIECE),
        ):
            begin = pl.multiple_of(base + (i2 ^ bits) * count, 16)
            out[at : at + count, :] = ref[pl.ds(begin, count), :]
            at += count


def sum_kernel(own, a, b, c, near, far):
    sums = total((own, a, b, c))
    near[0] = sums[:PIECE]
    near[1] = sums[PIECE : 2 * PIECE]
    far[...] = sums[2 * PIECE :]


def across_kernel(near, a, b, c, out):
    both = near[...].astype(F32) + a[...].astype(F32)
    add = b[...].astype(F32) + c[...].astype(F32)
    out[0, :EARLY_PIECE] = (both[0, :EARLY_PIECE] + add).astype(BF)
    out[0, EARLY_PIECE:] = both[0, EARLY_PIECE:].astype(BF)
    out[1] = both[1].astype(BF)


def stack_kernel(*refs):
    for k in range(2):
        for n in range(4):
            refs[4 + k][n] = refs[n][k]
    refs[6][...] = refs[3][0, :16]


def unpack_kernel(k, *refs):
    stacks, outs, whole, bufs, sem = refs[:4], refs[-16:-9], refs[-9], refs[-8:-1], refs[-1]
    i1, i2 = places()
    parts = ((0, EARLY_CHUNK, EARLY_PIECE), (EARLY_PACK, LATE_CHUNK, LATE_PIECE)) if k == 0 else ((0, CHUNK, PIECE),)
    for a, stack in zip((0, *FAR_FIRST), stacks):
        for slot, b in enumerate((0, *FAR_FIRST)):
            row = 0
            for base, chunk, piece in parts:
                at = pl.multiple_of(base + (i1 ^ a) * chunk + (i2 ^ b) * piece, 16)
                whole[pl.ds(at, piece), :] = stack[slot, row : row + piece, :]
                row += piece

    def rows(begin, count):
        if k == 0 and begin >= EARLY:
            begin += EARLY_PACK - EARLY
        return whole[begin : begin + count, :].astype(F32) * scale

    scale = 1.0 / math.sqrt(98304)
    copies = []
    for (name, (begin, count)), out, buf in zip(TABLES.items(), outs, bufs):
        if buf.shape[1] == 128:
            buf[...] = rows(begin, count)
        else:
            for i in range(count // 128):
                part = rows(begin + 128 * i, 128)
                buf[:, 128 * i : 128 * (i + 1)] = part.T if name == "basis" else part
        copies.append(pltpu.make_async_copy(buf, out.at[k], sem.at[len(copies)]))
        copies[-1].start()
    for copy in copies:
        copy.wait()


def shape(*dims, kind=F32):
    return jax.ShapeDtypeStruct(dims, kind)


def vmem(*dims, kind=BF):
    return pltpu.VMEM(dims, kind)


M1, M2, M3, M4, M5 = 12, 20, 12, 12, 8
DMA = pltpu.SemaphoreType.DMA
IN_VMEM = pl.BlockSpec(memory_space=pltpu.VMEM)
ANYWHERE = pl.BlockSpec(memory_space=pl.ANY)


def call(kernel, name, ins, outs, scratch, mib, us, aliases={}):
    return pl.pallas_call(
        kernel,
        out_shape=[o[0] for o in outs],
        in_specs=ins,
        out_specs=[o[1] for o in outs],
        scratch_shapes=scratch,
        compiler_params=pltpu.CompilerParams(vmem_limit_bytes=mib * 1024 * 1024),
        cost_estimate=pl.CostEstimate(
            flops=int(us * 8e8), bytes_accessed=int(us * 1e6), transcendentals=0
        ),
        name=name,
        input_output_aliases=aliases,
    )


ACTS = (4, 512, ROWS)
KEPT = [(560, ROWS), ACTS, ACTS, (2, 512, ROWS)]
TOP, LOW = USED - FOURTH, FOURTH


def plus(*parts):
    return sum(part.astype(F32) for part in parts).astype(BF)


def shards(lag, label, entry, second, third, fourth, back, fore, basis, adjoint, left):
    label = label[None, :]
    lag, adjoint, left = lag.T, adjoint.T, left.T
    whole, part = shape(PACK, 128, kind=BF), shape(CHUNK, 128, kind=BF)
    tables = (entry, second, third, fourth, back, fore, basis)
    quarter = call(
        quarter_kernel,
        "pack_quarter",
        [ANYWHERE] * 7,
        [(part, IN_VMEM)],
        [vmem(128, 640), DMA((8,))],
        60,
        1,
    )(*tables)[0]
    quarter, *tables = lax.optimization_barrier((quarter, *tables))
    both, one = call(
        pack_kernel,
        "pack",
        [IN_VMEM] * 7,
        [(shape(2, PACK, 128, kind=BF), IN_VMEM), (whole, IN_VMEM)],
        [],
        60,
        3,
    )(*tables)
    quarter = send(quarter, to_x_by_core())
    one, quarter = lax.optimization_barrier((one, quarter))
    across = send(one, to_x_by_core())
    quarters = [quarter] + [send(quarter, to_first(a)) for a in PEERS]
    other = send(both, to_core())
    across, *quarters = lax.optimization_barrier((across, *quarters))
    slots1 = (both, other, across, send(across, to_core()))
    across = call(join_kernel, "join", [IN_VMEM] * 4, [(whole, IN_VMEM)], [], M5, 1)(*quarters)[0]
    slots2 = (both, other, across, send(across, to_core()))
    state1, look1, e1, act1, slope1, theta1 = call(
        first_kernel,
        "forward_one",
        [IN_VMEM] * 6,
        [(shape(336, ROWS), IN_VMEM), (shape(48, ROWS), IN_VMEM)]
        + [(shape(*k, kind=BF), IN_VMEM) for k in KEPT],
        [],
        M1,
        6,
    )(label, lag, *slots1)
    rest, look, g1, mine2, theirs2 = call(
        second_kernel,
        "block_two",
        [IN_VMEM] * 9,
        [(shape(336, ROWS), IN_VMEM), (shape(48, ROWS), IN_VMEM), (shape(336, ROWS), IN_VMEM)]
        + [(shape(2, PACK, 128, kind=BF), IN_VMEM)] * 2,
        [vmem(*k) for k in KEPT],
        M2,
        14,
    )(label, state1, look1, left, adjoint, *slots2)
    got2 = send(theirs2, to_core())
    d_pre, mine1a, theirs1a = call(
        third_kernel,
        "backward_one_heads",
        [IN_VMEM] * 10,
        [(shape(512, ROWS, kind=BF), IN_VMEM)] + [(shape(2, TOP, 128, kind=BF), IN_VMEM)] * 2,
        [],
        M3,
        6,
    )(label, g1, adjoint, *slots1, act1, slope1, theta1)
    got1a = send(theirs1a, to_core())

    def small(kernel, name, outs, *args, scratch=()):
        return call(
            kernel,
            name,
            [IN_VMEM] * len(args),
            [(shape(*dims, 128, kind=BF), IN_VMEM) for dims in outs],
            scratch,
            M5,
            1,
        )(*args)

    *out2, own2 = small(cut_kernel, "cut_two", [(2, CHUNK)] * 4, mine2, got2)
    got2 = [send(part, to_first(a)) for part, a in zip(out2, PEERS)]
    near1, rest1, far1 = small(
        fold_heads_kernel, "fold_heads", [(TOP,), (EARLY - FOURTH,), (LATE,)], mine1a, got1a
    )
    d_pre, far1, *out2 = lax.optimization_barrier((d_pre, far1, *out2))
    came1 = send(far1, to_x_by_core())
    steep, mine1b, *theirs1b = call(
        fourth_kernel,
        "backward_one_layers",
        [IN_VMEM] * 10,
        [(shape(336, ROWS), ANYWHERE), (shape(2, LOW, 128, kind=BF), IN_VMEM)]
        + [(shape(LOW, 128, kind=BF), IN_VMEM)] * 2,
        [vmem(336, ROWS, kind=F32), DMA],
        M4,
        6,
    )(label, g1, d_pre, *slots1, e1, act1, slope1)
    got1b = [send(part, to_core()) for part in theirs1b]
    mine1b, got2[2] = lax.optimization_barrier((mine1b, got2[2]))
    *out1, own1 = small(
        cut_one_kernel,
        "cut_one",
        [(2 * EARLY_CHUNK + LATE_CHUNK,)] * 4,
        mine1b,
        *got1b,
        near1,
        rest1,
        came1,
        scratch=[vmem(2, EARLY_PACK, 128), vmem(LATE, 128)],
    )
    got1 = [send(part, to_first(a)) for part, a in zip(out1, PEERS)]

    near2, far2 = small(fold_kernel, "fold", [(CHUNK,)] * 2, own2, *got2)
    *out, own = small(
        piece_kernel,
        "pieces",
        [(2 * PIECE + EARLY_PIECE,)] * 4,
        own1,
        *got1,
        near2,
        send(far2, to_x_by_core()),
        scratch=[vmem(2 * EARLY_CHUNK + LATE_CHUNK, 128), vmem(CHUNK, 128)],
    )
    got = [send(part, to_second(b)) for part, b in zip(out, SECOND_STEP)]
    near, far = small(sum_kernel, "sums", [(2, PIECE), (EARLY_PIECE,)], own, *got)
    x1, x3 = send(far, to_x(1)), send(far, to_x(3))
    got = [send(near, to_x(2)), x3, x1]
    done = small(across_kernel, "across", [(2, PIECE)], near, *got)[0]
    got = [send(done, to_second(b)) for b in FAR_FIRST]
    *stack, here = small(stack_kernel, "stack", [(4, PIECE)] * 2 + [(16,)], done, *got)
    *stack, here = lax.optimization_barrier((*stack, send(here, to_core())))
    grads = ()
    for k in (1, 0):
        stacks = [stack[k]] + [send(stack[k], to_first(a)) for a in FAR_FIRST]
        outs = (
            (560, 128), (128, 512), (512, 128), (128, 512), (512, 128), (512, 128), (128, 640),
        )
        grads = call(
            functools.partial(unpack_kernel, k),
            "unpack",
            [IN_VMEM] * 4 + [ANYWHERE] * (len(grads) + 1),
            [(shape(2, *dims), ANYWHERE) for dims in outs],
            [vmem(PACK, 128)] + [vmem(*dims, kind=F32) for dims in outs] + [DMA((7,))],
            16,
            2,
            {4 + n: n for n in range(len(grads))},
        )(*stacks, *grads, here)
    return (look.T, rest.T, steep.T, *grads)


def solution(mesh):
    windows = P(("dp", "mp"), None)
    columns, rows = P(None, None, "mp"), P(None, "mp", None)
    tables = (columns, rows, columns, rows, columns, columns, rows)
    return jax.shard_map(
        shards,
        mesh=mesh,
        in_specs=(windows, P(("dp", "mp")), *tables, windows, windows),
        out_specs=(windows, windows, windows, *tables),
        check_vma=False,
    )
```

```python
import functools
import math

import jax
import jax.numpy as jnp
from jax import lax
from jax.experimental import pallas as pl
from jax.experimental.pallas import tpu as pltpu
from jax.sharding import PartitionSpec as P

BF = jnp.bfloat16
F32 = jnp.float32
ROWS = 768
ENTRY, SECOND, THIRD, FOURTH, BACK, FORE, BASIS, USED = 0, 560, 1072, 1584, 2096, 2608, 3120, 3760
PACK = 3840
PEERS = (1, 3, 2)
SECOND_STEP = (2, 3, 1)
EARLY, EARLY_PACK, LATE = 1712, 1792, 2048
EARLY_CHUNK, LATE_CHUNK = EARLY_PACK // 4, LATE // 4
EARLY_PIECE, LATE_PIECE = EARLY_PACK // 16, LATE // 16
FAR_FIRST = (1, 3, 2)
CHUNK, PIECE = PACK // 4, PACK // 16


def place(y, x, z, c):
    y, x, z, c = y % 4, x % 4, z % 4, c % 2
    return ((((y * 2 + x // 2) * 4 + z) * 2) + x % 2) * 2 + c


def pairs(move):
    out = []
    for y in range(4):
        for x in range(4):
            for z in range(4):
                for c in range(2):
                    out.append((place(y, x, z, c), place(*move(y, x, z, c))))
    return tuple(out)


def to_core():
    return pairs(lambda y, x, z, c: (y, x, z, 1 - c))


def to_x(bits):
    return pairs(lambda y, x, z, c: (y, x ^ bits, z, c))


def to_x_by_core():
    return pairs(lambda y, x, z, c: (y, x ^ (1 if c == 0 else 3), z, c))


def to_first(bits):
    return pairs(lambda y, x, z, c: (y ^ bits, x, z, c) if c == 0 else (y, x, z ^ bits, c))


def to_second(bits):
    return pairs(lambda y, x, z, c: (y, x, z ^ bits, c) if c == 0 else (y ^ bits, x, z, c))


def send(values, where):
    return lax.ppermute(values, ("dp", "mp"), where)


def row_of(count, begin=0):
    return lax.broadcasted_iota(jnp.int32, (count, ROWS), 0) + begin


def turn(values, shift):
    return pltpu.roll(values, shift % values.shape[0], 0)


def widen_look(v, label):
    zero = jnp.float32(0)
    e = [label == g for g in range(4)]
    near = turn(v[:56], 2)
    far = turn(v[:128], 2)
    top = row_of(56) < 2
    tip = row_of(8) < 2
    mid = jnp.where(
        top, jnp.where(e[0], v[40:96], zero), jnp.where(e[1], near, zero)
    )
    joint = jnp.where(
        tip, jnp.where(e[1], near[:8], zero), jnp.where(e[2], far[:8], zero)
    )
    return jnp.concatenate(
        [
            jnp.where(e[0], v[:40], zero),
            mid,
            joint,
            jnp.where(e[2], far[8:], zero),
            jnp.where(e[3], v, zero),
        ],
        axis=0,
    )


def pick_look(u, label):
    zero = jnp.float32(0)
    e = [label == g for g in range(4)]
    last = jnp.where(e[3], u[224:560], zero)
    near = turn(u[40:104], -2)
    far = turn(u[96:224], -2)
    row = row_of(56)
    begin = jnp.where(
        e[2],
        far[:56],
        jnp.where(e[1], near[:56], jnp.where(e[0] & (row < 42), u[:56], last[:56])),
    )
    middle = jnp.where(e[2] & (row_of(72, 56) < 126), far[56:], last[56:128])
    return jnp.concatenate([begin, middle, last[128:]], axis=0)


def widen_reach(a, label):
    zero = jnp.float32(0)
    e = [label == g for g in range(4)]
    one = turn(a[:16], 6)
    two = turn(a[:24], 6)
    row = row_of(8)
    return jnp.concatenate(
        [
            jnp.where(row < 6, jnp.where(e[0], a[:8], zero), jnp.where(e[1], one[:8], zero)),
            jnp.where(row < 6, jnp.where(e[1], one[8:], zero), jnp.where(e[2], two[:8], zero)),
            jnp.where(e[2], two[8:], zero),
            jnp.where(e[3], a, zero),
        ],
        axis=0,
    )


def pick_reach(u, label):
    zero = jnp.float32(0)
    e = [label == g for g in range(4)]
    last = jnp.where(e[3], u[32:], zero)
    one = turn(u[:16], -6)
    two = turn(u[8:32], -6)
    row = row_of(8)
    return jnp.concatenate(
        [
            jnp.where(
                e[2],
                two[:8],
                jnp.where(e[1], one[:8], jnp.where(e[0] & (row < 6), u[:8], last[:8])),
            ),
            jnp.where(e[2] & (row_of(16, 8) < 18), two[8:], last[8:24]),
            last[24:],
        ],
        axis=0,
    )


def look_mask(label):
    reach = jnp.where(label == 0, 42, jnp.where(label == 1, 56, jnp.where(label == 2, 126, 336)))
    return row_of(336) < reach


def by_columns(slots, begin, count):
    return jnp.concatenate([slot[begin : begin + count, :] for slot in slots], axis=1)


def by_rows(slots, begin, count):
    return jnp.concatenate(
        [
            jnp.concatenate(
                [slot[begin + 128 * i : begin + 128 * (i + 1), :] for i in range(count)], axis=1
            )
            for slot in slots
        ],
        axis=0,
    )


def dot(a, b):
    return jnp.dot(a, b, preferred_element_type=F32)


def dot_t(a, b):
    return lax.dot_general(a, b, (((1,), (1,)), ((), ())), preferred_element_type=F32)


def t_dot(a, b):
    return lax.dot_general(a, b, (((0,), (0,)), ((), ())), preferred_element_type=F32)


def silu_both(pre):
    s = jax.nn.sigmoid(pre)
    act = pre * s
    return act.astype(BF), (s + act * (1.0 - s)).astype(BF)


TABLES = {
    "entry": (ENTRY, 560),
    "second": (SECOND, 512),
    "third": (THIRD, 512),
    "fourth": (FOURTH, 512),
    "back": (BACK, 512),
    "fore": (FORE, 512),
    "basis": (BASIS, 640),
}


class Weights:
    def __init__(self, slots):
        self.slots = slots

    def get(self, name):
        begin, count = TABLES[name]
        if name in ("second", "fourth"):
            return by_rows(self.slots, begin, 4)
        return by_columns(self.slots, begin, count)


def run_forward(state, label, weights, e_ref, act_ref, slope_ref, theta_ref):
    e_ref[...] = widen_look(state, label).astype(BF)
    act, slope = silu_both(t_dot(weights.get("entry"), e_ref[...]))
    act_ref[0], slope_ref[0] = act, slope
    for i, name in enumerate(("second", "third", "fourth")):
        act, slope = silu_both(t_dot(weights.get(name), act_ref[i]))
        act_ref[i + 1], slope_ref[i + 1] = act, slope
    theta_ref[0] = t_dot(weights.get("back"), act_ref[3]).astype(BF)
    theta_ref[1] = t_dot(weights.get("fore"), act_ref[3]).astype(BF)
    basis = weights.get("basis")
    return dot(basis[:560], theta_ref[0]), dot(basis[560:], theta_ref[1])


class Grads:
    def __init__(self, outs, base=0):
        self.outs, self.base = outs, base

    def put(self, name, grad):
        begin, count = TABLES[name]
        at = begin - self.base
        for slot in range(4):
            out = self.outs[slot % 2]
            out = out[slot // 2] if isinstance(out, tuple) else out.at[slot // 2]
            if name in ("second", "fourth"):
                for i in range(4):
                    out[at + 128 * i : at + 128 * (i + 1), :] = grad[
                        128 * slot : 128 * (slot + 1), 128 * i : 128 * (i + 1)
                    ].astype(BF)
            else:
                out[at : at + count, :] = grad[:, 128 * slot : 128 * (slot + 1)].astype(BF)
        if name == "basis" and not self.base:
            for out in self.outs:
                out[:, USED:PACK, :] = jnp.zeros((2, PACK - USED, 128), BF)


def backward_heads(g, fore_wide, label, weights, act_ref, slope_ref, theta_ref, grads):
    d_back = -widen_look(g, label).astype(BF)
    d_fore = fore_wide.astype(BF)
    basis = weights.get("basis")
    d_theta_b = t_dot(basis[:560], d_back).astype(BF)
    d_theta_f = t_dot(basis[560:], d_fore).astype(BF)
    grads.put(
        "basis",
        jnp.concatenate([dot_t(d_back, theta_ref[0]), dot_t(d_fore, theta_ref[1])], axis=0),
    )
    d_act = dot(weights.get("back"), d_theta_b) + dot(weights.get("fore"), d_theta_f)
    grads.put("back", dot_t(act_ref[3], d_theta_b))
    grads.put("fore", dot_t(act_ref[3], d_theta_f))
    d_pre = (d_act * slope_ref[3].astype(F32)).astype(BF)
    grads.put("fourth", dot_t(act_ref[2], d_pre))
    return d_pre


def backward_layers(g, d_pre, label, weights, e_ref, act_ref, slope_ref, grads, take=None):
    d_act = dot(weights.get("fourth"), d_pre)
    d_pre = (d_act * slope_ref[2].astype(F32)).astype(BF)
    grads.put("third", dot_t(act_ref[1], d_pre))
    d_act = dot(weights.get("third"), d_pre)
    d_pre = (d_act * slope_ref[1].astype(F32)).astype(BF)
    grads.put("second", dot_t(act_ref[0], d_pre))
    d_act = dot(weights.get("second"), d_pre)
    d_pre = (d_act * slope_ref[0].astype(F32)).astype(BF)
    if take:
        take(g + pick_look(dot(weights.get("entry"), d_pre), label))
    grads.put("entry", dot_t(e_ref[...], d_pre))
    if not take:
        return g + pick_look(dot(weights.get("entry"), d_pre), label)


def places():
    dp, core = lax.axis_index("dp"), lax.rem(lax.axis_index("mp"), 2)
    y, z = lax.div(dp, 8), lax.rem(dp, 4)
    return jnp.where(core == 0, y, z), jnp.where(core == 0, z, y)


def pack_kernel(*refs):
    tables, both, one = refs[:7], refs[7], refs[8]
    for k in range(2):
        for (name, (begin, count)), table in zip(TABLES.items(), tables):
            if table.shape[2] == 128:
                both[k, begin : begin + count, :] = table[k]
                continue
            for i in range(count // 128):
                block = table[k, :, 128 * i : 128 * (i + 1)]
                both[k, begin + 128 * i : begin + 128 * (i + 1), :] = block.T if name == "basis" else block
        both[k, USED:PACK, :] = jnp.zeros((PACK - USED, 128), BF)
    one[...] = both[0]


def quarter_kernel(*refs):
    tables, out, turned, sem = refs[:7], refs[7], refs[8], refs[9]
    i1, _ = places()
    for n in range(4):

        @pl.when(i1 == n)
        def _():
            copies = []

            def copy(source, target):
                copies.append(pltpu.make_async_copy(source, target, sem.at[len(copies)]))
                copies[-1].start()

            for (name, (begin, count)), table in zip(TABLES.items(), tables):
                step = 128 if table.shape[2] > 128 else count
                for at in range(begin, begin + count, step):
                    low, high = max(at, n * CHUNK), min(at + step, (n + 1) * CHUNK)
                    if low >= high or name == "basis":
                        continue
                    columns = at - begin if step == 128 else 0
                    copy(
                        table.at[1, pl.ds(low - at, high - low), pl.ds(columns, 128)],
                        out.at[pl.ds(low - n * CHUNK, high - low)],
                    )
            if n == 3:
                copy(tables[6].at[1], turned)
                out[USED - n * CHUNK :, :] = jnp.zeros((PACK - USED, 128), BF)
            for c in copies:
                c.wait()
            if n == 3:
                for i in range(5):
                    at = BASIS - n * CHUNK + 128 * i
                    out[at : at + 128, :] = turned[:, 128 * i : 128 * (i + 1)].T


def join_kernel(q0, q1, q2, q3, out):
    i1, _ = places()
    for bits, quarter in zip((0, *PEERS), (q0, q1, q2, q3)):
        begin = pl.multiple_of((i1 ^ bits) * CHUNK, CHUNK)
        out[pl.ds(begin, CHUNK), :] = quarter[...]


def first_kernel(label, lag, s0, s1, s2, s3, state_out, look_out, e, act, slope, theta):
    weights = Weights((s0.at[0], s1.at[0], s2, s3))
    labels = label[...]
    state = jnp.where(look_mask(labels), lag[...].astype(F32), 0.0)
    heads, fore = run_forward(state, labels, weights, e, act, slope, theta)
    state_out[...] = state - pick_look(heads, labels)
    look_out[...] = pick_reach(fore, labels)


def second_kernel(
    label, state_in, look_in, left, adjoint, s0, s1, s2, s3, rest, look, g_out, mine, theirs, e, act, slope, theta
):
    weights = Weights((s0.at[1], s1.at[1], s2, s3))
    labels = label[...]
    heads, fore = run_forward(state_in[...], labels, weights, e, act, slope, theta)
    rest[...] = state_in[...] - pick_look(heads, labels)
    look[...] = look_in[...] + pick_reach(fore, labels)
    grads = Grads((mine, theirs))
    g = left[...].astype(F32)
    fore_wide = widen_reach(adjoint[...].astype(F32), labels)
    d_pre = backward_heads(g, fore_wide, labels, weights, act, slope, theta, grads)
    g_out[...] = backward_layers(g, d_pre, labels, weights, e, act, slope, grads)


def third_kernel(label, g_in, adjoint, s0, s1, s2, s3, act, slope, theta, d_out, mine, theirs):
    grads = Grads((mine, theirs), FOURTH)
    labels = label[...]
    fore_wide = widen_reach(adjoint[...].astype(F32), labels)
    d_out[...] = backward_heads(
        g_in[...], fore_wide, labels, Weights((s0.at[0], s1.at[0], s2, s3)), act, slope, theta, grads
    )


def fourth_kernel(
    label, g_in, d_in, s0, s1, s2, s3, e, act, slope, steep_out, mine, near, far, steep, sem
):
    grads = Grads((mine, (near, far)))
    labels = label[...]
    weights = Weights((s0.at[0], s1.at[0], s2, s3))
    copy = pltpu.make_async_copy(steep, steep_out, sem)

    def take(new):
        steep[...] = jnp.where(look_mask(labels), new, 0.0)
        copy.start()

    backward_layers(g_in[...], d_in[...], labels, weights, e, act, slope, grads, take)
    copy.wait()


def cut_kernel(mine, got, *outs):
    i1, _ = places()
    for bits, out in zip((*PEERS, 0), outs):
        rows = pl.ds(pl.multiple_of((i1 ^ bits) * CHUNK, CHUNK), CHUNK)
        out[...] = (mine[:, rows, :].astype(F32) + got[:, rows, :].astype(F32)).astype(BF)


def fold_heads_kernel(mine, got, near, rest, far):
    sums = (mine[...].astype(F32) + got[...].astype(F32)).astype(BF)
    near[...] = sums[0]
    rest[...] = sums[1, : EARLY - FOURTH]
    far[...] = sums[1, EARLY - FOURTH :]


def cut_one_kernel(mine, got0, got1, near, rest, came, *refs):
    outs, early, late = refs[:4], refs[4], refs[5]
    i1, _ = places()
    for half, got in enumerate((got0, got1)):
        early[half, :LOW] = (mine[half].astype(F32) + got[...].astype(F32)).astype(BF)
    early[0, LOW:EARLY] = near[: EARLY - LOW, :]
    early[1, LOW:EARLY] = rest[...]
    early[:, EARLY:] = jnp.zeros((2, EARLY_PACK - EARLY, 128), BF)
    late[...] = (near[EARLY - LOW :, :].astype(F32) + came[...].astype(F32)).astype(BF)
    for bits, out in zip((*PEERS, 0), outs):
        begin = pl.multiple_of((i1 ^ bits) * EARLY_CHUNK, EARLY_CHUNK)
        for half in range(2):
            out[half * EARLY_CHUNK : (half + 1) * EARLY_CHUNK, :] = early[half, pl.ds(begin, EARLY_CHUNK), :]
        begin = pl.multiple_of((i1 ^ bits) * LATE_CHUNK, LATE_CHUNK)
        out[2 * EARLY_CHUNK :, :] = late[pl.ds(begin, LATE_CHUNK), :]


def total(refs):
    a, b, c, d = (ref[...].astype(F32) for ref in refs)
    return ((a + b) + (c + d)).astype(BF)


def fold_kernel(own, a, b, c, near, far):
    near[...], far[...] = total((own, a, b, c))


def piece_kernel(own, a, b, c, near, came, *refs):
    outs, one, two = refs[:4], refs[4], refs[5]
    _, i2 = places()
    one[...] = total((own, a, b, c))
    two[...] = (near[...].astype(F32) + came[...].astype(F32)).astype(BF)
    for bits, out in zip((*SECOND_STEP, 0), outs):
        at = 0
        for ref, base, count in (
            (one, 0, EARLY_PIECE),
            (one, 2 * EARLY_CHUNK, LATE_PIECE),
            (two, 0, PIECE),
            (one, EARLY_CHUNK, EARLY_PIECE),
        ):
            begin = pl.multiple_of(base + (i2 ^ bits) * count, 16)
            out[at : at + count, :] = ref[pl.ds(begin, count), :]
            at += count


def sum_kernel(own, a, b, c, near, far):
    sums = total((own, a, b, c))
    near[0] = sums[:PIECE]
    near[1] = sums[PIECE : 2 * PIECE]
    far[...] = sums[2 * PIECE :]


def across_kernel(near, a, b, c, out):
    both = near[...].astype(F32) + a[...].astype(F32)
    add = b[...].astype(F32) + c[...].astype(F32)
    out[0, :EARLY_PIECE] = (both[0, :EARLY_PIECE] + add).astype(BF)
    out[0, EARLY_PIECE:] = both[0, EARLY_PIECE:].astype(BF)
    out[1] = both[1].astype(BF)


def stack_kernel(*refs):
    for k in range(2):
        for n in range(4):
            refs[4 + k][n] = refs[n][k]
    refs[6][...] = refs[3][0, :16]


def unpack_kernel(k, *refs):
    stacks, outs, whole, bufs, sem = refs[:4], refs[-16:-9], refs[-9], refs[-8:-1], refs[-1]
    i1, i2 = places()
    parts = ((0, EARLY_CHUNK, EARLY_PIECE), (EARLY_PACK, LATE_CHUNK, LATE_PIECE)) if k == 0 else ((0, CHUNK, PIECE),)
    for a, stack in zip((0, *FAR_FIRST), stacks):
        for slot, b in enumerate((0, *FAR_FIRST)):
            row = 0
            for base, chunk, piece in parts:
                at = pl.multiple_of(base + (i1 ^ a) * chunk + (i2 ^ b) * piece, 16)
                whole[pl.ds(at, piece), :] = stack[slot, row : row + piece, :]
                row += piece

    def rows(begin, count):
        if k == 0 and begin >= EARLY:
            begin += EARLY_PACK - EARLY
        return whole[begin : begin + count, :].astype(F32) * scale

    scale = 1.0 / math.sqrt(98304)
    copies = []
    for (name, (begin, count)), out, buf in zip(TABLES.items(), outs, bufs):
        if buf.shape[1] == 128:
            buf[...] = rows(begin, count)
        else:
            for i in range(count // 128):
                part = rows(begin + 128 * i, 128)
                buf[:, 128 * i : 128 * (i + 1)] = part.T if name == "basis" else part
        copies.append(pltpu.make_async_copy(buf, out.at[k], sem.at[len(copies)]))
        copies[-1].start()
    for copy in copies:
        copy.wait()


def shape(*dims, kind=F32):
    return jax.ShapeDtypeStruct(dims, kind)


def vmem(*dims, kind=BF):
    return pltpu.VMEM(dims, kind)


M1, M2, M3, M4, M5 = 12, 20, 12, 12, 8
DMA = pltpu.SemaphoreType.DMA
IN_VMEM = pl.BlockSpec(memory_space=pltpu.VMEM)
ANYWHERE = pl.BlockSpec(memory_space=pl.ANY)


def call(kernel, name, ins, outs, scratch, mib, us, aliases={}):
    return pl.pallas_call(
        kernel,
        out_shape=[o[0] for o in outs],
        in_specs=ins,
        out_specs=[o[1] for o in outs],
        scratch_shapes=scratch,
        compiler_params=pltpu.CompilerParams(vmem_limit_bytes=mib * 1024 * 1024),
        cost_estimate=pl.CostEstimate(
            flops=int(us * 8e8), bytes_accessed=int(us * 1e6), transcendentals=0
        ),
        name=name,
        input_output_aliases=aliases,
    )


ACTS = (4, 512, ROWS)
KEPT = [(560, ROWS), ACTS, ACTS, (2, 512, ROWS)]
TOP, LOW = USED - FOURTH, FOURTH


def plus(*parts):
    return sum(part.astype(F32) for part in parts).astype(BF)


def shards(lag, label, entry, second, third, fourth, back, fore, basis, adjoint, left):
    label = label[None, :]
    lag, adjoint, left = lag.T, adjoint.T, left.T
    whole, part = shape(PACK, 128, kind=BF), shape(CHUNK, 128, kind=BF)
    tables = (entry, second, third, fourth, back, fore, basis)
    quarter = call(
        quarter_kernel,
        "pack_quarter",
        [ANYWHERE] * 7,
        [(part, IN_VMEM)],
        [vmem(128, 640), DMA((8,))],
        60,
        1,
    )(*tables)[0]
    quarter, *tables = lax.optimization_barrier((quarter, *tables))
    both, one = call(
        pack_kernel,
        "pack",
        [IN_VMEM] * 7,
        [(shape(2, PACK, 128, kind=BF), IN_VMEM), (whole, IN_VMEM)],
        [],
        60,
        3,
    )(*tables)
    quarter = send(quarter, to_x_by_core())
    one, quarter = lax.optimization_barrier((one, quarter))
    across = send(one, to_x_by_core())
    quarters = [quarter] + [send(quarter, to_first(a)) for a in PEERS]
    other = send(both, to_core())
    across, *quarters = lax.optimization_barrier((across, *quarters))
    slots1 = (both, other, across, send(across, to_core()))
    across = call(join_kernel, "join", [IN_VMEM] * 4, [(whole, IN_VMEM)], [], M5, 1)(*quarters)[0]
    slots2 = (both, other, across, send(across, to_core()))
    state1, look1, e1, act1, slope1, theta1 = call(
        first_kernel,
        "forward_one",
        [IN_VMEM] * 6,
        [(shape(336, ROWS), IN_VMEM), (shape(48, ROWS), IN_VMEM)]
        + [(shape(*k, kind=BF), IN_VMEM) for k in KEPT],
        [],
        M1,
        6,
    )(label, lag, *slots1)
    rest, look, g1, mine2, theirs2 = call(
        second_kernel,
        "block_two",
        [IN_VMEM] * 9,
        [(shape(336, ROWS), IN_VMEM), (shape(48, ROWS), IN_VMEM), (shape(336, ROWS), IN_VMEM)]
        + [(shape(2, PACK, 128, kind=BF), IN_VMEM)] * 2,
        [vmem(*k) for k in KEPT],
        M2,
        14,
    )(label, state1, look1, left, adjoint, *slots2)
    got2 = send(theirs2, to_core())
    d_pre, mine1a, theirs1a = call(
        third_kernel,
        "backward_one_heads",
        [IN_VMEM] * 10,
        [(shape(512, ROWS, kind=BF), IN_VMEM)] + [(shape(2, TOP, 128, kind=BF), IN_VMEM)] * 2,
        [],
        M3,
        6,
    )(label, g1, adjoint, *slots1, act1, slope1, theta1)
    got1a = send(theirs1a, to_core())

    def small(kernel, name, outs, *args, scratch=()):
        return call(
            kernel,
            name,
            [IN_VMEM] * len(args),
            [(shape(*dims, 128, kind=BF), IN_VMEM) for dims in outs],
            scratch,
            M5,
            1,
        )(*args)

    *out2, own2 = small(cut_kernel, "cut_two", [(2, CHUNK)] * 4, mine2, got2)
    got2 = [send(part, to_first(a)) for part, a in zip(out2, PEERS)]
    near1, rest1, far1 = small(
        fold_heads_kernel, "fold_heads", [(TOP,), (EARLY - FOURTH,), (LATE,)], mine1a, got1a
    )
    d_pre, far1, *out2 = lax.optimization_barrier((d_pre, far1, *out2))
    came1 = send(far1, to_x_by_core())
    steep, mine1b, *theirs1b = call(
        fourth_kernel,
        "backward_one_layers",
        [IN_VMEM] * 10,
        [(shape(336, ROWS), ANYWHERE), (shape(2, LOW, 128, kind=BF), IN_VMEM)]
        + [(shape(LOW, 128, kind=BF), IN_VMEM)] * 2,
        [vmem(336, ROWS, kind=F32), DMA],
        M4,
        6,
    )(label, g1, d_pre, *slots1, e1, act1, slope1)
    got1b = [send(part, to_core()) for part in theirs1b]
    mine1b, got2[0], got2[1] = lax.optimization_barrier((mine1b, got2[0], got2[1]))
    *out1, own1 = small(
        cut_one_kernel,
        "cut_one",
        [(2 * EARLY_CHUNK + LATE_CHUNK,)] * 4,
        mine1b,
        *got1b,
        near1,
        rest1,
        came1,
        scratch=[vmem(2, EARLY_PACK, 128), vmem(LATE, 128)],
    )
    got1 = [send(part, to_first(a)) for part, a in zip(out1, PEERS)]

    near2, far2 = small(fold_kernel, "fold", [(CHUNK,)] * 2, own2, *got2)
    *out, own = small(
        piece_kernel,
        "pieces",
        [(2 * PIECE + EARLY_PIECE,)] * 4,
        own1,
        *got1,
        near2,
        send(far2, to_x_by_core()),
        scratch=[vmem(2 * EARLY_CHUNK + LATE_CHUNK, 128), vmem(CHUNK, 128)],
    )
    got = [send(part, to_second(b)) for part, b in zip(out, SECOND_STEP)]
    near, far = small(sum_kernel, "sums", [(2, PIECE), (EARLY_PIECE,)], own, *got)
    x1, x3 = send(far, to_x(1)), send(far, to_x(3))
    got = [send(near, to_x(2)), x3, x1]
    done = small(across_kernel, "across", [(2, PIECE)], near, *got)[0]
    got = [send(done, to_second(b)) for b in FAR_FIRST]
    *stack, here = small(stack_kernel, "stack", [(4, PIECE)] * 2 + [(16,)], done, *got)
    *stack, here = lax.optimization_barrier((*stack, send(here, to_core())))
    grads = ()
    for k in (1, 0):
        stacks = [stack[k]] + [send(stack[k], to_first(a)) for a in FAR_FIRST]
        outs = (
            (560, 128), (128, 512), (512, 128), (128, 512), (512, 128), (512, 128), (128, 640),
        )
        grads = call(
            functools.partial(unpack_kernel, k),
            "unpack",
            [IN_VMEM] * 4 + [ANYWHERE] * (len(grads) + 1),
            [(shape(2, *dims), ANYWHERE) for dims in outs],
            [vmem(PACK, 128)] + [vmem(*dims, kind=F32) for dims in outs] + [DMA((7,))],
            16,
            2,
            {4 + n: n for n in range(len(grads))},
        )(*stacks, *grads, here)
    return (look.T, rest.T, steep.T, *grads)


def solution(mesh):
    windows = P(("dp", "mp"), None)
    columns, rows = P(None, None, "mp"), P(None, "mp", None)
    tables = (columns, rows, columns, rows, columns, columns, rows)
    return jax.shard_map(
        shards,
        mesh=mesh,
        in_specs=(windows, P(("dp", "mp")), *tables, windows, windows),
        out_specs=(windows, windows, windows, *tables),
        check_vma=False,
    )
```
